512 devices in a mesh: sensor: 8 (over y, core), tm: 64 (over z, x).
Axes of the slice: x: 4, y: 4, z: 16, core: 2. Of those that a mesh axis runs over, the one named last changes fastest.
Arguments:
- recording: bfloat16 [256, 65536], P('sensor', 'tm'), may hold values from -6 to 6
- spatial_w: bfloat16 [512, 256], P(None, 'sensor'), may hold values from -0.375 to 0.375
- conv_w: bfloat16 [3, 3, 512, 512], P(None, None, 'sensor'), may hold values from -0.15625 to 0.15625
- conv_b: float32 [3, 512], P(None, 'sensor'), may hold values from -3 to 3
- dilations: int32 [3], replicated, may hold values from 1 to 16, as said below
- valid_frames: int32 [64], P('tm'), may hold values from 512 to 1024, as said below
- key_w: bfloat16 [512, 512], P('sensor'), may hold values from -0.25 to 0.25
- value_w: bfloat16 [512, 512], P('sensor'), may hold values from -0.25 to 0.25
- queries: bfloat16 [512, 2048], P('sensor'), may hold values from -60 to 60
Outputs:
- features: bfloat16 [512, 65536], P('sensor', 'tm')
- attended: bfloat16 [512, 2048], P('sensor')
The draws below stay inside these ranges and needn't reach their ends.
Inputs may be any that keep to these rules, and one draw needn't show every extreme that they name: `dilations`: one layer has dilation exactly 16 and another exactly 1. `valid_frames`: one block is full and one holds exactly half of its 1024 frames.
All inputs are finite; a program needn't handle non-finite values.
Results may differ from the reference program's by a relative error of at most 0.015.
The reference program's roundings to bfloat16 on the way count: a program that leaves them out, or rounds other values in their place, can miss the bound.
Values may be sent and summed in bfloat16 or wider, within the bound.
A program may use at most 64 MiB of HBM per device.

```python
import math
import jax
import jax.numpy as jnp
from jax import lax

SENSORS = 256
CH = 512
LATW = 512
HD = 64
LATENTS = 2048
LAYERS = 3
DMAX = 16
F_DEV = 1024
FRAMES = 65536
BLOCKS = 64
HEADS = 8


def draw_dilations(key, part):
    ranking = jax.random.permutation(jax.random.fold_in(key, 11), LAYERS)
    baseline = jax.random.randint(jax.random.fold_in(key, 12), (LAYERS,), 1, DMAX + 1)
    return baseline.at[ranking[0]].set(DMAX).at[ranking[1]].set(1).astype(jnp.int32)


def draw_valid_frames(key, part):
    ranking = jax.random.permutation(jax.random.fold_in(key, 21), BLOCKS)
    baseline = jax.random.randint(jax.random.fold_in(key, 22), (BLOCKS,), F_DEV // 2, F_DEV + 1)
    return baseline.at[ranking[0]].set(F_DEV).at[ranking[1]].set(F_DEV // 2).astype(jnp.int32)


def draw_queries(key, part):
    values = jnp.clip(3.0 * jax.random.normal(jax.random.fold_in(key, 34), (LATW, LATENTS)), -12.0, 12.0)
    return values.astype(jnp.bfloat16)


def steps_of(rng, extent, split, low, largest):
    level = 1.0
    for position, parts in split:
        heights = jax.random.uniform(jax.random.fold_in(jax.random.fold_in(rng, 6), position), (parts,), jnp.float32, low / len(split), largest / len(split))
        level = level * jnp.repeat(jnp.exp(heights), extent[position] // parts).reshape((-1,) + (1,) * (len(extent) - 1 - position))
    return level


def scatter_about(key, extent, spread, bound, shards=(), kind=jnp.bfloat16):
    drawn = spread * jax.random.normal(key, extent, jnp.float32)
    if shards:
        drawn = drawn * steps_of(key, extent, shards, -0.22, 0.18)
    return jnp.clip(drawn, -bound, bound).astype(kind)


def setup_inputs(seed: int = 0) -> dict:
    keys = jax.random.split(jax.random.key(seed), 10)
    return {
        "recording": scatter_about(keys[0], (SENSORS, FRAMES), 1.0, 6.0, ((0, 8), (1, 64))),
        "spatial_w": scatter_about(keys[1], (CH, SENSORS), SENSORS ** -0.5, 0.375, ((1, 8),)),
        "conv_w": scatter_about(keys[2], (LAYERS, 3, CH, CH), (3 * CH) ** -0.5, 0.15625, ((2, 8),)),
        "conv_b": scatter_about(keys[3], (LAYERS, CH), 0.5, 3.0, ((1, 8),), jnp.float32),
        "dilations": draw_dilations(jax.random.fold_in(keys[9], 71), 0),
        "valid_frames": draw_valid_frames(jax.random.fold_in(keys[9], 71), 0),
        "key_w": scatter_about(keys[6], (LATW, CH), CH ** -0.5, 0.25, ((0, 8),)),
        "value_w": scatter_about(keys[7], (LATW, CH), CH ** -0.5, 0.25, ((0, 8),)),
        "queries": draw_queries(jax.random.fold_in(keys[9], 71), 0),
    }


def reference(recording, spatial_w, conv_w, conv_b, dilations, valid_frames, key_w, value_w, queries):
    hidden = jnp.dot(spatial_w, recording, preferred_element_type=jnp.float32).astype(jnp.bfloat16)
    for layer in range(LAYERS):
        dilation = dilations[layer]
        padded = jnp.pad(hidden, ((0, 0), (DMAX, DMAX)))
        preact = jnp.broadcast_to(conv_b[layer][:, None], (CH, FRAMES)).astype(jnp.float32)
        for tap_index in range(3):
            offset = (DMAX + (tap_index - 1) * dilation).astype(jnp.int32)
            shifted = lax.dynamic_slice_in_dim(padded, offset, FRAMES, 1)
            preact = preact + jnp.dot(conv_w[layer, tap_index], shifted, preferred_element_type=jnp.float32)
        hidden = (hidden.astype(jnp.float32) + jax.nn.gelu(preact, approximate=False)).astype(jnp.bfloat16)
    features = hidden
    key_rows = jnp.dot(key_w, features, preferred_element_type=jnp.float32).astype(jnp.bfloat16)
    value_rows = jnp.dot(value_w, features, preferred_element_type=jnp.float32).astype(jnp.bfloat16)
    frame_mask = jnp.arange(FRAMES) % F_DEV < jnp.repeat(valid_frames, F_DEV)
    block_rows = min(LATENTS, 512)
    block_count = LATENTS // block_rows
    key_heads = key_rows.reshape(HEADS, HD, FRAMES)
    value_heads = value_rows.reshape(HEADS, HD, FRAMES)
    query_blocks = queries.reshape(HEADS, HD, block_count, block_rows).transpose(0, 2, 1, 3)
    query_blocks = query_blocks.reshape(HEADS * block_count, HD, block_rows)
    scale = 1.0 / math.sqrt(HD)

    def attend(index):
        head = index // block_count
        query_block = query_blocks[index]
        key_head = lax.dynamic_index_in_dim(key_heads, head, 0, keepdims=False)
        value_head = lax.dynamic_index_in_dim(value_heads, head, 0, keepdims=False)
        scores = jnp.dot(query_block.T, key_head, preferred_element_type=jnp.float32) * scale
        scores = jnp.where(frame_mask[None, :], scores, -jnp.inf)
        peaks = lax.optimization_barrier(jnp.max(scores, axis=1))
        probs = jnp.where(frame_mask[None, :], jnp.exp(scores - peaks[:, None]), 0.0)
        totals = lax.optimization_barrier(jnp.sum(probs, axis=1))
        weighted = jnp.dot(value_head, probs.astype(jnp.bfloat16).T, preferred_element_type=jnp.float32)
        return weighted / totals[None, :]
    outputs = lax.map(attend, jnp.arange(HEADS * block_count, dtype=jnp.int32))
    attended = outputs.reshape(HEADS, block_count, HD, block_rows).transpose(0, 2, 1, 3)
    attended = attended.reshape(LATW, LATENTS).astype(jnp.bfloat16)
    return (features, attended)
```

```python
import jax
import jax.numpy as jnp
from jax import lax
from jax.experimental import pallas as pl
from jax.experimental.pallas import tpu as pltpu
from jax.sharding import PartitionSpec as P

MESH = pl.DeviceIdType.MESH
BF16 = jnp.bfloat16
F32 = jnp.float32
NY, NX, NZ = 4, 4, 16
HD = 64
LATENTS = 2048
QUARTER = 512
LB = 256


def dot(a, b):
    return jnp.dot(a, b, preferred_element_type=F32)


def kernel(
    dil_ref, valid_ref, rec_ref, sw_ref, cw_ref, cb_ref, kw_ref, vw_ref, q_ref,
    feat_ref, att_ref,
    swt, st, sfull, rec, wc, bias, kvw, h0, h1, h2, h3, taps, resid, kv, kvall, ka, kt, va, qa,
    xsend, xlse_send, xrecv, xlse, zsend, zlse_send, zrecv, zlse,
    st_s, st_r, rec_s, rec_r, w_s, w_r, loc, g_s, g_r, kv_s, kv_r, f_s, f_r,
    xs, xr, xls, xlr, zs, zr, zls, zlr, as_, ar, bs, br,
):
    s = lax.axis_index("sensor")
    t = lax.axis_index("tm")
    y, c = s // 2, lax.rem(s, 2)
    z, x = t // NX, lax.rem(t, NX)
    other = 1 - c

    def at_y(i, core):
        return (lax.rem(y + i, NY) * 2 + core, t)

    sibling = (y * 2 + other, t)
    prev_tm = lax.rem(t + 63, 64)
    next_tm = lax.rem(t + 1, 64)

    def at_x(i):
        return (s, z * NX + lax.rem(x + i, NX))

    def at_z(i):
        return (s, lax.rem(z + i, NZ) * NX + x)

    barrier = pltpu.get_barrier_semaphore()

    def greet(device):
        pl.semaphore_signal(barrier, inc=1, device_id=device, device_id_type=MESH)

    for i in range(NY):
        for core in range(2):
            greet((i * 2 + core, jnp.where(c == 0, prev_tm, next_tm)))
    for i in range(1, NY):
        greet(at_y(i, c))
        greet(at_y(i, other))
    greet(sibling)
    for i in range(1, NX):
        greet(at_x(i))

    def greet_z(i, carry):
        greet(at_z(i))
        return carry

    lax.fori_loop(1, NZ, greet_z, 0)

    swt[...] = jnp.transpose(sw_ref[...].astype(F32)).astype(BF16)
    bias[c] = jnp.zeros((8, 128), F32)
    bias[c, 0:3, 0:64] = cb_ref[...]
    own_rows = pl.ds(pl.multiple_of(32 * s, 32), 32)
    st[own_rows, :] = swt[...]

    pl.semaphore_wait(barrier, 8 + 7 + 3 + 15)

    def remote(src, dst, ssem, rsem, device):
        copy = pltpu.make_async_remote_copy(
            src_ref=src, dst_ref=dst, send_sem=ssem, recv_sem=rsem,
            device_id=device, device_id_type=MESH,
        )
        copy.start()
        return copy

    rec_copies = []
    st_copies = []
    peers = [(i, k) for i in range(1, NY) for k in range(2)] + [(0, 1)]
    for n, (i, k) in enumerate(peers):
        core = lax.rem(c + k, 2)
        device = at_y(i, core)
        st_copies.append(remote(swt, st.at[own_rows], st_s.at[n], st_r.at[n], device))
        src = rec_ref.at[:, pl.ds(pl.multiple_of(384 * core, 128), 640)]
        dst = rec.at[own_rows, pl.ds(pl.multiple_of(128 - 128 * core, 128), 640)]
        rec_copies.append(remote(src, dst, rec_s.at[n], rec_r.at[n], device))
    for i in range(NY):
        rec_copies.append(
            remote(
                rec_ref.at[:, 896:1024], rec.at[own_rows, 0:128],
                rec_s.at[7 + i], rec_r.at[7 + 2 * i + c],
                (lax.rem(y + i, NY) * 2, next_tm),
            )
        )
        rec_copies.append(
            remote(
                rec_ref.at[:, 0:128], rec.at[own_rows, 640:768],
                rec_s.at[11 + i], rec_r.at[7 + 2 * i + c],
                (lax.rem(y + i, NY) * 2 + 1, prev_tm),
            )
        )
    own_w = pl.ds(pl.multiple_of(64 * c, 64), 64)
    own_k = pl.ds(pl.multiple_of(128 * c, 64), 64)
    own_v = pl.ds(pl.multiple_of(128 * c + 64, 64), 64)
    w_copies = [
        remote(cw_ref, wc.at[:, :, own_w, :], w_s.at[0], w_r.at[0], sibling),
        remote(kw_ref, kvw.at[own_k], w_s.at[1], w_r.at[1], sibling),
        remote(vw_ref, kvw.at[own_v], w_s.at[2], w_r.at[2], sibling),
        remote(bias.at[c], bias.at[c], w_s.at[3], w_r.at[3], sibling),
    ]
    local = [
        pltpu.make_async_copy(cw_ref, wc.at[:, :, own_w, :], loc.at[0]),
        pltpu.make_async_copy(kw_ref, kvw.at[own_k], loc.at[1]),
        pltpu.make_async_copy(vw_ref, kvw.at[own_v], loc.at[2]),
        pltpu.make_async_copy(
            rec_ref.at[:, pl.ds(pl.multiple_of(384 * c, 128), 640)],
            rec.at[own_rows, pl.ds(pl.multiple_of(128 - 128 * c, 128), 640)],
            loc.at[3],
        ),
    ]
    for copy in local:
        copy.start()
    qa[0:64, :] = q_ref[...]
    first = lax.broadcasted_iota(jnp.int32, (64, LATENTS), 0) == 0
    qa[64:128, :] = jnp.where(first, 1.0, 0.0).astype(BF16)
    va[64:80, :] = jnp.ones((16, 1024), BF16)
    frame = lax.broadcasted_iota(jnp.int32, (64, 1024), 1)
    row = lax.broadcasted_iota(jnp.int32, (64, 1024), 0)
    ka[64:128, :] = jnp.where((row == 0) & (frame >= valid_ref[0]), -1e30, 0.0).astype(BF16)

    for copy in st_copies:
        copy.wait()
    sfull[...] = jnp.transpose(st[...].astype(F32)).astype(BF16)
    for copy in local:
        copy.wait()
    for copy in rec_copies[:7]:
        copy.wait()
    for n, copy in enumerate(rec_copies[7:]):
        copy.wait_send()
    for n in range(8):
        pltpu.make_async_copy(rec_ref.at[:, 0:128], rec.at[0:32, 0:128], rec_r.at[7 + n]).wait()

    low = jnp.where((t == 0) & (c == 0), 0, -4096)
    high = jnp.where((t == 63) & (c == 1), 512, 4096)

    def inside(rows, lanes, start):
        f = lax.broadcasted_iota(jnp.int32, (rows, lanes), 1) + start
        return (f >= low) & (f < high)

    for n in range(0, 768, 256):
        part = dot(sfull[...], rec[:, n : n + 256])
        h0[:, n : n + 256] = jnp.where(inside(512, 256, n - 128), part, 0.0).astype(BF16)

    for copy in w_copies:
        copy.wait()
    both_bias = jnp.transpose(
        jnp.concatenate([bias[0][:, 0:64], bias[1][:, 0:64]], axis=1)
    )

    def shifted(ref, rows, tiles, amount):
        lane = lax.broadcasted_iota(jnp.int32, (128, 128), 1)
        keep = lane < 128 - amount
        turn = lax.rem(128 - amount, 128)
        last = ref.shape[1] // 128 - 1
        rolled = [
            pltpu.roll(ref[rows, 128 * k : 128 * k + 128], turn, 1)
            for k in range(min(tiles, last) + 1)
        ]
        return [jnp.where(keep, rolled[k], rolled[min(k + 1, last)]) for k in range(tiles)]

    chip_rows = pl.ds(pl.multiple_of(128 * y, 128), 128)

    def conv(layer, source, target, width, offset, tiles, start):
        w = wc[layer].reshape(384, 512)
        for n in range(0, width, 256):
            size = min(256, width - n)
            taps[:, n : n + size] = dot(w, source[:, n : n + size])
        resid[:, 0:width] = source[chip_rows, :].astype(F32)
        d = dil_ref[layer]
        view = taps.at[:, 0:width]
        a = shifted(view, slice(0, 128), tiles, offset - d)
        b = shifted(view, slice(128, 256), tiles, jnp.int32(offset))
        e = shifted(view, slice(256, 384), tiles, offset + d)
        r = shifted(resid.at[:, 0:width], slice(0, 128), tiles, jnp.int32(offset))
        col = both_bias[:, layer : layer + 1]
        for k in range(tiles):
            pre = col + a[k] + b[k] + e[k]
            out = r[k] + 0.5 * pre * (1.0 + lax.erf(pre * 0.7071067811865476))
            out = jnp.where(inside(128, 128, start + 128 * k), out, 0.0)
            target[chip_rows, 128 * k : 128 * k + 128] = out.astype(BF16)
        return [
            remote(
                target.at[chip_rows], target.at[chip_rows],
                g_s.at[3 * layer + i - 1], g_r.at[3 * layer + i - 1], at_y(i, c),
            )
            for i in range(1, NY)
        ]

    for copy in conv(0, h0, h1, 768, 64, 5, -64):
        copy.wait()
    for copy in conv(1, h1, h2, 640, 16, 5, -48):
        copy.wait()
    gather = conv(2, h2, h3, 640, 48, 4, 0)
    half = pl.ds(pl.multiple_of(512 * c, 512), 512)
    feature_copy = remote(
        h3.at[pl.ds(pl.multiple_of(128 * y + 64 * other, 64), 64)], feat_ref.at[:, half],
        f_s, f_r, sibling,
    )
    feat_ref[:, half] = h3[pl.ds(pl.multiple_of(128 * y + 64 * c, 64), 64), :]
    for copy in gather:
        copy.wait()

    for n in range(0, 512, 256):
        kv[:, n : n + 256] = dot(kvw[...], h3[:, n : n + 256]).astype(BF16)
    kv_copy = remote(
        kv.at[pl.ds(pl.multiple_of(128 * other, 128), 128)], kvall.at[:, half], kv_s, kv_r, sibling
    )
    kvall[:, half] = kv[pl.ds(pl.multiple_of(128 * c, 128), 128), :]
    kv_copy.wait()
    ka[0:64, :] = (kvall[0:64, :].astype(F32) * 0.125).astype(BF16)
    va[0:64, :] = kvall[64:128, :]
    kt[...] = jnp.transpose(ka[...].astype(F32)).astype(BF16)

    def attend(quarter, slot):
        def block(j, carry):
            lanes = pl.ds(pl.multiple_of(quarter * QUARTER + j * LB, LB), LB)
            scores = dot(kt[...], qa[:, lanes])
            peak = jnp.max(scores, axis=0, keepdims=True)
            probs = jnp.exp(scores - peak).astype(BF16)
            both = dot(va[...], probs)
            total = both[64:65, :]
            here = pl.ds(pl.multiple_of(j * LB, LB), LB)
            xsend[slot, :, here] = (both[0:64, :] / total).astype(BF16)
            xlse_send[slot, :, here] = peak + jnp.log(total)
            return carry

        lax.fori_loop(0, QUARTER // LB, block, 0)

    def x_copies(i):
        device = at_x(i)
        return (
            pltpu.make_async_remote_copy(
                src_ref=xsend.at[i], dst_ref=xrecv.at[i], send_sem=xs.at[i], recv_sem=xr.at[i],
                device_id=device, device_id_type=MESH),
            pltpu.make_async_remote_copy(
                src_ref=xlse_send.at[i], dst_ref=xlse.at[i], send_sem=xls.at[i], recv_sem=xlr.at[i],
                device_id=device, device_id_type=MESH),
        )

    def peer_quarter(i, carry):
        attend(lax.rem(x + i, NX), i)
        for copy in x_copies(i):
            copy.start()
        return carry

    lax.fori_loop(1, NX, peer_quarter, 0)
    attend(x, 0)

    def merge(parts, lses):
        peak = lses[0]
        for v in lses[1:]:
            peak = jnp.maximum(peak, v)
        total = jnp.zeros_like(peak)
        out = None
        for part, v in zip(parts, lses):
            weight = jnp.exp(v - peak)
            total = total + weight
            term = part.astype(F32) * weight
            out = term if out is None else out + term
        return out / total, peak + jnp.log(total)

    for i in range(1, NX):
        for copy in x_copies(i):
            copy.wait()
    for b in range(4):
        lanes = slice(128 * b, 128 * b + 128)
        out, lse = merge(
            [xsend[0, :, lanes]] + [xrecv[i, :, lanes] for i in range(1, NX)],
            [xlse_send[0, :, lanes]] + [xlse[i, :, lanes] for i in range(1, NX)],
        )
        zsend[:, lanes] = out.astype(BF16)
        zlse_send[b] = lse

    def tile_of(zz):
        a, b = zz // 4, lax.rem(zz, 4)
        return pl.ds(pl.multiple_of(16 * a, 16), 16), pl.ds(pl.multiple_of(128 * b, 128), 128), b

    def z_copies(i):
        rows, lanes, b = tile_of(lax.rem(z + i, NZ))
        device = at_z(i)
        return (
            pltpu.make_async_remote_copy(
                src_ref=zsend.at[rows, lanes], dst_ref=zrecv.at[i], send_sem=zs.at[i],
                recv_sem=zr.at[i], device_id=device, device_id_type=MESH),
            pltpu.make_async_remote_copy(
                src_ref=zlse_send.at[b], dst_ref=zlse.at[i], send_sem=zls.at[i],
                recv_sem=zlr.at[i], device_id=device, device_id_type=MESH),
        )

    def z_start(i, carry):
        for copy in z_copies(i):
            copy.start()
        return carry

    def z_wait(i, carry):
        for copy in z_copies(i):
            copy.wait()
        return carry

    lax.fori_loop(1, NZ, z_start, 0)
    my_rows, my_lanes, my_b = tile_of(z)
    zrecv[0] = zsend[my_rows, my_lanes]
    zlse[0] = zlse_send[my_b]
    lax.fori_loop(1, NZ, z_wait, 0)
    out, _ = merge([zrecv[i] for i in range(NZ)], [zlse[i] for i in range(NZ)])

    def out_tile(zz):
        rows, _, b = tile_of(zz)
        return rows, pl.ds(pl.multiple_of(512 * x + 128 * b, 128), 128)

    rows, lanes = out_tile(z)
    att_ref[rows, lanes] = out.astype(BF16)

    def a_copy(i, zz):
        tile = att_ref.at[out_tile(zz)]
        return pltpu.make_async_remote_copy(
            src_ref=tile, dst_ref=tile, send_sem=as_.at[i], recv_sem=ar.at[i],
            device_id=at_z(i), device_id_type=MESH)

    def spread(zz):
        tile = att_ref.at[out_tile(zz)]
        for i in range(1, NX):
            remote(tile, tile, bs.at[i], br.at[i], at_x(i))

    def a_start(i, carry):
        a_copy(i, z).start()
        return carry

    def a_forward(i, carry):
        zz = lax.rem(z + NZ - i, NZ)
        a_copy(i, zz).wait_recv()
        spread(zz)
        return carry

    def a_done(i, carry):
        a_copy(i, z).wait_send()
        return carry

    lax.fori_loop(1, NZ, a_start, 0)
    spread(z)
    lax.fori_loop(1, NZ, a_forward, 0)
    for i in range(1, NX):
        quarter = att_ref.at[:, pl.ds(pl.multiple_of(512 * x, 512), 512)]
        whole = pltpu.make_async_remote_copy(
            src_ref=quarter, dst_ref=quarter, send_sem=bs.at[i], recv_sem=br.at[i],
            device_id=at_x(i), device_id_type=MESH)
        whole.wait_recv()
        whole.wait_send()
    lax.fori_loop(1, NZ, a_done, 0)
    feature_copy.wait()


def on_device(recording, spatial_w, conv_w, conv_b, dilations, valid_frames, key_w, value_w, queries):
    vmem = pl.BlockSpec(memory_space=pltpu.VMEM)
    smem = pl.BlockSpec(memory_space=pltpu.SMEM)
    dma = pltpu.SemaphoreType.DMA
    V = pltpu.VMEM
    return pl.pallas_call(
        kernel,
        out_shape=(
            jax.ShapeDtypeStruct((64, 1024), BF16),
            jax.ShapeDtypeStruct((64, LATENTS), BF16),
        ),
        in_specs=[smem, smem] + [vmem] * 7,
        out_specs=(vmem, vmem),
        scratch_shapes=[
            V((32, 512), BF16), V((256, 512), BF16), V((512, 256), BF16), V((256, 768), BF16),
            V((3, 3, 128, 512), BF16), V((2, 8, 128), F32), V((256, 512), BF16),
            V((512, 768), BF16), V((512, 640), BF16), V((512, 640), BF16), V((512, 512), BF16),
            V((384, 768), F32), V((128, 768), F32),
            V((256, 512), BF16), V((128, 1024), BF16),
            V((128, 1024), BF16), V((1024, 128), BF16), V((80, 1024), BF16), V((128, LATENTS), BF16),
            V((4, 64, 512), BF16), V((4, 1, 512), F32), V((4, 64, 512), BF16), V((4, 1, 512), F32),
            V((64, 512), BF16), V((4, 1, 128), F32), V((16, 16, 128), BF16), V((16, 1, 128), F32),
            dma((7,)), dma((7,)), dma((15,)), dma((15,)), dma((4,)), dma((4,)), dma((4,)),
            dma((9,)), dma((9,)), dma, dma, dma, dma,
            dma((4,)), dma((4,)), dma((4,)), dma((4,)),
            dma((16,)), dma((16,)), dma((16,)), dma((16,)),
            dma((16,)), dma((16,)), dma((4,)), dma((4,)),
        ],
        compiler_params=pltpu.CompilerParams(
            collective_id=0, has_side_effects=True, vmem_limit_bytes=56 * 2**20
        ),
        name="encoder",
    )(dilations, valid_frames, recording, spatial_w, conv_w, conv_b, key_w, value_w, queries)


def solution(mesh):
    return jax.shard_map(
        on_device,
        mesh=mesh,
        in_specs=(
            P("sensor", "tm"),
            P(None, "sensor"),
            P(None, None, "sensor", None),
            P(None, "sensor"),
            P(),
            P("tm"),
            P("sensor", None),
            P("sensor", None),
            P("sensor", None),
        ),
        out_specs=(P("sensor", "tm"), P("sensor", None)),
        check_vma=False,
    )
```

```python
import jax
import jax.numpy as jnp
from jax import lax
from jax.experimental import pallas as pl
from jax.experimental.pallas import tpu as pltpu
from jax.sharding import PartitionSpec as P

MESH = pl.DeviceIdType.MESH
BF16 = jnp.bfloat16
F32 = jnp.float32
NY, NX, NZ = 4, 4, 16
HD = 64
LATENTS = 2048
QUARTER = 512
LB = 256


def dot(a, b):
    return jnp.dot(a, b, preferred_element_type=F32)


def kernel(
    dil_ref, valid_ref, rec_ref, sw_ref, cw_ref, cb_ref, kw_ref, vw_ref, q_ref,
    feat_ref, att_ref,
    st, sfull, rec, rwin, wc, bias, kvw, h0, h1, h2, h3, taps, kv, kvall, ka, kt, va, qa,
    xsend, xlse_send, xrecv, xlse, zsend, zlse_send, zrecv, zlse,
    loc, rec_s, rec_r, hal_s, hal_r, b_s, b_r, st_s, st_r, sf_s, sf_r, so_s, so_r,
    y_s, y_r, xp_s, xp_r, xm_s, xm_r, o_s, o_r, fy_s, fy_r, fx_s, fx_r,
    f_s, f_r, kv_s, kv_r, z1, z2, z4,
    xs, xr, xls, xlr, zs, zr, zls, zlr, as_, ar, bs, br,
):
    s = lax.axis_index("sensor")
    t = lax.axis_index("tm")
    y, c = s // 2, lax.rem(s, 2)
    z, x = t // NX, lax.rem(t, NX)
    other = 1 - c
    parity = lax.rem(x, 2)

    def at_y(i, core):
        return (lax.rem(y + i, NY) * 2 + core, t)

    def at_x(i):
        return (s, z * NX + lax.rem(x + i, NX))

    def at_z(i):
        return (s, lax.rem(z + i, NZ) * NX + x)

    sibling = (y * 2 + other, t)
    prev_tm = lax.rem(t + 63, 64)
    next_tm = lax.rem(t + 1, 64)
    peers = [(i, k) for i in range(1, NY) for k in range(2)] + [(0, 1)]

    def signal(sem, device):
        pl.semaphore_signal(sem, inc=1, device_id=device, device_id_type=MESH)

    barrier = pltpu.get_barrier_semaphore()
    for i, k in peers:
        signal(barrier, at_y(i, lax.rem(c + k, 2)))
    for i in range(1, NX):
        signal(barrier, at_x(i))
    signal(barrier, at_z(1))
    signal(barrier, at_z(NZ - 1))

    @pl.when((s == 0) | (s == 7))
    def _():
        block = jnp.where(s == 0, prev_tm, next_tm)
        for k in range(8):
            signal(barrier, (k, block))

    def rows(start, size, align):
        return pl.ds(pl.multiple_of(start, align), size)

    def of_head(index):
        return rows(128 * index, 128, 128)

    own_rec = rows(32 * s, 32, 32)
    own_out = rows(64 * s, 64, 64)
    local = [
        pltpu.make_async_copy(cw_ref, wc.at[:, :, own_out, :], loc.at[0]),
        pltpu.make_async_copy(kw_ref, kvw.at[rows(128 * s, 64, 64)], loc.at[1]),
        pltpu.make_async_copy(vw_ref, kvw.at[rows(128 * s + 64, 64, 64)], loc.at[2]),
        pltpu.make_async_copy(q_ref, qa.at[0:64], loc.at[3]),
    ]
    for copy in local:
        copy.start()
    st[own_rec, :] = sw_ref[...]
    bias[s] = jnp.zeros((8, 128), F32)
    bias[s, 0:3, 0:64] = cb_ref[...]

    def rec_window(index):
        start = jnp.clip(index - 1, 0, 5)
        return rows(128 * start, 384, 128), rows(128 * (start - index + 2), 384, 128)

    here_src, here_dst = rec_window(s)
    rec[own_rec, here_dst] = rec_ref[:, here_src]

    pl.semaphore_wait(barrier, 7 + 3 + 2 + 2)

    def remote(src, dst, ssem, rsem, device):
        return pltpu.make_async_remote_copy(
            src_ref=src, dst_ref=dst, send_sem=ssem, recv_sem=rsem,
            device_id=device, device_id_type=MESH,
        )

    def same(ref, ssem, rsem, device):
        return remote(ref, ref, ssem, rsem, device)

    signal(z1.at[0], at_z(1))
    signal(z1.at[1], at_z(NZ - 1))

    def of_sensor(i):
        return lax.rem(y + NY - i, NY) * 2 + c

    st_y = [same(st.at[own_rec], st_s.at[i], st_r.at[i], at_y(i, c)) for i in range(1, NY)]
    st_own = same(st.at[own_rec], so_s, so_r, sibling)
    for copy in st_y:
        copy.start()
    st_own.start()
    rec_copies = []
    for n, (i, k) in enumerate(peers):
        core = lax.rem(c + k, 2)
        src, dst = rec_window(lax.rem(y + i, NY) * 2 + core)
        rec_copies.append(
            remote(rec_ref.at[:, src], rec.at[own_rec, dst], rec_s.at[n], rec_r.at[n], at_y(i, core))
        )
    halo = [
        remote(rec_ref.at[:, 896:1024], rec.at[own_rec, 128:256], hal_s.at[0], hal_r.at[s], (0, next_tm)),
        remote(rec_ref.at[:, 0:128], rec.at[own_rec, 384:512], hal_s.at[1], hal_r.at[s], (7, prev_tm)),
    ]
    bias_copies = [
        same(bias.at[s], b_s.at[n], b_r.at[n], at_y(i, lax.rem(c + k, 2)))
        for n, (i, k) in enumerate(peers)
    ]
    for copy in halo + rec_copies + bias_copies:
        copy.start()
    for copy in local:
        copy.wait()

    def piece(g, index, start, count):
        if g < 3:
            return wc.at[g, :, rows(64 * index + 16 * start, 16 * count, 16), :]
        return kvw.at[rows(128 * index + 32 * start, 32 * count, 32), :]

    def y_copies(g):
        return [
            same(piece(g, s, 2 * parity, 2), y_s.at[g, i], y_r.at[g, i], at_y(i, c))
            for i in range(1, NY)
        ]

    def own_copy(g):
        return same(piece(g, s, 0, 4), o_s.at[g], o_r.at[g], sibling)

    def issue(g):
        for copy in y_copies(g):
            copy.start()
        own_copy(g).start()

    def x_plus(g, i):
        return same(piece(g, of_sensor(i), 2 * parity, 1), xp_s.at[g, i], xp_r.at[g, i], at_x(1))

    def x_minus(g, i):
        return same(piece(g, of_sensor(i), 2 * parity + 1, 1), xm_s.at[g, i], xm_r.at[g, i], at_x(3))

    def sib_y(g, i):
        return same(piece(g, of_sensor(i), 2 * parity, 2), fy_s.at[g, i], fy_r.at[g, i], sibling)

    def sib_x(g, i):
        return same(piece(g, of_sensor(i), 2 - 2 * parity, 2), fx_s.at[g, i], fx_r.at[g, i], sibling)

    def forward_y(g):
        copies = y_copies(g)
        for i in (1, 3, 2):
            copies[i - 1].wait_recv()
            x_plus(g, i).start()
            x_minus(g, i).start()
            sib_y(g, i).start()

    def forward_x(g):
        for i in (1, 3, 2):
            x_plus(g, i).wait_recv()
            x_minus(g, i).wait_recv()
            sib_x(g, i).start()

    def ready(g):
        own_copy(g).wait_recv()
        for i in range(1, NY):
            sib_y(g, i).wait_recv()
            sib_x(g, i).wait_recv()

    def sent(g):
        for copy in y_copies(g):
            copy.wait_send()
        own_copy(g).wait_send()
        for i in range(1, NY):
            for copy in (x_plus, x_minus, sib_y, sib_x):
                copy(g, i).wait_send()

    issue(0)
    issue(1)

    first = lax.broadcasted_iota(jnp.int32, (64, LATENTS), 0) == 0
    qa[64:128, :] = jnp.where(first, 1.0, 0.0).astype(BF16)
    va[64:80, :] = jnp.ones((16, 1024), BF16)
    frame = lax.broadcasted_iota(jnp.int32, (64, 1024), 1)
    row = lax.broadcasted_iota(jnp.int32, (64, 1024), 0)
    ka[64:128, :] = jnp.where((row == 0) & (frame >= valid_ref[0]), -1e30, 0.0).astype(BF16)

    def sib_st(i):
        return same(
            st.at[rows(32 * of_sensor(i), 32, 32)], sf_s.at[i], sf_r.at[i], sibling
        )

    for i in (1, 3, 2):
        st_y[i - 1].wait_recv()
        sib_st(i).start()
    for copy in rec_copies:
        copy.wait_recv()

    @pl.when((s == 0) | (s == 7))
    def _():
        for k in range(8):
            tile = rec.at[0:32, 0:128]
            pltpu.make_async_copy(tile, tile, hal_r.at[k]).wait()

    def turned(tiles, count, amount):
        lane = lax.broadcasted_iota(jnp.int32, tiles[0].shape, 1)
        keep = lane < 128 - amount
        turn = lax.rem(128 - amount, 128)
        rolled = [pltpu.roll(tile, turn, 1) for tile in tiles]
        last = len(tiles) - 1
        return [jnp.where(keep, rolled[k], rolled[min(k + 1, last)]) for k in range(count)]

    window = turned(
        [rec[:, 128 * k : 128 * k + 128].astype(F32) for k in range(1, 4)], 2, jnp.int32(64)
    )
    for k in range(2):
        rwin[:, 128 * k : 128 * k + 128] = window[k].astype(BF16)

    low = jnp.where((t == 0) & (s == 0), 0, -4096)
    high = jnp.where((t == 63) & (s == 7), 128, 4096)

    def inside(lanes, start):
        f = lax.broadcasted_iota(jnp.int32, (128, lanes), 1) + start
        return (f >= low) & (f < high)

    st_own.wait_recv()
    for i in range(1, NY):
        sib_st(i).wait_recv()
    sfull[...] = jnp.transpose(st[...].astype(F32)).astype(BF16)
    for n in range(0, 512, 128):
        part = dot(sfull[n : n + 128, :], rwin[...])
        h0[n : n + 128, :] = jnp.where(inside(256, -64), part, 0.0).astype(BF16)

    for copy in bias_copies:
        copy.wait_recv()
    all_bias = jnp.transpose(
        jnp.concatenate([bias[k][:, 0:64] for k in range(8)], axis=1)
    )

    def conv(layer, source, target, offset, tiles, start):
        d = dil_ref[layer]
        for n in range(0, 512, 128):
            w = wc[layer, :, n : n + 128, :].reshape(384, 512)
            taps[...] = dot(w, source[...])
            a, b, e = [
                turned(
                    [taps[128 * j : 128 * j + 128, 128 * k : 128 * k + 128] for k in range(2)],
                    tiles, offset + (j - 1) * d,
                )
                for j in range(3)
            ]
            r = turned(
                [source[n : n + 128, 128 * k : 128 * k + 128].astype(F32) for k in range(2)],
                tiles, jnp.int32(offset),
            )
            col = all_bias[n : n + 128, layer : layer + 1]
            for k in range(tiles):
                pre = col + a[k] + b[k] + e[k]
                out = r[k] + 0.5 * pre * (1.0 + lax.erf(pre * 0.7071067811865476))
                out = jnp.where(inside(128, start + 128 * k), out, 0.0)
                target[n : n + 128, 128 * k : 128 * k + 128] = out.astype(BF16)

    forward_y(0)
    issue(2)
    pl.semaphore_wait(z1.at[0], 1)
    pl.semaphore_wait(z1.at[1], 1)
    signal(z2.at[0], at_z(2))
    signal(z2.at[1], at_z(NZ - 2))
    forward_y(1)
    issue(3)
    forward_x(0)
    ready(0)
    conv(0, h0, h1, 16, 2, -48)
    forward_y(2)
    forward_x(1)
    pl.semaphore_wait(z2.at[0], 1)
    pl.semaphore_wait(z2.at[1], 1)
    signal(z4.at[0], at_z(4))
    signal(z4.at[1], at_z(NZ - 4))
    ready(1)
    conv(1, h1, h2, 16, 2, -32)
    forward_y(3)
    forward_x(2)
    ready(2)
    conv(2, h2, h3, 32, 1, 0)
    forward_x(3)
    ready(3)

    own_lanes = rows(128 * s, 128, 128)
    for n in range(0, 1024, 256):
        kv[n : n + 256, :] = dot(kvw[n : n + 256, :], h3[...]).astype(BF16)
    kv_copies = []
    feature_copies = []
    for n, (i, k) in enumerate(peers):
        core = lax.rem(c + k, 2)
        to = lax.rem(y + i, NY) * 2 + core
        kv_copies.append(
            remote(kv.at[of_head(to)], kvall.at[:, own_lanes], kv_s.at[n], kv_r.at[n], at_y(i, core))
        )
        feature_copies.append(
            remote(
                h3.at[rows(64 * to, 64, 64)], feat_ref.at[:, own_lanes],
                f_s.at[n], f_r.at[n], at_y(i, core),
            )
        )
    for copy in kv_copies + feature_copies:
        copy.start()
    kvall[:, own_lanes] = kv[of_head(s), :]
    feat_ref[:, own_lanes] = h3[own_out, :]
    pl.semaphore_wait(z4.at[0], 1)
    pl.semaphore_wait(z4.at[1], 1)
    for copy in st_y + [st_own] + rec_copies + halo + bias_copies:
        copy.wait_send()
    for i in range(1, NY):
        sib_st(i).wait_send()
    for g in range(4):
        sent(g)
    for copy in kv_copies:
        copy.wait()
    ka[0:64, :] = (kvall[0:64, :].astype(F32) * 0.125).astype(BF16)
    va[0:64, :] = kvall[64:128, :]
    kt[...] = jnp.transpose(ka[...].astype(F32)).astype(BF16)

    def attend(quarter, slot):
        def block(j, carry):
            lanes = pl.ds(pl.multiple_of(quarter * QUARTER + j * LB, LB), LB)
            scores = dot(kt[...], qa[:, lanes])
            peak = jnp.max(scores, axis=0, keepdims=True)
            probs = jnp.exp(scores - peak).astype(BF16)
            both = dot(va[...], probs)
            total = both[64:65, :]
            here = pl.ds(pl.multiple_of(j * LB, LB), LB)
            xsend[slot, :, here] = (both[0:64, :] / total).astype(BF16)
            xlse_send[slot, :, here] = peak + jnp.log(total)
            return carry

        lax.fori_loop(0, QUARTER // LB, block, 0)

    def x_copies(i):
        device = at_x(i)
        return (
            pltpu.make_async_remote_copy(
                src_ref=xsend.at[i], dst_ref=xrecv.at[i], send_sem=xs.at[i], recv_sem=xr.at[i],
                device_id=device, device_id_type=MESH),
            pltpu.make_async_remote_copy(
                src_ref=xlse_send.at[i], dst_ref=xlse.at[i], send_sem=xls.at[i], recv_sem=xlr.at[i],
                device_id=device, device_id_type=MESH),
        )

    def peer_quarter(i, carry):
        attend(lax.rem(x + i, NX), i)
        for copy in x_copies(i):
            copy.start()
        return carry

    lax.fori_loop(1, NX, peer_quarter, 0)
    attend(x, 0)

    def merge(parts, lses):
        peak = lses[0]
        for v in lses[1:]:
            peak = jnp.maximum(peak, v)
        total = jnp.zeros_like(peak)
        out = None
        for part, v in zip(parts, lses):
            weight = jnp.exp(v - peak)
            total = total + weight
            term = part.astype(F32) * weight
            out = term if out is None else out + term
        return out / total, peak + jnp.log(total)

    for i in range(1, NX):
        for copy in x_copies(i):
            copy.wait()
    for b in range(4):
        lanes = slice(128 * b, 128 * b + 128)
        out, lse = merge(
            [xsend[0, :, lanes]] + [xrecv[i, :, lanes] for i in range(1, NX)],
            [xlse_send[0, :, lanes]] + [xlse[i, :, lanes] for i in range(1, NX)],
        )
        zsend[:, lanes] = out.astype(BF16)
        zlse_send[b] = lse

    def tile_of(zz):
        a, b = zz // 4, lax.rem(zz, 4)
        return pl.ds(pl.multiple_of(16 * a, 16), 16), pl.ds(pl.multiple_of(128 * b, 128), 128), b

    def z_copies(i):
        rows, lanes, b = tile_of(lax.rem(z + i, NZ))
        device = at_z(i)
        return (
            pltpu.make_async_remote_copy(
                src_ref=zsend.at[rows, lanes], dst_ref=zrecv.at[i], send_sem=zs.at[i],
                recv_sem=zr.at[i], device_id=device, device_id_type=MESH),
            pltpu.make_async_remote_copy(
                src_ref=zlse_send.at[b], dst_ref=zlse.at[i], send_sem=zls.at[i],
                recv_sem=zlr.at[i], device_id=device, device_id_type=MESH),
        )

    def far_first(n):
        k = (n + 1) // 2
        return 8 + k * (1 - 2 * lax.rem(n, 2))

    def near_first(n):
        return far_first(14 - n)

    def z_start(n, carry):
        for copy in z_copies(far_first(n)):
            copy.start()
        return carry

    def z_wait(n, carry):
        for copy in z_copies(near_first(n)):
            copy.wait()
        return carry

    lax.fori_loop(0, NZ - 1, z_start, 0)
    my_rows, my_lanes, my_b = tile_of(z)
    zrecv[0] = zsend[my_rows, my_lanes]
    zlse[0] = zlse_send[my_b]
    lax.fori_loop(0, NZ - 1, z_wait, 0)
    out, _ = merge([zrecv[i] for i in range(NZ)], [zlse[i] for i in range(NZ)])

    def out_tile(zz):
        rows, _, b = tile_of(zz)
        return rows, pl.ds(pl.multiple_of(512 * x + 128 * b, 128), 128)

    rows, lanes = out_tile(z)
    att_ref[rows, lanes] = out.astype(BF16)

    def a_copy(i, zz):
        tile = att_ref.at[out_tile(zz)]
        return pltpu.make_async_remote_copy(
            src_ref=tile, dst_ref=tile, send_sem=as_.at[i], recv_sem=ar.at[i],
            device_id=at_z(i), device_id_type=MESH)

    def spread(zz):
        tile = att_ref.at[out_tile(zz)]
        for i in range(1, NX):
            remote(tile, tile, bs.at[i], br.at[i], at_x(i)).start()

    def a_start(n, carry):
        a_copy(far_first(n), z).start()
        return carry

    def a_forward(n, carry):
        i = near_first(n)
        zz = lax.rem(z + NZ - i, NZ)
        a_copy(i, zz).wait_recv()
        spread(zz)
        return carry

    def a_done(i, carry):
        a_copy(i, z).wait_send()
        return carry

    lax.fori_loop(0, NZ - 1, a_start, 0)
    spread(z)
    lax.fori_loop(0, NZ - 1, a_forward, 0)
    for i in range(1, NX):
        quarter = att_ref.at[:, pl.ds(pl.multiple_of(512 * x, 512), 512)]
        whole = pltpu.make_async_remote_copy(
            src_ref=quarter, dst_ref=quarter, send_sem=bs.at[i], recv_sem=br.at[i],
            device_id=at_x(i), device_id_type=MESH)
        whole.wait_recv()
        whole.wait_send()
    lax.fori_loop(1, NZ, a_done, 0)
    for copy in feature_copies:
        copy.wait()


def on_device(recording, spatial_w, conv_w, conv_b, dilations, valid_frames, key_w, value_w, queries):
    vmem = pl.BlockSpec(memory_space=pltpu.VMEM)
    smem = pl.BlockSpec(memory_space=pltpu.SMEM)
    hbm = pl.BlockSpec(memory_space=pl.ANY)
    dma = pltpu.SemaphoreType.DMA
    regular = pltpu.SemaphoreType.REGULAR
    V = pltpu.VMEM
    return pl.pallas_call(
        kernel,
        out_shape=(
            jax.ShapeDtypeStruct((64, 1024), BF16),
            jax.ShapeDtypeStruct((64, LATENTS), BF16),
        ),
        in_specs=[smem, smem, vmem, vmem, hbm, vmem, hbm, hbm, hbm],
        out_specs=(vmem, vmem),
        scratch_shapes=[
            V((256, 512), BF16), V((512, 256), BF16), V((256, 640), BF16), V((256, 256), BF16),
            V((3, 3, 512, 512), BF16), V((8, 8, 128), F32), V((1024, 512), BF16),
            V((512, 256), BF16), V((512, 256), BF16), V((512, 256), BF16), V((512, 128), BF16),
            V((384, 256), F32), V((1024, 128), BF16), V((128, 1024), BF16),
            V((128, 1024), BF16), V((1024, 128), BF16), V((80, 1024), BF16), V((128, LATENTS), BF16),
            V((4, 64, 512), BF16), V((4, 1, 512), F32), V((4, 64, 512), BF16), V((4, 1, 512), F32),
            V((64, 512), BF16), V((4, 1, 128), F32), V((16, 16, 128), BF16), V((16, 1, 128), F32),
            dma((4,)), dma((7,)), dma((7,)), dma((2,)), dma((8,)), dma((7,)), dma((7,)),
            dma((4,)), dma((4,)), dma((4,)), dma((4,)), dma, dma,
            dma((4, 4)), dma((4, 4)), dma((4, 4)), dma((4, 4)), dma((4, 4)), dma((4, 4)),
            dma((4,)), dma((4,)), dma((4, 4)), dma((4, 4)), dma((4, 4)), dma((4, 4)),
            dma((7,)), dma((7,)), dma((7,)), dma((7,)),
            regular((2,)), regular((2,)), regular((2,)),
            dma((4,)), dma((4,)), dma((4,)), dma((4,)),
            dma((16,)), dma((16,)), dma((16,)), dma((16,)),
            dma((16,)), dma((16,)), dma((4,)), dma((4,)),
        ],
        compiler_params=pltpu.CompilerParams(
            collective_id=0, has_side_effects=True, vmem_limit_bytes=56 * 2**20
        ),
        name="encoder",
    )(dilations, valid_frames, recording, spatial_w.T, conv_w, conv_b, key_w, value_w, queries)


def solution(mesh):
    return jax.shard_map(
        on_device,
        mesh=mesh,
        in_specs=(
            P("sensor", "tm"),
            P(None, "sensor"),
            P(None, None, "sensor", None),
            P(None, "sensor"),
            P(),
            P("tm"),
            P("sensor", None),
            P("sensor", None),
            P("sensor", None),
        ),
        out_specs=(P("sensor", "tm"), P("sensor", None)),
        check_vma=False,
    )
```

```python
import jax
import jax.numpy as jnp
from jax import lax
from jax.experimental import pallas as pl
from jax.experimental.pallas import tpu as pltpu
from jax.sharding import PartitionSpec as P

MESH = pl.DeviceIdType.MESH
BF16 = jnp.bfloat16
F32 = jnp.float32
NY, NX, NZ = 4, 4, 16
HD = 64
LATENTS = 2048
QUARTER = 512
LB = 256


def dot(a, b):
    return jnp.dot(a, b, preferred_element_type=F32)


def kernel(
    dil_ref, valid_ref, rec_ref, sw_ref, cw_ref, cb_ref, kw_ref, vw_ref, q_ref,
    feat_ref, att_ref,
    st, sfull, rec, rwin, wc, bias, kvw, h0, h1, h2, h3, taps, kv, kvall, ka, kt, va, qa,
    xsend, xlse_send, xrecv, xlse, zsend, zlse_send, zrecv, zlse,
    loc, rec_s, rec_r, hal_s, hal_r, b_s, b_r, st_s, st_r, sf_s, sf_r, so_s, so_r,
    y_s, y_r, o_s, o_r, r_s, r_r, c_s, c_r,
    f_s, f_r, kv_s, kv_r, z1, z2, z4,
    xs, xr, xls, xlr, zs, zr, zls, zlr, as_, ar, bs, br,
):
    s = lax.axis_index("sensor")
    t = lax.axis_index("tm")
    y, c = s // 2, lax.rem(s, 2)
    z, x = t // NX, lax.rem(t, NX)
    other = 1 - c
    parity = lax.rem(x, 2)

    def at_y(i, core):
        return (lax.rem(y + i, NY) * 2 + core, t)

    def at_x(i):
        return (s, z * NX + lax.rem(x + i, NX))

    def at_z(i):
        return (s, lax.rem(z + i, NZ) * NX + x)

    sibling = (y * 2 + other, t)
    prev_tm = lax.rem(t + 63, 64)
    next_tm = lax.rem(t + 1, 64)
    peers = [(i, k) for i in range(1, NY) for k in range(2)] + [(0, 1)]

    def signal(sem, device):
        pl.semaphore_signal(sem, inc=1, device_id=device, device_id_type=MESH)

    barrier = pltpu.get_barrier_semaphore()
    for i, k in peers:
        signal(barrier, at_y(i, lax.rem(c + k, 2)))
    for i in range(1, NX):
        signal(barrier, at_x(i))
    signal(barrier, at_z(1))
    signal(barrier, at_z(NZ - 1))

    @pl.when((s == 0) | (s == 7))
    def _():
        block = jnp.where(s == 0, prev_tm, next_tm)
        for k in range(8):
            signal(barrier, (k, block))

    def rows(start, size, align):
        return pl.ds(pl.multiple_of(start, align), size)

    def of_head(index):
        return rows(128 * index, 128, 128)

    own_rec = rows(32 * s, 32, 32)
    own_out = rows(64 * s, 64, 64)
    local = [
        pltpu.make_async_copy(cw_ref, wc.at[:, :, own_out, :], loc.at[0]),
        pltpu.make_async_copy(kw_ref, kvw.at[rows(128 * s, 64, 64)], loc.at[1]),
        pltpu.make_async_copy(vw_ref, kvw.at[rows(128 * s + 64, 64, 64)], loc.at[2]),
        pltpu.make_async_copy(q_ref, qa.at[0:64], loc.at[3]),
    ]
    for copy in local:
        copy.start()
    st[own_rec, :] = sw_ref[...]
    bias[s] = jnp.zeros((8, 128), F32)
    bias[s, 0:3, 0:64] = cb_ref[...]

    def rec_window(index):
        start = jnp.clip(index - 1, 0, 5)
        return rows(128 * start, 384, 128), rows(128 * (start - index + 2), 384, 128)

    here_src, here_dst = rec_window(s)
    rec[own_rec, here_dst] = rec_ref[:, here_src]

    pl.semaphore_wait(barrier, 7 + 3 + 2 + 2)

    def remote(src, dst, ssem, rsem, device):
        return pltpu.make_async_remote_copy(
            src_ref=src, dst_ref=dst, send_sem=ssem, recv_sem=rsem,
            device_id=device, device_id_type=MESH,
        )

    def same(ref, ssem, rsem, device):
        return remote(ref, ref, ssem, rsem, device)

    signal(z1.at[0], at_z(1))
    signal(z1.at[1], at_z(NZ - 1))

    def of_sensor(i):
        return lax.rem(y + NY - i, NY) * 2 + c

    st_y = [same(st.at[own_rec], st_s.at[i], st_r.at[i], at_y(i, c)) for i in range(1, NY)]
    st_own = same(st.at[own_rec], so_s, so_r, sibling)
    rec_copies = []
    for n, (i, k) in enumerate(peers):
        core = lax.rem(c + k, 2)
        src, dst = rec_window(lax.rem(y + i, NY) * 2 + core)
        rec_copies.append(
            remote(rec_ref.at[:, src], rec.at[own_rec, dst], rec_s.at[n], rec_r.at[n], at_y(i, core))
        )
    halo = [
        remote(rec_ref.at[:, 896:1024], rec.at[own_rec, 128:256], hal_s.at[0], hal_r.at[s], (0, next_tm)),
        remote(rec_ref.at[:, 0:128], rec.at[own_rec, 384:512], hal_s.at[1], hal_r.at[s], (7, prev_tm)),
    ]
    bias_copies = [
        same(bias.at[s], b_s.at[n], b_r.at[n], at_y(i, lax.rem(c + k, 2)))
        for n, (i, k) in enumerate(peers)
    ]
    def colour(g):
        return lax.rem(x + 2 * z, 4) if g % 2 == 0 else lax.rem(2 * x + z, 4)

    def along(g):
        ways = ((at_x(1), at_x(NX - 1)), (at_z(1), at_z(NZ - 1)))
        return ways if g % 2 == 0 else ways[::-1]

    def piece(g, index, quarter, count=1, lanes=slice(0, 512)):
        if g < 3:
            return wc.at[g, :, rows(64 * index + 16 * quarter, 16 * count, 16), lanes]
        return kvw.at[rows(128 * index + 32 * quarter, 32 * count, 32), lanes]

    def y_copies(g):
        return [
            same(piece(g, s, colour(g)), y_s.at[g, i], y_r.at[g, i], at_y(i, c))
            for i in range(1, NY)
        ]

    def own_copy(g):
        return same(piece(g, s, 0, 4), o_s.at[g], o_r.at[g], sibling)

    def issue(g):
        for copy in y_copies(g):
            copy.start()
        own_copy(g).start()

    def relays(g, i):
        (next_full, prev_full), (next_half, prev_half) = along(g)
        full = piece(g, of_sensor(i), colour(g))
        low_half = piece(g, of_sensor(i), colour(g), 1, slice(0, 256))
        high_half = piece(g, of_sensor(i), colour(g), 1, slice(256, 512))
        return [
            same(full, r_s.at[g, i, 0], r_r.at[g, i, 0], next_full),
            same(full, r_s.at[g, i, 1], r_r.at[g, i, 1], prev_full),
            same(low_half, r_s.at[g, i, 2], r_r.at[g, i, 2], next_half),
            same(high_half, r_s.at[g, i, 3], r_r.at[g, i, 3], prev_half),
        ]

    def to_sibling(g, i, k):
        quarter = lax.rem(colour(g) + k, 4)
        return same(piece(g, of_sensor(i), quarter), c_s.at[g, i, k], c_r.at[g, i, k], sibling)

    def forward_y(g):
        copies = y_copies(g)
        for i in (1, 3, 2):
            copies[i - 1].wait_recv()
            for copy in relays(g, i):
                copy.start()
            to_sibling(g, i, 0).start()

    def forward_relays(g):
        for i in (1, 3, 2):
            copies = relays(g, i)
            copies[0].wait_recv()
            to_sibling(g, i, 3).start()
            copies[1].wait_recv()
            to_sibling(g, i, 1).start()
            copies[2].wait_recv()
            copies[3].wait_recv()
            to_sibling(g, i, 2).start()

    def ready(g):
        own_copy(g).wait_recv()
        for i in range(1, NY):
            for k in range(4):
                to_sibling(g, i, k).wait_recv()

    def sent(g):
        for copy in y_copies(g):
            copy.wait_send()
        own_copy(g).wait_send()
        for i in range(1, NY):
            for copy in relays(g, i):
                copy.wait_send()
            for k in range(4):
                to_sibling(g, i, k).wait_send()


    for copy in local:
        copy.wait()
    issue(0)
    for copy in st_y + [st_own] + halo + rec_copies + bias_copies:
        copy.start()

    first = lax.broadcasted_iota(jnp.int32, (64, LATENTS), 0) == 0
    qa[64:128, :] = jnp.where(first, 1.0, 0.0).astype(BF16)
    va[64:80, :] = jnp.ones((16, 1024), BF16)
    frame = lax.broadcasted_iota(jnp.int32, (64, 1024), 1)
    row = lax.broadcasted_iota(jnp.int32, (64, 1024), 0)
    ka[64:128, :] = jnp.where((row == 0) & (frame >= valid_ref[0]), -1e30, 0.0).astype(BF16)

    def sib_st(i):
        return same(
            st.at[rows(32 * of_sensor(i), 32, 32)], sf_s.at[i], sf_r.at[i], sibling
        )

    forward_y(0)
    issue(1)
    for i in (1, 3, 2):
        st_y[i - 1].wait_recv()
        sib_st(i).start()
    for copy in rec_copies:
        copy.wait_recv()

    @pl.when((s == 0) | (s == 7))
    def _():
        for k in range(8):
            tile = rec.at[0:32, 0:128]
            pltpu.make_async_copy(tile, tile, hal_r.at[k]).wait()

    def turned(tiles, count, amount):
        lane = lax.broadcasted_iota(jnp.int32, tiles[0].shape, 1)
        keep = lane < 128 - amount
        turn = lax.rem(128 - amount, 128)
        rolled = [pltpu.roll(tile, turn, 1) for tile in tiles]
        last = len(tiles) - 1
        return [jnp.where(keep, rolled[k], rolled[min(k + 1, last)]) for k in range(count)]

    window = turned(
        [rec[:, 128 * k : 128 * k + 128].astype(F32) for k in range(1, 4)], 2, jnp.int32(64)
    )
    for k in range(2):
        rwin[:, 128 * k : 128 * k + 128] = window[k].astype(BF16)

    low = jnp.where((t == 0) & (s == 0), 0, -4096)
    high = jnp.where((t == 63) & (s == 7), 128, 4096)

    def inside(lanes, start):
        f = lax.broadcasted_iota(jnp.int32, (128, lanes), 1) + start
        return (f >= low) & (f < high)

    st_own.wait_recv()
    for i in range(1, NY):
        sib_st(i).wait_recv()
    sfull[...] = jnp.transpose(st[...].astype(F32)).astype(BF16)
    for n in range(0, 512, 128):
        part = dot(sfull[n : n + 128, :], rwin[...])
        h0[n : n + 128, :] = jnp.where(inside(256, -64), part, 0.0).astype(BF16)

    for copy in bias_copies:
        copy.wait_recv()
    all_bias = jnp.transpose(
        jnp.concatenate([bias[k][:, 0:64] for k in range(8)], axis=1)
    )

    def conv(layer, source, target, offset, tiles, start):
        d = dil_ref[layer]
        for n in range(0, 512, 128):
            w = wc[layer, :, n : n + 128, :].reshape(384, 512)
            taps[...] = dot(w, source[...])
            a, b, e = [
                turned(
                    [taps[128 * j : 128 * j + 128, 128 * k : 128 * k + 128] for k in range(2)],
                    tiles, offset + (j - 1) * d,
                )
                for j in range(3)
            ]
            r = turned(
                [source[n : n + 128, 128 * k : 128 * k + 128].astype(F32) for k in range(2)],
                tiles, jnp.int32(offset),
            )
            col = all_bias[n : n + 128, layer : layer + 1]
            for k in range(tiles):
                pre = col + a[k] + b[k] + e[k]
                out = r[k] + 0.5 * pre * (1.0 + lax.erf(pre * 0.7071067811865476))
                out = jnp.where(inside(128, start + 128 * k), out, 0.0)
                target[n : n + 128, 128 * k : 128 * k + 128] = out.astype(BF16)

    forward_y(1)
    issue(2)
    pl.semaphore_wait(z1.at[0], 1)
    pl.semaphore_wait(z1.at[1], 1)
    signal(z2.at[0], at_z(2))
    signal(z2.at[1], at_z(NZ - 2))
    forward_relays(0)
    ready(0)
    conv(0, h0, h1, 16, 2, -48)
    forward_y(2)
    issue(3)
    forward_relays(1)
    pl.semaphore_wait(z2.at[0], 1)
    pl.semaphore_wait(z2.at[1], 1)
    signal(z4.at[0], at_z(4))
    signal(z4.at[1], at_z(NZ - 4))
    ready(1)
    conv(1, h1, h2, 16, 2, -32)
    forward_y(3)
    forward_relays(2)
    ready(2)
    conv(2, h2, h3, 32, 1, 0)
    forward_relays(3)
    ready(3)

    own_lanes = rows(128 * s, 128, 128)
    for n in range(0, 1024, 256):
        kv[n : n + 256, :] = dot(kvw[n : n + 256, :], h3[...]).astype(BF16)
    kv_copies = []
    feature_copies = []
    for n, (i, k) in enumerate(peers):
        core = lax.rem(c + k, 2)
        to = lax.rem(y + i, NY) * 2 + core
        kv_copies.append(
            remote(kv.at[of_head(to)], kvall.at[:, own_lanes], kv_s.at[n], kv_r.at[n], at_y(i, core))
        )
        feature_copies.append(
            remote(
                h3.at[rows(64 * to, 64, 64)], feat_ref.at[:, own_lanes],
                f_s.at[n], f_r.at[n], at_y(i, core),
            )
        )
    for copy in kv_copies + feature_copies:
        copy.start()
    kvall[:, own_lanes] = kv[of_head(s), :]
    feat_ref[:, own_lanes] = h3[own_out, :]
    pl.semaphore_wait(z4.at[0], 1)
    pl.semaphore_wait(z4.at[1], 1)
    for copy in st_y + [st_own] + rec_copies + halo + bias_copies:
        copy.wait_send()
    for i in range(1, NY):
        sib_st(i).wait_send()
    for g in range(4):
        sent(g)
    for copy in kv_copies:
        copy.wait()
    ka[0:64, :] = (kvall[0:64, :].astype(F32) * 0.125).astype(BF16)
    va[0:64, :] = kvall[64:128, :]
    kt[...] = jnp.transpose(ka[...].astype(F32)).astype(BF16)

    def attend(quarter, slot):
        def block(j, carry):
            lanes = pl.ds(pl.multiple_of(quarter * QUARTER + j * LB, LB), LB)
            scores = dot(kt[...], qa[:, lanes])
            peak = jnp.max(scores, axis=0, keepdims=True)
            probs = jnp.exp(scores - peak).astype(BF16)
            both = dot(va[...], probs)
            total = both[64:65, :]
            here = pl.ds(pl.multiple_of(j * LB, LB), LB)
            xsend[slot, :, here] = (both[0:64, :] / total).astype(BF16)
            xlse_send[slot, :, here] = peak + jnp.log(total)
            return carry

        lax.fori_loop(0, QUARTER // LB, block, 0)

    def x_copies(i):
        device = at_x(i)
        return (
            pltpu.make_async_remote_copy(
                src_ref=xsend.at[i], dst_ref=xrecv.at[i], send_sem=xs.at[i], recv_sem=xr.at[i],
                device_id=device, device_id_type=MESH),
            pltpu.make_async_remote_copy(
                src_ref=xlse_send.at[i], dst_ref=xlse.at[i], send_sem=xls.at[i], recv_sem=xlr.at[i],
                device_id=device, device_id_type=MESH),
        )

    def peer_quarter(i, carry):
        attend(lax.rem(x + i, NX), i)
        for copy in x_copies(i):
            copy.start()
        return carry

    lax.fori_loop(1, NX, peer_quarter, 0)
    attend(x, 0)

    def merge(parts, lses):
        peak = lses[0]
        for v in lses[1:]:
            peak = jnp.maximum(peak, v)
        total = jnp.zeros_like(peak)
        out = None
        for part, v in zip(parts, lses):
            weight = jnp.exp(v - peak)
            total = total + weight
            term = part.astype(F32) * weight
            out = term if out is None else out + term
        return out / total, peak + jnp.log(total)

    for i in range(1, NX):
        for copy in x_copies(i):
            copy.wait()
    for b in range(4):
        lanes = slice(128 * b, 128 * b + 128)
        out, lse = merge(
            [xsend[0, :, lanes]] + [xrecv[i, :, lanes] for i in range(1, NX)],
            [xlse_send[0, :, lanes]] + [xlse[i, :, lanes] for i in range(1, NX)],
        )
        zsend[:, lanes] = out.astype(BF16)
        zlse_send[b] = lse

    def tile_of(zz):
        a, b = zz // 4, lax.rem(zz, 4)
        return pl.ds(pl.multiple_of(16 * a, 16), 16), pl.ds(pl.multiple_of(128 * b, 128), 128), b

    def z_copies(i):
        rows, lanes, b = tile_of(lax.rem(z + i, NZ))
        device = at_z(i)
        return (
            pltpu.make_async_remote_copy(
                src_ref=zsend.at[rows, lanes], dst_ref=zrecv.at[i], send_sem=zs.at[i],
                recv_sem=zr.at[i], device_id=device, device_id_type=MESH),
            pltpu.make_async_remote_copy(
                src_ref=zlse_send.at[b], dst_ref=zlse.at[i], send_sem=zls.at[i],
                recv_sem=zlr.at[i], device_id=device, device_id_type=MESH),
        )

    def far_first(n):
        k = (n + 1) // 2
        return 8 + k * (1 - 2 * lax.rem(n, 2))

    def near_first(n):
        return far_first(14 - n)

    def z_start(n, carry):
        for copy in z_copies(far_first(n)):
            copy.start()
        return carry

    def z_wait(n, carry):
        for copy in z_copies(near_first(n)):
            copy.wait()
        return carry

    lax.fori_loop(0, NZ - 1, z_start, 0)
    my_rows, my_lanes, my_b = tile_of(z)
    zrecv[0] = zsend[my_rows, my_lanes]
    zlse[0] = zlse_send[my_b]
    lax.fori_loop(0, NZ - 1, z_wait, 0)
    out, _ = merge([zrecv[i] for i in range(NZ)], [zlse[i] for i in range(NZ)])

    def out_tile(zz):
        rows, _, b = tile_of(zz)
        return rows, pl.ds(pl.multiple_of(512 * x + 128 * b, 128), 128)

    rows, lanes = out_tile(z)
    att_ref[rows, lanes] = out.astype(BF16)

    def a_copy(i, zz):
        tile = att_ref.at[out_tile(zz)]
        return pltpu.make_async_remote_copy(
            src_ref=tile, dst_ref=tile, send_sem=as_.at[i], recv_sem=ar.at[i],
            device_id=at_z(i), device_id_type=MESH)

    def spread(zz):
        tile = att_ref.at[out_tile(zz)]
        for i in range(1, NX):
            remote(tile, tile, bs.at[i], br.at[i], at_x(i)).start()

    def a_start(n, carry):
        a_copy(far_first(n), z).start()
        return carry

    def a_forward(n, carry):
        i = near_first(n)
        zz = lax.rem(z + NZ - i, NZ)
        a_copy(i, zz).wait_recv()
        spread(zz)
        return carry

    def a_done(i, carry):
        a_copy(i, z).wait_send()
        return carry

    lax.fori_loop(0, NZ - 1, a_start, 0)
    spread(z)
    lax.fori_loop(0, NZ - 1, a_forward, 0)
    for i in range(1, NX):
        quarter = att_ref.at[:, pl.ds(pl.multiple_of(512 * x, 512), 512)]
        whole = pltpu.make_async_remote_copy(
            src_ref=quarter, dst_ref=quarter, send_sem=bs.at[i], recv_sem=br.at[i],
            device_id=at_x(i), device_id_type=MESH)
        whole.wait_recv()
        whole.wait_send()
    lax.fori_loop(1, NZ, a_done, 0)
    for copy in feature_copies:
        copy.wait()


def on_device(recording, spatial_w, conv_w, conv_b, dilations, valid_frames, key_w, value_w, queries):
    vmem = pl.BlockSpec(memory_space=pltpu.VMEM)
    smem = pl.BlockSpec(memory_space=pltpu.SMEM)
    hbm = pl.BlockSpec(memory_space=pl.ANY)
    dma = pltpu.SemaphoreType.DMA
    regular = pltpu.SemaphoreType.REGULAR
    V = pltpu.VMEM
    return pl.pallas_call(
        kernel,
        out_shape=(
            jax.ShapeDtypeStruct((64, 1024), BF16),
            jax.ShapeDtypeStruct((64, LATENTS), BF16),
        ),
        in_specs=[smem, smem, vmem, vmem, hbm, vmem, hbm, hbm, hbm],
        out_specs=(vmem, vmem),
        scratch_shapes=[
            V((256, 512), BF16), V((512, 256), BF16), V((256, 640), BF16), V((256, 256), BF16),
            V((3, 3, 512, 512), BF16), V((8, 8, 128), F32), V((1024, 512), BF16),
            V((512, 256), BF16), V((512, 256), BF16), V((512, 256), BF16), V((512, 128), BF16),
            V((384, 256), F32), V((1024, 128), BF16), V((128, 1024), BF16),
            V((128, 1024), BF16), V((1024, 128), BF16), V((80, 1024), BF16), V((128, LATENTS), BF16),
            V((4, 64, 512), BF16), V((4, 1, 512), F32), V((4, 64, 512), BF16), V((4, 1, 512), F32),
            V((64, 512), BF16), V((4, 1, 128), F32), V((16, 16, 128), BF16), V((16, 1, 128), F32),
            dma((4,)), dma((7,)), dma((7,)), dma((2,)), dma((8,)), dma((7,)), dma((7,)),
            dma((4,)), dma((4,)), dma((4,)), dma((4,)), dma, dma,
            dma((4, 4)), dma((4, 4)), dma((4,)), dma((4,)),
            dma((4, 4, 4)), dma((4, 4, 4)), dma((4, 4, 4)), dma((4, 4, 4)),
            dma((7,)), dma((7,)), dma((7,)), dma((7,)),
            regular((2,)), regular((2,)), regular((2,)),
            dma((4,)), dma((4,)), dma((4,)), dma((4,)),
            dma((16,)), dma((16,)), dma((16,)), dma((16,)),
            dma((16,)), dma((16,)), dma((4,)), dma((4,)),
        ],
        compiler_params=pltpu.CompilerParams(
            collective_id=0, has_side_effects=True, vmem_limit_bytes=56 * 2**20
        ),
        name="encoder",
    )(dilations, valid_frames, recording, spatial_w.T, conv_w, conv_b, key_w, value_w, queries)


def solution(mesh):
    return jax.shard_map(
        on_device,
        mesh=mesh,
        in_specs=(
            P("sensor", "tm"),
            P(None, "sensor"),
            P(None, None, "sensor", None),
            P(None, "sensor"),
            P(),
            P("tm"),
            P("sensor", None),
            P("sensor", None),
            P("sensor", None),
        ),
        out_specs=(P("sensor", "tm"), P("sensor", None)),
        check_vma=False,
    )
```

```python
import jax
import jax.numpy as jnp
from jax import lax
from jax.experimental import pallas as pl
from jax.experimental.pallas import tpu as pltpu
from jax.sharding import PartitionSpec as P

MESH = pl.DeviceIdType.MESH
BF16 = jnp.bfloat16
F32 = jnp.float32
NY, NX, NZ = 4, 4, 16
HD = 64
LATENTS = 2048
QUARTER = 512
LB = 256


def dot(a, b):
    return jnp.dot(a, b, preferred_element_type=F32)


def kernel(
    dil_ref, valid_ref, rec_ref, sw_ref, cw_ref, cb_ref, kw_ref, vw_ref, q_ref,
    feat_ref, att_ref,
    st, sfull, rec, rwin, wc, bias, kvw, h0, h1, h2, h3, taps, kv, kvall, ka, kt, va, qa,
    score0, score1, xsend, xlse_send, xrecv, xlse, zsend, zlse_send, zrecv, zlse,
    loc, rec_s, rec_r, hal_s, hal_r, b_s, b_r, st_s, st_r, sf_s, sf_r, so_s, so_r,
    y_s, y_r, o_s, o_r, r_s, r_r, c_s, c_r,
    f_s, f_r, kv_s, kv_r, z1, z2, z4,
    xs, xr, xls, xlr, zs, zr, zls, zlr, as_, ar, bs, br,
):
    s = lax.axis_index("sensor")
    t = lax.axis_index("tm")
    y, c = s // 2, lax.rem(s, 2)
    z, x = t // NX, lax.rem(t, NX)
    other = 1 - c
    parity = lax.rem(x, 2)

    def at_y(i, core):
        return (lax.rem(y + i, NY) * 2 + core, t)

    def at_x(i):
        return (s, z * NX + lax.rem(x + i, NX))

    def at_z(i):
        return (s, lax.rem(z + i, NZ) * NX + x)

    sibling = (y * 2 + other, t)
    prev_tm = lax.rem(t + 63, 64)
    next_tm = lax.rem(t + 1, 64)
    peers = [(i, k) for i in range(1, NY) for k in range(2)] + [(0, 1)]

    def signal(sem, device):
        pl.semaphore_signal(sem, inc=1, device_id=device, device_id_type=MESH)

    barrier = pltpu.get_barrier_semaphore()
    for i, k in peers:
        signal(barrier, at_y(i, lax.rem(c + k, 2)))
    for i in range(1, NX):
        signal(barrier, at_x(i))
    signal(barrier, at_z(1))
    signal(barrier, at_z(NZ - 1))

    @pl.when((s == 0) | (s == 7))
    def _():
        block = jnp.where(s == 0, prev_tm, next_tm)
        for k in range(8):
            signal(barrier, (k, block))

    def rows(start, size, align):
        return pl.ds(pl.multiple_of(start, align), size)

    def of_head(index):
        return rows(128 * index, 128, 128)

    own_rec = rows(32 * s, 32, 32)
    own_out = rows(64 * s, 64, 64)
    local = [
        pltpu.make_async_copy(cw_ref, wc.at[:, :, :, c, 0], loc.at[0]),
        pltpu.make_async_copy(kw_ref, kvw.at[0:2, c, 0], loc.at[1]),
        pltpu.make_async_copy(vw_ref, kvw.at[2:4, c, 0], loc.at[2]),
        pltpu.make_async_copy(q_ref, qa.at[0:64], loc.at[3]),
    ]
    for copy in local:
        copy.start()
    st[own_rec, :] = sw_ref[...]
    bias[c, 0] = jnp.zeros((8, 128), F32)
    bias[c, 0, 0:3, 0:64] = cb_ref[...]

    def rec_window(index):
        start = jnp.clip(index - 1, 0, 5)
        return rows(128 * start, 384, 128), rows(128 * (start - index + 2), 384, 128)

    here_src, here_dst = rec_window(s)
    rec[own_rec, here_dst] = rec_ref[:, here_src]

    pl.semaphore_wait(barrier, 7 + 3 + 2 + 2)

    def remote(src, dst, ssem, rsem, device):
        return pltpu.make_async_remote_copy(
            src_ref=src, dst_ref=dst, send_sem=ssem, recv_sem=rsem,
            device_id=device, device_id_type=MESH,
        )

    def same(ref, ssem, rsem, device):
        return remote(ref, ref, ssem, rsem, device)

    signal(z1.at[0], at_z(1))
    signal(z1.at[1], at_z(NZ - 1))

    def of_sensor(i):
        return lax.rem(y + NY - i, NY) * 2 + c

    st_y = [same(st.at[own_rec], st_s.at[i], st_r.at[i], at_y(i, c)) for i in range(1, NY)]
    st_own = same(st.at[own_rec], so_s, so_r, sibling)
    rec_copies = []
    for n, (i, k) in enumerate(peers):
        core = lax.rem(c + k, 2)
        src, dst = rec_window(lax.rem(y + i, NY) * 2 + core)
        rec_copies.append(
            remote(rec_ref.at[:, src], rec.at[own_rec, dst], rec_s.at[n], rec_r.at[n], at_y(i, core))
        )
    halo = [
        remote(rec_ref.at[:, 896:1024], rec.at[own_rec, 128:256], hal_s.at[0], hal_r.at[s], (0, next_tm)),
        remote(rec_ref.at[:, 0:128], rec.at[own_rec, 384:512], hal_s.at[1], hal_r.at[s], (7, prev_tm)),
    ]
    bias_copies = [
        remote(bias.at[c, 0], bias.at[c, i], b_s.at[n], b_r.at[n], at_y(i, lax.rem(c + k, 2)))
        for n, (i, k) in enumerate(peers)
    ]

    def colour(g):
        return lax.rem(x + 2 * z, 4) if g % 2 == 0 else lax.rem(2 * x + z, 4)

    def along(g):
        ways = ((at_x(1), at_x(NX - 1)), (at_z(1), at_z(NZ - 1)))
        return ways if g % 2 == 0 else ways[::-1]

    def piece(g, quarter, core, blocks, lanes=slice(0, 512)):
        if g < 3:
            return wc.at[g, :, quarter, core, blocks, :, lanes]
        return kvw.at[quarter, core, blocks, :, lanes]

    def y_copies(g):
        return [
            remote(
                piece(g, colour(g), c, 0), piece(g, colour(g), c, i),
                y_s.at[g, i], y_r.at[g, i], at_y(i, c),
            )
            for i in range(1, NY)
        ]

    def own_copy(g):
        own = wc.at[g, :, :, c, 0] if g < 3 else kvw.at[:, c, 0]
        return same(own, o_s.at[g], o_r.at[g], sibling)

    def issue(g):
        for copy in y_copies(g):
            copy.start()
        own_copy(g).start()

    others = slice(1, NY)

    def relays(g):
        (next_full, prev_full), (next_half, prev_half) = along(g)
        full = piece(g, colour(g), c, others)
        low_half = piece(g, colour(g), c, others, slice(0, 256))
        high_half = piece(g, colour(g), c, others, slice(256, 512))
        return [
            same(full, r_s.at[g, 0], r_r.at[g, 0], next_full),
            same(full, r_s.at[g, 1], r_r.at[g, 1], prev_full),
            same(low_half, r_s.at[g, 2], r_r.at[g, 2], next_half),
            same(high_half, r_s.at[g, 3], r_r.at[g, 3], prev_half),
        ]

    def to_sibling(g, k):
        quarter = lax.rem(colour(g) + k, 4)
        return same(piece(g, quarter, c, others), c_s.at[g, k], c_r.at[g, k], sibling)

    def forward_y(g):
        for copy in y_copies(g):
            copy.wait_recv()
        for copy in relays(g):
            copy.start()
        to_sibling(g, 0).start()

    def forward_relays(g):
        copies = relays(g)
        copies[0].wait_recv()
        to_sibling(g, 3).start()
        copies[1].wait_recv()
        to_sibling(g, 1).start()
        copies[2].wait_recv()
        copies[3].wait_recv()
        to_sibling(g, 2).start()

    def ready(g):
        own_copy(g).wait_recv()
        for k in range(4):
            to_sibling(g, k).wait_recv()

    def sent(g):
        for copy in y_copies(g) + relays(g):
            copy.wait_send()
        own_copy(g).wait_send()
        for k in range(4):
            to_sibling(g, k).wait_send()

    for copy in local:
        copy.wait()
    issue(0)
    for copy in st_y + [st_own] + halo + rec_copies + bias_copies:
        copy.start()
    issue(1)

    first = lax.broadcasted_iota(jnp.int32, (64, LATENTS), 0) == 0
    qa[64:128, :] = jnp.where(first, 1.0, 0.0).astype(BF16)
    va[64:80, :] = jnp.ones((16, 1024), BF16)
    frame = lax.broadcasted_iota(jnp.int32, (64, 1024), 1)
    row = lax.broadcasted_iota(jnp.int32, (64, 1024), 0)
    ka[64:128, :] = jnp.where((row == 0) & (frame >= valid_ref[0]), -1e30, 0.0).astype(BF16)

    def sib_st(i):
        return same(
            st.at[rows(32 * of_sensor(i), 32, 32)], sf_s.at[i], sf_r.at[i], sibling
        )

    forward_y(0)
    issue(2)
    for i in (1, 3, 2):
        st_y[i - 1].wait_recv()
        sib_st(i).start()
    for copy in rec_copies:
        copy.wait_recv()

    @pl.when((s == 0) | (s == 7))
    def _():
        for k in range(8):
            tile = rec.at[0:32, 0:128]
            pltpu.make_async_copy(tile, tile, hal_r.at[k]).wait()

    def turned(tiles, count, amount):
        lane = lax.broadcasted_iota(jnp.int32, tiles[0].shape, 1)
        keep = lane < 128 - amount
        turn = lax.rem(128 - amount, 128)
        rolled = [pltpu.roll(tile, turn, 1) for tile in tiles]
        last = len(tiles) - 1
        return [jnp.where(keep, rolled[k], rolled[min(k + 1, last)]) for k in range(count)]

    window = turned(
        [rec[:, 128 * k : 128 * k + 128].astype(F32) for k in range(1, 4)], 2, jnp.int32(64)
    )
    for k in range(2):
        rwin[:, 128 * k : 128 * k + 128] = window[k].astype(BF16)

    low = jnp.where((t == 0) & (s == 0), 0, -4096)
    high = jnp.where((t == 63) & (s == 7), 128, 4096)

    def inside(lanes, start):
        f = lax.broadcasted_iota(jnp.int32, (128, lanes), 1) + start
        return (f >= low) & (f < high)

    st_own.wait_recv()
    for i in range(1, NY):
        sib_st(i).wait_recv()
    sfull[...] = jnp.transpose(st[...].astype(F32)).astype(BF16)
    for n in range(0, 512, 128):
        part = dot(sfull[n : n + 128, :], rwin[...])
        h0[n : n + 128, :] = jnp.where(inside(256, -64), part, 0.0).astype(BF16)

    for copy in bias_copies:
        copy.wait_recv()
    order = [(core, i) for core in range(2) for i in range(NY)]
    place = [2 * lax.rem(y + NY - i, NY) + core for core, i in order]
    columns = [jnp.transpose(bias[core, i]) for core, i in order]

    def conv(layer, source, target, offset, tiles, start):
        d = dil_ref[layer]
        for q in range(4):
            w = wc[layer, :, q].reshape(384, 512)
            taps[...] = dot(w, source[...])
            here = [rows(64 * p + 16 * q, 16, 16) for p in place]
            old = jnp.concatenate([source[h, :] for h in here], axis=0).astype(F32)
            col = jnp.concatenate([v[16 * q : 16 * q + 16] for v in columns], axis=0)
            col = col[:, layer : layer + 1]
            a, b, e = [
                turned(
                    [taps[128 * j : 128 * j + 128, 128 * k : 128 * k + 128] for k in range(2)],
                    tiles, offset + (j - 1) * d,
                )
                for j in range(3)
            ]
            r = turned([old[:, 0:128], old[:, 128:256]], tiles, jnp.int32(offset))
            for k in range(tiles):
                pre = col + a[k] + b[k] + e[k]
                out = r[k] + 0.5 * pre * (1.0 + lax.erf(pre * 0.7071067811865476))
                out = jnp.where(inside(128, start + 128 * k), out, 0.0).astype(BF16)
                for n, h in enumerate(here):
                    target[h, 128 * k : 128 * k + 128] = out[16 * n : 16 * n + 16]

    forward_y(1)
    issue(3)
    pl.semaphore_wait(z1.at[0], 1)
    pl.semaphore_wait(z1.at[1], 1)
    signal(z2.at[0], at_z(2))
    signal(z2.at[1], at_z(NZ - 2))
    forward_relays(0)
    ready(0)
    conv(0, h0, h1, 16, 2, -48)
    forward_y(2)
    forward_relays(1)
    pl.semaphore_wait(z2.at[0], 1)
    pl.semaphore_wait(z2.at[1], 1)
    signal(z4.at[0], at_z(4))
    signal(z4.at[1], at_z(NZ - 4))
    ready(1)
    conv(1, h1, h2, 16, 2, -32)
    forward_y(3)
    forward_relays(2)
    ready(2)
    conv(2, h2, h3, 32, 1, 0)
    forward_relays(3)
    ready(3)

    own_lanes = rows(128 * s, 128, 128)
    for q in range(4):
        part = dot(kvw[q].reshape(256, 512), h3[...]).astype(BF16)
        for n, p in enumerate(place):
            kv[rows(128 * p + 32 * q, 32, 32), :] = part[32 * n : 32 * n + 32]
    kv_copies = []
    feature_copies = []
    for n, (i, k) in enumerate(peers):
        core = lax.rem(c + k, 2)
        to = lax.rem(y + i, NY) * 2 + core
        kv_copies.append(
            remote(kv.at[of_head(to)], kvall.at[:, own_lanes], kv_s.at[n], kv_r.at[n], at_y(i, core))
        )
        feature_copies.append(
            remote(
                h3.at[rows(64 * to, 64, 64)], feat_ref.at[:, own_lanes],
                f_s.at[n], f_r.at[n], at_y(i, core),
            )
        )
    for copy in kv_copies + feature_copies:
        copy.start()
    kvall[:, own_lanes] = kv[of_head(s), :]
    feat_ref[:, own_lanes] = h3[own_out, :]
    for copy in st_y + [st_own] + rec_copies + halo + bias_copies:
        copy.wait_send()
    for i in range(1, NY):
        sib_st(i).wait_send()
    for g in range(4):
        sent(g)
    for copy in kv_copies:
        copy.wait()
    ka[0:64, :] = (kvall[0:64, :].astype(F32) * 0.125).astype(BF16)
    va[0:64, :] = kvall[64:128, :]
    kt[...] = jnp.transpose(ka[...].astype(F32)).astype(BF16)

    def block_lanes(quarter, j):
        return pl.ds(pl.multiple_of(quarter * QUARTER + j * LB, LB), LB)

    def finish(scores, slot, j):
        peak = jnp.max(scores[...], axis=0, keepdims=True)
        probs = jnp.exp(scores[...] - peak).astype(BF16)
        both = dot(va[...], probs)
        total = both[64:65, :]
        here = slice(j * LB, j * LB + LB)
        xsend[slot, :, here] = (both[0:64, :] / total).astype(BF16)
        xlse_send[slot, :, here] = peak + jnp.log(total)

    def x_copies(i):
        device = at_x(i)
        return (
            pltpu.make_async_remote_copy(
                src_ref=xsend.at[i], dst_ref=xrecv.at[i], send_sem=xs.at[i], recv_sem=xr.at[i],
                device_id=device, device_id_type=MESH),
            pltpu.make_async_remote_copy(
                src_ref=xlse_send.at[i], dst_ref=xlse.at[i], send_sem=xls.at[i], recv_sem=xlr.at[i],
                device_id=device, device_id_type=MESH),
        )

    def attend(n, carry):
        quarter = lax.rem(x + n + 1, NX)
        slot = lax.rem(n + 1, NX)
        score1[...] = dot(kt[...], qa[:, block_lanes(quarter, 1)])
        finish(score0, slot, 0)
        score0[...] = dot(kt[...], qa[:, block_lanes(lax.rem(quarter + 1, NX), 0)])
        finish(score1, slot, 1)

        @pl.when(n < NX - 1)
        def _():
            for copy in x_copies(n + 1):
                copy.start()

        return carry

    score0[...] = dot(kt[...], qa[:, block_lanes(lax.rem(x + 1, NX), 0)])
    lax.fori_loop(0, NX, attend, 0)

    def merge(parts, lses):
        peak = lses[0]
        for v in lses[1:]:
            peak = jnp.maximum(peak, v)
        total = jnp.zeros_like(peak)
        out = None
        for part, v in zip(parts, lses):
            weight = jnp.exp(v - peak)
            total = total + weight
            term = part.astype(F32) * weight
            out = term if out is None else out + term
        return out / total, peak + jnp.log(total)

    for i in range(1, NX):
        for copy in x_copies(i):
            copy.wait()
    for b in range(4):
        lanes = slice(128 * b, 128 * b + 128)
        out, lse = merge(
            [xsend[0, :, lanes]] + [xrecv[i, :, lanes] for i in range(1, NX)],
            [xlse_send[0, :, lanes]] + [xlse[i, :, lanes] for i in range(1, NX)],
        )
        zsend[:, lanes] = out.astype(BF16)
        zlse_send[b] = lse

    pl.semaphore_wait(z4.at[0], 1)
    pl.semaphore_wait(z4.at[1], 1)

    def tile_of(zz):
        a, b = zz // 4, lax.rem(zz, 4)
        return pl.ds(pl.multiple_of(16 * a, 16), 16), pl.ds(pl.multiple_of(128 * b, 128), 128), b

    def z_copies(i):
        rows, lanes, b = tile_of(lax.rem(z + i, NZ))
        device = at_z(i)
        return (
            pltpu.make_async_remote_copy(
                src_ref=zsend.at[rows, lanes], dst_ref=zrecv.at[i], send_sem=zs.at[i],
                recv_sem=zr.at[i], device_id=device, device_id_type=MESH),
            pltpu.make_async_remote_copy(
                src_ref=zlse_send.at[b], dst_ref=zlse.at[i], send_sem=zls.at[i],
                recv_sem=zlr.at[i], device_id=device, device_id_type=MESH),
        )

    def far_first(n):
        k = (n + 1) // 2
        return 8 + k * (1 - 2 * lax.rem(n, 2))

    def near_first(n):
        return far_first(14 - n)

    def z_start(n, carry):
        for copy in z_copies(far_first(n)):
            copy.start()
        return carry

    def z_wait(n, carry):
        for copy in z_copies(near_first(n)):
            copy.wait()
        return carry

    lax.fori_loop(0, NZ - 1, z_start, 0)
    my_rows, my_lanes, my_b = tile_of(z)
    zrecv[0] = zsend[my_rows, my_lanes]
    zlse[0] = zlse_send[my_b]
    lax.fori_loop(0, NZ - 1, z_wait, 0)
    out, _ = merge([zrecv[i] for i in range(NZ)], [zlse[i] for i in range(NZ)])

    def out_tile(zz):
        rows, _, b = tile_of(zz)
        return rows, pl.ds(pl.multiple_of(512 * x + 128 * b, 128), 128)

    rows, lanes = out_tile(z)
    att_ref[rows, lanes] = out.astype(BF16)

    def a_copy(i, zz):
        tile = att_ref.at[out_tile(zz)]
        return pltpu.make_async_remote_copy(
            src_ref=tile, dst_ref=tile, send_sem=as_.at[i], recv_sem=ar.at[i],
            device_id=at_z(i), device_id_type=MESH)

    def spread(da):
        a = lax.rem(z // 4 + da + 4, 4)
        strip = att_ref.at[
            pl.ds(pl.multiple_of(16 * a, 16), 16), pl.ds(pl.multiple_of(512 * x, 512), 512)
        ]
        for i in range(1, NX):
            remote(strip, strip, bs.at[i], br.at[i], at_x(i)).start()

    def a_start(n, carry):
        a_copy(far_first(n), z).start()
        return carry

    def a_arrived(i, zz):
        a_copy(i, zz).wait_recv()

    def a_done(i, carry):
        a_copy(i, z).wait_send()
        return carry

    lax.fori_loop(0, NZ - 1, a_start, 0)
    for da in (0, 1, -1, 2):
        for b in range(4):
            zz = 4 * lax.rem(z // 4 + da + 4, 4) + b
            i = lax.rem(z - zz + NZ, NZ)
            if da == 0:
                pl.when(i != 0)(lambda: a_arrived(i, zz))
            else:
                a_arrived(i, zz)
        spread(da)
    for i in range(1, NX):
        quarter = att_ref.at[:, pl.ds(pl.multiple_of(512 * x, 512), 512)]
        whole = pltpu.make_async_remote_copy(
            src_ref=quarter, dst_ref=quarter, send_sem=bs.at[i], recv_sem=br.at[i],
            device_id=at_x(i), device_id_type=MESH)
        whole.wait_recv()
        whole.wait_send()
    lax.fori_loop(1, NZ, a_done, 0)
    for copy in feature_copies:
        copy.wait()


def on_device(recording, spatial_w, conv_w, conv_b, dilations, valid_frames, key_w, value_w, queries):
    vmem = pl.BlockSpec(memory_space=pltpu.VMEM)
    smem = pl.BlockSpec(memory_space=pltpu.SMEM)
    hbm = pl.BlockSpec(memory_space=pl.ANY)
    dma = pltpu.SemaphoreType.DMA
    regular = pltpu.SemaphoreType.REGULAR
    V = pltpu.VMEM
    return pl.pallas_call(
        kernel,
        out_shape=(
            jax.ShapeDtypeStruct((64, 1024), BF16),
            jax.ShapeDtypeStruct((64, LATENTS), BF16),
        ),
        in_specs=[smem, smem, vmem, vmem, hbm, vmem, hbm, hbm, hbm],
        out_specs=(vmem, vmem),
        scratch_shapes=[
            V((256, 512), BF16), V((512, 256), BF16), V((256, 640), BF16), V((256, 256), BF16),
            V((3, 3, 4, 2, 4, 16, 512), BF16), V((2, 4, 8, 128), F32), V((4, 2, 4, 32, 512), BF16),
            V((512, 256), BF16), V((512, 256), BF16), V((512, 256), BF16), V((512, 128), BF16),
            V((384, 256), F32), V((1024, 128), BF16), V((128, 1024), BF16),
            V((128, 1024), BF16), V((1024, 128), BF16), V((80, 1024), BF16), V((128, LATENTS), BF16),
            V((1024, LB), F32), V((1024, LB), F32),
            V((4, 64, 512), BF16), V((4, 1, 512), F32), V((4, 64, 512), BF16), V((4, 1, 512), F32),
            V((64, 512), BF16), V((4, 1, 128), F32), V((16, 16, 128), BF16), V((16, 1, 128), F32),
            dma((4,)), dma((7,)), dma((7,)), dma((2,)), dma((8,)), dma((7,)), dma((7,)),
            dma((4,)), dma((4,)), dma((4,)), dma((4,)), dma, dma,
            dma((4, 4)), dma((4, 4)), dma((4,)), dma((4,)),
            dma((4, 4)), dma((4, 4)), dma((4, 4)), dma((4, 4)),
            dma((7,)), dma((7,)), dma((7,)), dma((7,)),
            regular((2,)), regular((2,)), regular((2,)),
            dma((4,)), dma((4,)), dma((4,)), dma((4,)),
            dma((16,)), dma((16,)), dma((16,)), dma((16,)),
            dma((16,)), dma((16,)), dma((4,)), dma((4,)),
        ],
        compiler_params=pltpu.CompilerParams(
            collective_id=0, has_side_effects=True, vmem_limit_bytes=56 * 2**20
        ),
        name="encoder",
    )(
        dilations, valid_frames, recording, spatial_w.T, conv_w.reshape(3, 3, 4, 16, 512), conv_b,
        key_w.reshape(2, 32, 512), value_w.reshape(2, 32, 512), queries,
    )


def solution(mesh):
    return jax.shard_map(
        on_device,
        mesh=mesh,
        in_specs=(
            P("sensor", "tm"),
            P(None, "sensor"),
            P(None, None, "sensor", None),
            P(None, "sensor"),
            P(),
            P("tm"),
            P("sensor", None),
            P("sensor", None),
            P("sensor", None),
        ),
        out_specs=(P("sensor", "tm"), P("sensor", None)),
        check_vma=False,
    )
```

```python
import jax
import jax.numpy as jnp
from jax import lax
from jax.experimental import pallas as pl
from jax.experimental.pallas import tpu as pltpu
from jax.sharding import PartitionSpec as P

MESH = pl.DeviceIdType.MESH
BF16 = jnp.bfloat16
F32 = jnp.float32
NY, NX, NZ = 4, 4, 16
HD = 64
LATENTS = 2048
QUARTER = 512
LB = 256


def dot(a, b):
    return jnp.dot(a, b, preferred_element_type=F32)


def kernel(
    dil_ref, valid_ref, rec_ref, sw_ref, cw_ref, cb_ref, kw_ref, vw_ref, q_ref,
    feat_ref, att_ref,
    st, sfull, rec, rwin, wc, bias, kvw, h0, h1, h2, h3, taps, kv, kvall, ka, kt, va, qa,
    score0, score1, xsend, xlse_send, xrecv, xlse, zsend, zlse_send, zrecv, zlse,
    loc, rec_s, rec_r, hal_s, hal_r, b_s, b_r, st_s, st_r, sf_s, sf_r, so_s, so_r,
    y_s, y_r, o_s, o_r, r_s, r_r, c_s, c_r,
    f_s, f_r, kv_s, kv_r, z1, z2, z4,
    xs, xr, xls, xlr, zs, zr, zls, zlr, as_, ar, bs, br,
):
    s = lax.axis_index("sensor")
    t = lax.axis_index("tm")
    y, c = s // 2, lax.rem(s, 2)
    z, x = t // NX, lax.rem(t, NX)
    other = 1 - c
    parity = lax.rem(x, 2)

    def at_y(i, core):
        return (lax.rem(y + i, NY) * 2 + core, t)

    def at_x(i):
        return (s, z * NX + lax.rem(x + i, NX))

    def at_z(i):
        return (s, lax.rem(z + i, NZ) * NX + x)

    sibling = (y * 2 + other, t)
    prev_tm = lax.rem(t + 63, 64)
    next_tm = lax.rem(t + 1, 64)
    peers = [(i, k) for i in range(1, NY) for k in range(2)] + [(0, 1)]

    def signal(sem, device):
        pl.semaphore_signal(sem, inc=1, device_id=device, device_id_type=MESH)

    barrier = pltpu.get_barrier_semaphore()
    for i, k in peers:
        signal(barrier, at_y(i, lax.rem(c + k, 2)))
    for i in range(1, NX):
        signal(barrier, at_x(i))
    signal(barrier, at_z(1))
    signal(barrier, at_z(NZ - 1))

    @pl.when((s == 0) | (s == 7))
    def _():
        block = jnp.where(s == 0, prev_tm, next_tm)
        for k in range(8):
            signal(barrier, (k, block))

    def rows(start, size, align):
        return pl.ds(pl.multiple_of(start, align), size)

    def of_head(index):
        return rows(128 * index, 128, 128)

    own_rec = rows(32 * s, 32, 32)
    own_out = rows(64 * s, 64, 64)
    local = [
        pltpu.make_async_copy(cw_ref, wc.at[:, :, :, c, 0], loc.at[0]),
        pltpu.make_async_copy(kw_ref, kvw.at[0:2, c, 0], loc.at[1]),
        pltpu.make_async_copy(vw_ref, kvw.at[2:4, c, 0], loc.at[2]),
        pltpu.make_async_copy(q_ref, qa.at[0:64], loc.at[3]),
    ]
    for copy in local:
        copy.start()
    st[own_rec, :] = sw_ref[...]
    bias[c, 0] = jnp.zeros((8, 128), F32)
    bias[c, 0, 0:3, 0:64] = cb_ref[...]

    def rec_window(index):
        start = jnp.clip(index - 1, 0, 5)
        return rows(128 * start, 384, 128), rows(128 * (start - index + 2), 384, 128)

    here_src, here_dst = rec_window(s)
    rec[own_rec, here_dst] = rec_ref[:, here_src]

    pl.semaphore_wait(barrier, 7 + 3 + 2 + 2)

    def remote(src, dst, ssem, rsem, device):
        return pltpu.make_async_remote_copy(
            src_ref=src, dst_ref=dst, send_sem=ssem, recv_sem=rsem,
            device_id=device, device_id_type=MESH,
        )

    def same(ref, ssem, rsem, device):
        return remote(ref, ref, ssem, rsem, device)

    signal(z1.at[0], at_z(1))
    signal(z1.at[1], at_z(NZ - 1))

    def of_sensor(i):
        return lax.rem(y + NY - i, NY) * 2 + c

    st_y = [same(st.at[own_rec], st_s.at[i], st_r.at[i], at_y(i, c)) for i in range(1, NY)]
    st_own = same(st.at[own_rec], so_s, so_r, sibling)
    rec_copies = []
    for n, (i, k) in enumerate(peers):
        core = lax.rem(c + k, 2)
        src, dst = rec_window(lax.rem(y + i, NY) * 2 + core)
        rec_copies.append(
            remote(rec_ref.at[:, src], rec.at[own_rec, dst], rec_s.at[n], rec_r.at[n], at_y(i, core))
        )
    halo = [
        remote(rec_ref.at[:, 896:1024], rec.at[own_rec, 128:256], hal_s.at[0], hal_r.at[s], (0, next_tm)),
        remote(rec_ref.at[:, 0:128], rec.at[own_rec, 384:512], hal_s.at[1], hal_r.at[s], (7, prev_tm)),
    ]
    bias_copies = [
        remote(bias.at[c, 0], bias.at[c, i], b_s.at[n], b_r.at[n], at_y(i, lax.rem(c + k, 2)))
        for n, (i, k) in enumerate(peers)
    ]

    def colour(g):
        return lax.rem(x + 2 * z, 4) if g % 2 == 0 else lax.rem(2 * x + z, 4)

    def along(g):
        ways = ((at_x(1), at_x(NX - 1)), (at_z(1), at_z(NZ - 1)))
        return ways if g % 2 == 0 else ways[::-1]

    def piece(g, quarter, core, blocks, lanes=slice(0, 512)):
        if g < 3:
            return wc.at[g, :, quarter, core, blocks, :, lanes]
        return kvw.at[quarter, core, blocks, :, lanes]

    def y_copies(g):
        return [
            remote(
                piece(g, colour(g), c, 0), piece(g, colour(g), c, i),
                y_s.at[g, i], y_r.at[g, i], at_y(i, c),
            )
            for i in range(1, NY)
        ]

    def own_copy(g):
        own = wc.at[g, :, :, c, 0] if g < 3 else kvw.at[:, c, 0]
        return same(own, o_s.at[g], o_r.at[g], sibling)

    def issue(g):
        for copy in y_copies(g):
            copy.start()
        own_copy(g).start()

    others = slice(1, NY)

    def relays(g):
        (next_full, prev_full), (next_half, prev_half) = along(g)
        full = piece(g, colour(g), c, others)
        low_half = piece(g, colour(g), c, others, slice(0, 256))
        high_half = piece(g, colour(g), c, others, slice(256, 512))
        return [
            same(full, r_s.at[g, 0], r_r.at[g, 0], next_full),
            same(full, r_s.at[g, 1], r_r.at[g, 1], prev_full),
            same(low_half, r_s.at[g, 2], r_r.at[g, 2], next_half),
            same(high_half, r_s.at[g, 3], r_r.at[g, 3], prev_half),
        ]

    def to_sibling(g, k):
        quarter = lax.rem(colour(g) + k, 4)
        return same(piece(g, quarter, c, others), c_s.at[g, k], c_r.at[g, k], sibling)

    def forward_y(g):
        for copy in y_copies(g):
            copy.wait_recv()
        for copy in relays(g):
            copy.start()
        to_sibling(g, 0).start()

    def forward_relays(g):
        copies = relays(g)
        copies[0].wait_recv()
        to_sibling(g, 3).start()
        copies[1].wait_recv()
        to_sibling(g, 1).start()
        copies[2].wait_recv()
        copies[3].wait_recv()
        to_sibling(g, 2).start()

    def ready(g):
        own_copy(g).wait_recv()
        for k in range(4):
            to_sibling(g, k).wait_recv()

    def sent(g):
        for copy in y_copies(g) + relays(g):
            copy.wait_send()
        own_copy(g).wait_send()
        for k in range(4):
            to_sibling(g, k).wait_send()

    for copy in local:
        copy.wait()
    issue(0)
    for copy in st_y + [st_own] + halo + rec_copies + bias_copies:
        copy.start()
    issue(1)

    first = lax.broadcasted_iota(jnp.int32, (64, LATENTS), 0) == 0
    qa[64:128, :] = jnp.where(first, 1.0, 0.0).astype(BF16)
    va[64:80, :] = jnp.ones((16, 1024), BF16)
    frame = lax.broadcasted_iota(jnp.int32, (64, 1024), 1)
    row = lax.broadcasted_iota(jnp.int32, (64, 1024), 0)
    ka[64:128, :] = jnp.where((row == 0) & (frame >= valid_ref[0]), -1e30, 0.0).astype(BF16)

    def sib_st(i):
        return same(
            st.at[rows(32 * of_sensor(i), 32, 32)], sf_s.at[i], sf_r.at[i], sibling
        )

    forward_y(0)
    issue(2)
    for i in (1, 3, 2):
        st_y[i - 1].wait_recv()
        sib_st(i).start()
    for copy in rec_copies:
        copy.wait_recv()

    @pl.when((s == 0) | (s == 7))
    def _():
        for k in range(8):
            tile = rec.at[0:32, 0:128]
            pltpu.make_async_copy(tile, tile, hal_r.at[k]).wait()

    def turned(tiles, count, amount):
        lane = lax.broadcasted_iota(jnp.int32, tiles[0].shape, 1)
        keep = lane < 128 - amount
        turn = lax.rem(128 - amount, 128)
        rolled = [pltpu.roll(tile, turn, 1) for tile in tiles]
        last = len(tiles) - 1
        return [jnp.where(keep, rolled[k], rolled[min(k + 1, last)]) for k in range(count)]

    window = turned(
        [rec[:, 128 * k : 128 * k + 128].astype(F32) for k in range(1, 4)], 2, jnp.int32(64)
    )
    for k in range(2):
        rwin[:, 128 * k : 128 * k + 128] = window[k].astype(BF16)

    low = jnp.where((t == 0) & (s == 0), 0, -4096)
    high = jnp.where((t == 63) & (s == 7), 128, 4096)

    def inside(lanes, start):
        f = lax.broadcasted_iota(jnp.int32, (128, lanes), 1) + start
        return (f >= low) & (f < high)

    st_own.wait_recv()
    for i in range(1, NY):
        sib_st(i).wait_recv()
    sfull[...] = jnp.transpose(st[...].astype(F32)).astype(BF16)
    for n in range(0, 512, 128):
        part = dot(sfull[n : n + 128, :], rwin[...])
        h0[n : n + 128, :] = jnp.where(inside(256, -64), part, 0.0).astype(BF16)

    for copy in bias_copies:
        copy.wait_recv()
    order = [(core, i) for core in range(2) for i in range(NY)]
    place = [2 * lax.rem(y + NY - i, NY) + core for core, i in order]
    columns = [jnp.transpose(bias[core, i]) for core, i in order]

    def conv(layer, source, target, offset, tiles, start):
        d = dil_ref[layer]
        for q in range(4):
            if q == 2:
                forward_relays(layer + 1)
            w = wc[layer, :, q].reshape(384, 512)
            taps[...] = dot(w, source[...])
            here = [rows(64 * p + 16 * q, 16, 16) for p in place]
            old = jnp.concatenate([source[h, :] for h in here], axis=0).astype(F32)
            col = jnp.concatenate([v[16 * q : 16 * q + 16] for v in columns], axis=0)
            col = col[:, layer : layer + 1]
            a, b, e = [
                turned(
                    [taps[128 * j : 128 * j + 128, 128 * k : 128 * k + 128] for k in range(2)],
                    tiles, offset + (j - 1) * d,
                )
                for j in range(3)
            ]
            r = turned([old[:, 0:128], old[:, 128:256]], tiles, jnp.int32(offset))
            for k in range(tiles):
                pre = col + a[k] + b[k] + e[k]
                out = r[k] + 0.5 * pre * (1.0 + lax.erf(pre * 0.7071067811865476))
                out = jnp.where(inside(128, start + 128 * k), out, 0.0).astype(BF16)
                for n, h in enumerate(here):
                    target[h, 128 * k : 128 * k + 128] = out[16 * n : 16 * n + 16]

    forward_y(1)
    issue(3)
    pl.semaphore_wait(z1.at[0], 1)
    pl.semaphore_wait(z1.at[1], 1)
    signal(z2.at[0], at_z(2))
    signal(z2.at[1], at_z(NZ - 2))
    forward_y(2)
    forward_relays(0)
    forward_y(3)
    ready(0)
    conv(0, h0, h1, 16, 2, -48)
    pl.semaphore_wait(z2.at[0], 1)
    pl.semaphore_wait(z2.at[1], 1)
    signal(z4.at[0], at_z(4))
    signal(z4.at[1], at_z(NZ - 4))
    ready(1)
    conv(1, h1, h2, 16, 2, -32)
    ready(2)
    conv(2, h2, h3, 32, 1, 0)
    ready(3)

    own_lanes = rows(128 * s, 128, 128)
    for q in range(4):
        part = dot(kvw[q].reshape(256, 512), h3[...]).astype(BF16)
        for n, p in enumerate(place):
            kv[rows(128 * p + 32 * q, 32, 32), :] = part[32 * n : 32 * n + 32]
    kv_copies = []
    feature_copies = []
    for n, (i, k) in enumerate(peers):
        core = lax.rem(c + k, 2)
        to = lax.rem(y + i, NY) * 2 + core
        kv_copies.append(
            remote(kv.at[of_head(to)], kvall.at[:, own_lanes], kv_s.at[n], kv_r.at[n], at_y(i, core))
        )
        feature_copies.append(
            remote(
                h3.at[rows(64 * to, 64, 64)], feat_ref.at[:, own_lanes],
                f_s.at[n], f_r.at[n], at_y(i, core),
            )
        )
    for copy in kv_copies + feature_copies:
        copy.start()
    kvall[:, own_lanes] = kv[of_head(s), :]
    feat_ref[:, own_lanes] = h3[own_out, :]
    for copy in st_y + [st_own] + rec_copies + halo + bias_copies:
        copy.wait_send()
    for i in range(1, NY):
        sib_st(i).wait_send()
    for g in range(4):
        sent(g)
    for copy in kv_copies:
        copy.wait()
    ka[0:64, :] = (kvall[0:64, :].astype(F32) * 0.125).astype(BF16)
    va[0:64, :] = kvall[64:128, :]
    kt[...] = jnp.transpose(ka[...].astype(F32)).astype(BF16)

    def block_lanes(quarter, j):
        return pl.ds(pl.multiple_of(quarter * QUARTER + j * LB, LB), LB)

    def finish(scores, slot, j):
        peak = jnp.max(scores[...], axis=0, keepdims=True)
        probs = jnp.exp(scores[...] - peak).astype(BF16)
        both = dot(va[...], probs)
        total = both[64:65, :]
        here = slice(j * LB, j * LB + LB)
        xsend[slot, :, here] = (both[0:64, :] / total).astype(BF16)
        xlse_send[slot, :, here] = peak + jnp.log(total)

    def x_copies(i):
        device = at_x(i)
        return (
            pltpu.make_async_remote_copy(
                src_ref=xsend.at[i], dst_ref=xrecv.at[i], send_sem=xs.at[i], recv_sem=xr.at[i],
                device_id=device, device_id_type=MESH),
            pltpu.make_async_remote_copy(
                src_ref=xlse_send.at[i], dst_ref=xlse.at[i], send_sem=xls.at[i], recv_sem=xlr.at[i],
                device_id=device, device_id_type=MESH),
        )

    def attend(n, carry):
        quarter = lax.rem(x + n + 1, NX)
        slot = lax.rem(n + 1, NX)
        score1[...] = dot(kt[...], qa[:, block_lanes(quarter, 1)])
        finish(score0, slot, 0)
        score0[...] = dot(kt[...], qa[:, block_lanes(lax.rem(quarter + 1, NX), 0)])
        finish(score1, slot, 1)

        @pl.when(n < NX - 1)
        def _():
            for copy in x_copies(n + 1):
                copy.start()

        return carry

    score0[...] = dot(kt[...], qa[:, block_lanes(lax.rem(x + 1, NX), 0)])
    lax.fori_loop(0, NX, attend, 0)

    def merge(parts, lses):
        peak = lses[0]
        for v in lses[1:]:
            peak = jnp.maximum(peak, v)
        total = jnp.zeros_like(peak)
        out = None
        for part, v in zip(parts, lses):
            weight = jnp.exp(v - peak)
            total = total + weight
            term = part.astype(F32) * weight
            out = term if out is None else out + term
        return out / total, peak + jnp.log(total)

    for i in range(1, NX):
        for copy in x_copies(i):
            copy.wait()
    for b in range(4):
        lanes = slice(128 * b, 128 * b + 128)
        out, lse = merge(
            [xsend[0, :, lanes]] + [xrecv[i, :, lanes] for i in range(1, NX)],
            [xlse_send[0, :, lanes]] + [xlse[i, :, lanes] for i in range(1, NX)],
        )
        zsend[:, lanes] = out.astype(BF16)
        zlse_send[b] = lse

    pl.semaphore_wait(z4.at[0], 1)
    pl.semaphore_wait(z4.at[1], 1)

    def tile_of(zz):
        a, b = zz // 4, lax.rem(zz, 4)
        return pl.ds(pl.multiple_of(16 * a, 16), 16), pl.ds(pl.multiple_of(128 * b, 128), 128), b

    def z_copies(i):
        rows, lanes, b = tile_of(lax.rem(z + i, NZ))
        device = at_z(i)
        return (
            pltpu.make_async_remote_copy(
                src_ref=zsend.at[rows, lanes], dst_ref=zrecv.at[i], send_sem=zs.at[i],
                recv_sem=zr.at[i], device_id=device, device_id_type=MESH),
            pltpu.make_async_remote_copy(
                src_ref=zlse_send.at[b], dst_ref=zlse.at[i], send_sem=zls.at[i],
                recv_sem=zlr.at[i], device_id=device, device_id_type=MESH),
        )

    def far_first(n):
        k = (n + 1) // 2
        return 8 + k * (1 - 2 * lax.rem(n, 2))

    def near_first(n):
        return far_first(14 - n)

    def z_start(n, carry):
        for copy in z_copies(far_first(n)):
            copy.start()
        return carry

    def z_wait(n, carry):
        for copy in z_copies(near_first(n)):
            copy.wait()
        return carry

    lax.fori_loop(0, NZ - 1, z_start, 0)
    my_rows, my_lanes, my_b = tile_of(z)
    zrecv[0] = zsend[my_rows, my_lanes]
    zlse[0] = zlse_send[my_b]
    lax.fori_loop(0, NZ - 1, z_wait, 0)
    out, _ = merge([zrecv[i] for i in range(NZ)], [zlse[i] for i in range(NZ)])

    def out_tile(zz):
        rows, _, b = tile_of(zz)
        return rows, pl.ds(pl.multiple_of(512 * x + 128 * b, 128), 128)

    rows, lanes = out_tile(z)
    att_ref[rows, lanes] = out.astype(BF16)

    def a_copy(i, zz):
        tile = att_ref.at[out_tile(zz)]
        return pltpu.make_async_remote_copy(
            src_ref=tile, dst_ref=tile, send_sem=as_.at[i], recv_sem=ar.at[i],
            device_id=at_z(i), device_id_type=MESH)

    def spread(da):
        a = lax.rem(z // 4 + da + 4, 4)
        strip = att_ref.at[
            pl.ds(pl.multiple_of(16 * a, 16), 16), pl.ds(pl.multiple_of(512 * x, 512), 512)
        ]
        for i in range(1, NX):
            remote(strip, strip, bs.at[i], br.at[i], at_x(i)).start()

    def a_start(n, carry):
        a_copy(far_first(n), z).start()
        return carry

    def a_arrived(i, zz):
        a_copy(i, zz).wait_recv()

    def a_done(i, carry):
        a_copy(i, z).wait_send()
        return carry

    lax.fori_loop(0, NZ - 1, a_start, 0)
    for da in (0, 1, -1, 2):
        for b in range(4):
            zz = 4 * lax.rem(z // 4 + da + 4, 4) + b
            i = lax.rem(z - zz + NZ, NZ)
            if da == 0:
                pl.when(i != 0)(lambda: a_arrived(i, zz))
            else:
                a_arrived(i, zz)
        spread(da)
    for i in range(1, NX):
        quarter = att_ref.at[:, pl.ds(pl.multiple_of(512 * x, 512), 512)]
        whole = pltpu.make_async_remote_copy(
            src_ref=quarter, dst_ref=quarter, send_sem=bs.at[i], recv_sem=br.at[i],
            device_id=at_x(i), device_id_type=MESH)
        whole.wait_recv()
        whole.wait_send()
    lax.fori_loop(1, NZ, a_done, 0)
    for copy in feature_copies:
        copy.wait()


def on_device(recording, spatial_w, conv_w, conv_b, dilations, valid_frames, key_w, value_w, queries):
    vmem = pl.BlockSpec(memory_space=pltpu.VMEM)
    smem = pl.BlockSpec(memory_space=pltpu.SMEM)
    hbm = pl.BlockSpec(memory_space=pl.ANY)
    dma = pltpu.SemaphoreType.DMA
    regular = pltpu.SemaphoreType.REGULAR
    V = pltpu.VMEM
    return pl.pallas_call(
        kernel,
        out_shape=(
            jax.ShapeDtypeStruct((64, 1024), BF16),
            jax.ShapeDtypeStruct((64, LATENTS), BF16),
        ),
        in_specs=[smem, smem, vmem, vmem, hbm, vmem, hbm, hbm, hbm],
        out_specs=(vmem, vmem),
        scratch_shapes=[
            V((256, 512), BF16), V((512, 256), BF16), V((256, 640), BF16), V((256, 256), BF16),
            V((3, 3, 4, 2, 4, 16, 512), BF16), V((2, 4, 8, 128), F32), V((4, 2, 4, 32, 512), BF16),
            V((512, 256), BF16), V((512, 256), BF16), V((512, 256), BF16), V((512, 128), BF16),
            V((384, 256), F32), V((1024, 128), BF16), V((128, 1024), BF16),
            V((128, 1024), BF16), V((1024, 128), BF16), V((80, 1024), BF16), V((128, LATENTS), BF16),
            V((1024, LB), F32), V((1024, LB), F32),
            V((4, 64, 512), BF16), V((4, 1, 512), F32), V((4, 64, 512), BF16), V((4, 1, 512), F32),
            V((64, 512), BF16), V((4, 1, 128), F32), V((16, 16, 128), BF16), V((16, 1, 128), F32),
            dma((4,)), dma((7,)), dma((7,)), dma((2,)), dma((8,)), dma((7,)), dma((7,)),
            dma((4,)), dma((4,)), dma((4,)), dma((4,)), dma, dma,
            dma((4, 4)), dma((4, 4)), dma((4,)), dma((4,)),
            dma((4, 4)), dma((4, 4)), dma((4, 4)), dma((4, 4)),
            dma((7,)), dma((7,)), dma((7,)), dma((7,)),
            regular((2,)), regular((2,)), regular((2,)),
            dma((4,)), dma((4,)), dma((4,)), dma((4,)),
            dma((16,)), dma((16,)), dma((16,)), dma((16,)),
            dma((16,)), dma((16,)), dma((4,)), dma((4,)),
        ],
        compiler_params=pltpu.CompilerParams(
            collective_id=0, has_side_effects=True, vmem_limit_bytes=56 * 2**20
        ),
        name="encoder",
    )(
        dilations, valid_frames, recording, spatial_w.T, conv_w.reshape(3, 3, 4, 16, 512), conv_b,
        key_w.reshape(2, 32, 512), value_w.reshape(2, 32, 512), queries,
    )


def solution(mesh):
    return jax.shard_map(
        on_device,
        mesh=mesh,
        in_specs=(
            P("sensor", "tm"),
            P(None, "sensor"),
            P(None, None, "sensor", None),
            P(None, "sensor"),
            P(),
            P("tm"),
            P("sensor", None),
            P("sensor", None),
            P("sensor", None),
        ),
        out_specs=(P("sensor", "tm"), P("sensor", None)),
        check_vma=False,
    )
```

```python
import jax
import jax.numpy as jnp
from jax import lax
from jax.experimental import pallas as pl
from jax.experimental.pallas import tpu as pltpu
from jax.sharding import PartitionSpec as P

MESH = pl.DeviceIdType.MESH
BF16 = jnp.bfloat16
F32 = jnp.float32
NY, NX, NZ = 4, 4, 16
HD = 64
LATENTS = 2048
QUARTER = 512
LB = 256


def dot(a, b):
    return jnp.dot(a, b, preferred_element_type=F32)


def kernel(
    dil_ref, valid_ref, rec_ref, sw_ref, cw_ref, cb_ref, kw_ref, vw_ref, q_ref,
    feat_ref, att_ref,
    st, sfull, rec, rwin, wc, bias, kvw, h0, h1, h2, h3, taps, kv, kvall, ka, kt, va, qa,
    score0, score1, xsend, xlse_send, xrecv, xlse, zsend, zlse_send, zrecv, zlse,
    loc, rec_s, rec_r, hal_s, hal_r, b_s, b_r, st_s, st_r, sf_s, sf_r,
    y_s, y_r, r_s, r_r, c_s, c_r, f_s, f_r, kv_s, kv_r, z1, z2, z4,
    xs, xr, xls, xlr, zs, zr, zls, zlr, as_, ar, bs, br,
):
    s = lax.axis_index("sensor")
    t = lax.axis_index("tm")
    y, c = s // 2, lax.rem(s, 2)
    z, x = t // NX, lax.rem(t, NX)
    other = 1 - c
    parity = lax.rem(x, 2)

    def at_y(i, core):
        return (lax.rem(y + i, NY) * 2 + core, t)

    def at_x(i):
        return (s, z * NX + lax.rem(x + i, NX))

    def at_z(i):
        return (s, lax.rem(z + i, NZ) * NX + x)

    sibling = (y * 2 + other, t)
    prev_tm = lax.rem(t + 63, 64)
    next_tm = lax.rem(t + 1, 64)
    peers = [(i, k) for i in range(1, NY) for k in range(2)] + [(0, 1)]

    def signal(sem, device):
        pl.semaphore_signal(sem, inc=1, device_id=device, device_id_type=MESH)

    barrier = pltpu.get_barrier_semaphore()
    for i, k in peers:
        signal(barrier, at_y(i, lax.rem(c + k, 2)))
    for i in range(1, NX):
        signal(barrier, at_x(i))
    signal(barrier, at_z(1))
    signal(barrier, at_z(NZ - 1))

    @pl.when((s == 0) | (s == 7))
    def _():
        block = jnp.where(s == 0, prev_tm, next_tm)
        for k in range(8):
            signal(barrier, (k, block))

    def rows(start, size, align):
        return pl.ds(pl.multiple_of(start, align), size)

    def of_head(index):
        return rows(128 * index, 128, 128)

    own_rec = rows(32 * s, 32, 32)
    own_out = rows(64 * s, 64, 64)
    local = [
        pltpu.make_async_copy(cw_ref, wc.at[:, :, :, c, 0], loc.at[0]),
        pltpu.make_async_copy(kw_ref, kvw.at[0:2, c, 0], loc.at[1]),
        pltpu.make_async_copy(vw_ref, kvw.at[2:4, c, 0], loc.at[2]),
        pltpu.make_async_copy(q_ref, qa.at[0:64], loc.at[3]),
    ]
    for copy in local:
        copy.start()
    st[own_rec, :] = sw_ref[...]
    bias[NY * c] = jnp.zeros((8, 128), F32)
    bias[NY * c, 0:3, 0:64] = cb_ref[...]

    def rec_window(index):
        start = jnp.clip(index - 1, 0, 5)
        return rows(128 * start, 384, 128), rows(128 * (start - index + 2), 384, 128)

    here_src, here_dst = rec_window(s)
    rec[own_rec, here_dst] = rec_ref[:, here_src]

    pl.semaphore_wait(barrier, 7 + 3 + 2 + 2)

    def remote(src, dst, ssem, rsem, device):
        return pltpu.make_async_remote_copy(
            src_ref=src, dst_ref=dst, send_sem=ssem, recv_sem=rsem,
            device_id=device, device_id_type=MESH,
        )

    def same(ref, ssem, rsem, device):
        return remote(ref, ref, ssem, rsem, device)

    def drain(sem, ref):
        pltpu.make_async_copy(ref, ref, sem).wait()

    signal(z1, at_z(1))
    signal(z1, at_z(NZ - 1))

    def of_sensor(i):
        return lax.rem(y + NY - i, NY) * 2 + c

    st_y = [same(st.at[own_rec], st_s, st_r, at_y(i, c)) for i in range(1, NY)]
    st_own = same(st.at[own_rec], sf_s, sf_r, sibling)
    rec_copies = []
    for n, (i, k) in enumerate(peers):
        core = lax.rem(c + k, 2)
        src, dst = rec_window(lax.rem(y + i, NY) * 2 + core)
        rec_copies.append(
            remote(rec_ref.at[:, src], rec.at[own_rec, dst], rec_s, rec_r, at_y(i, core))
        )
    halo = [
        remote(rec_ref.at[:, 896:1024], rec.at[own_rec, 128:256], hal_s, hal_r, (0, next_tm)),
        remote(rec_ref.at[:, 0:128], rec.at[own_rec, 384:512], hal_s, hal_r, (7, prev_tm)),
    ]
    bias_copies = [
        remote(bias.at[NY * c], bias.at[NY * c + i], b_s, b_r, at_y(i, lax.rem(c + k, 2)))
        for n, (i, k) in enumerate(peers)
    ]

    def colour(g):
        return lax.rem(x + 2 * z, 4) if g % 2 == 0 else lax.rem(2 * x + z, 4)

    def along(g):
        ways = ((at_x(1), at_x(NX - 1)), (at_z(1), at_z(NZ - 1)))
        return ways if g % 2 == 0 else ways[::-1]

    def piece(g, quarter, core, blocks, lanes=slice(0, 512)):
        if g < 3:
            return wc.at[g, :, quarter, core, blocks, :, lanes]
        return kvw.at[quarter, core, blocks, :, lanes]

    def y_copies(g):
        return [
            remote(
                piece(g, colour(g), c, 0), piece(g, colour(g), c, i),
                y_s.at[g], y_r.at[g], at_y(i, c),
            )
            for i in range(1, NY)
        ]

    def own_copy(g):
        own = wc.at[g, :, :, c, 0] if g < 3 else kvw.at[:, c, 0]
        return same(own, c_s.at[g], c_r.at[g], sibling)

    def issue(g):
        for copy in y_copies(g):
            copy.start()
        own_copy(g).start()

    others = slice(1, NY)

    def relays(g):
        (next_full, prev_full), (next_half, prev_half) = along(g)
        full = piece(g, colour(g), c, others)
        low_half = piece(g, colour(g), c, others, slice(0, 256))
        high_half = piece(g, colour(g), c, others, slice(256, 512))
        return [
            same(full, r_s.at[g], r_r.at[g], next_full),
            same(full, r_s.at[g], r_r.at[g], prev_full),
            same(low_half, r_s.at[g], r_r.at[g], next_half),
            same(high_half, r_s.at[g], r_r.at[g], prev_half),
        ]

    def to_sibling(g, k):
        quarter = lax.rem(colour(g) + k, 4)
        return same(piece(g, quarter, c, others), c_s.at[g], c_r.at[g], sibling)

    def forward_y(g):
        drain(y_r.at[g], piece(g, 0, c, others))
        for copy in relays(g):
            copy.start()
        to_sibling(g, 0).start()

    def three_quarters(g):
        return wc.at[g, :, others, c, others] if g < 3 else kvw.at[others, c, others]

    def forward_relays(g):
        drain(r_r.at[g], three_quarters(g))
        for k in (3, 1, 2):
            to_sibling(g, k).start()

    def core_blocks(g, core):
        return wc.at[g, :, :, core] if g < 3 else kvw.at[:, core]

    def ready(g):
        drain(c_r.at[g], core_blocks(g, other))

    def sent(g):
        drain(y_s.at[g], piece(g, 0, c, others))
        drain(r_s.at[g], three_quarters(g))
        drain(c_s.at[g], core_blocks(g, c))

    for copy in local:
        copy.wait()
    issue(0)
    for copy in st_y + [st_own] + halo + rec_copies + bias_copies:
        copy.start()
    issue(1)

    first = lax.broadcasted_iota(jnp.int32, (64, LATENTS), 0) == 0
    qa[64:128, :] = jnp.where(first, 1.0, 0.0).astype(BF16)
    va[64:80, :] = jnp.ones((16, 1024), BF16)
    frame = lax.broadcasted_iota(jnp.int32, (64, 1024), 1)
    row = lax.broadcasted_iota(jnp.int32, (64, 1024), 0)
    ka[64:128, :] = jnp.where((row == 0) & (frame >= valid_ref[...]), -1e30, 0.0).astype(BF16)

    def sib_st(i):
        return same(
            st.at[rows(32 * of_sensor(i), 32, 32)], sf_s, sf_r, sibling
        )

    forward_y(0)
    issue(2)
    drain(st_r, st.at[0:96])
    for i in range(1, NY):
        sib_st(i).start()
    drain(rec_r, rec.at[0:224, 0:384])

    @pl.when((s == 0) | (s == 7))
    def _():
        drain(hal_r, rec.at[:, 0:128])

    def turned(tiles, count, amount):
        lane = lax.broadcasted_iota(jnp.int32, tiles[0].shape, 1)
        keep = lane < 128 - amount
        turn = lax.rem(128 - amount, 128)
        rolled = [pltpu.roll(tile, turn, 1) for tile in tiles]
        last = len(tiles) - 1
        return [jnp.where(keep, rolled[k], rolled[min(k + 1, last)]) for k in range(count)]

    window = turned(
        [rec[:, 128 * k : 128 * k + 128].astype(F32) for k in range(1, 4)], 2, jnp.int32(64)
    )
    for k in range(2):
        rwin[:, 128 * k : 128 * k + 128] = window[k].astype(BF16)

    low = jnp.where((t == 0) & (s == 0), 0, -4096)
    high = jnp.where((t == 63) & (s == 7), 128, 4096)

    def inside(lanes, start):
        f = lax.broadcasted_iota(jnp.int32, (128, lanes), 1) + start
        return (f >= low) & (f < high)

    drain(sf_r, st.at[0:128])
    sfull[...] = jnp.transpose(st[...].astype(F32)).astype(BF16)
    for n in range(0, 512, 128):
        part = dot(sfull[n : n + 128, :], rwin[...])
        h0[n : n + 128, :] = jnp.where(inside(256, -64), part, 0.0).astype(BF16)

    drain(b_r, bias.at[1:8])
    order = [(core, i) for core in range(2) for i in range(NY)]
    place = [2 * lax.rem(y + NY - i, NY) + core for core, i in order]
    columns = [jnp.transpose(bias[NY * core + i]) for core, i in order]

    def conv(layer, source, target, offset, tiles, start):
        d = dil_ref[0, layer]
        for q in range(4):
            if q == 2:
                forward_relays(layer + 1)
            w = wc[layer, :, q].reshape(384, 512)
            taps[...] = dot(w, source[...])
            here = [rows(64 * p + 16 * q, 16, 16) for p in place]
            old = jnp.concatenate([source[h, :] for h in here], axis=0).astype(F32)
            col = jnp.concatenate([v[16 * q : 16 * q + 16] for v in columns], axis=0)
            col = col[:, layer : layer + 1]
            a, b, e = [
                turned(
                    [taps[128 * j : 128 * j + 128, 128 * k : 128 * k + 128] for k in range(2)],
                    tiles, offset + (j - 1) * d,
                )
                for j in range(3)
            ]
            r = turned([old[:, 0:128], old[:, 128:256]], tiles, jnp.int32(offset))
            for k in range(tiles):
                pre = col + a[k] + b[k] + e[k]
                out = r[k] + 0.5 * pre * (1.0 + lax.erf(pre * 0.7071067811865476))
                out = jnp.where(inside(128, start + 128 * k), out, 0.0).astype(BF16)
                for n, h in enumerate(here):
                    target[h, 128 * k : 128 * k + 128] = out[16 * n : 16 * n + 16]

    forward_y(1)
    issue(3)
    pl.semaphore_wait(z1, 2)
    signal(z2, at_z(2))
    signal(z2, at_z(NZ - 2))
    forward_y(2)
    forward_relays(0)
    forward_y(3)
    ready(0)
    conv(0, h0, h1, 16, 2, -48)
    pl.semaphore_wait(z2, 2)
    signal(z4, at_z(4))
    signal(z4, at_z(NZ - 4))
    ready(1)
    conv(1, h1, h2, 16, 2, -32)
    ready(2)
    conv(2, h2, h3, 32, 1, 0)
    ready(3)

    own_lanes = rows(128 * s, 128, 128)
    for q in range(4):
        part = dot(kvw[q].reshape(256, 512), h3[...]).astype(BF16)
        for n, p in enumerate(place):
            kv[rows(128 * p + 32 * q, 32, 32), :] = part[32 * n : 32 * n + 32]
    kv_copies = []
    feature_copies = []
    for n, (i, k) in enumerate(peers):
        core = lax.rem(c + k, 2)
        to = lax.rem(y + i, NY) * 2 + core
        kv_copies.append(
            remote(kv.at[of_head(to)], kvall.at[:, own_lanes], kv_s, kv_r, at_y(i, core))
        )
        feature_copies.append(
            remote(
                h3.at[rows(64 * to, 64, 64)], feat_ref.at[:, own_lanes],
                f_s, f_r, at_y(i, core),
            )
        )
    for copy in kv_copies + feature_copies:
        copy.start()
    kvall[:, own_lanes] = kv[of_head(s), :]
    feat_ref[:, own_lanes] = h3[own_out, :]
    drain(st_s, st.at[0:96])
    drain(sf_s, st.at[0:128])
    drain(rec_s, rec.at[0:224, 0:384])
    drain(hal_s, rec.at[0:64, 0:128])
    drain(b_s, bias.at[1:8])
    for g in range(4):
        sent(g)
    drain(kv_r, kvall.at[:, 0:896])
    ka[0:64, :] = (kvall[0:64, :].astype(F32) * 0.125).astype(BF16)
    va[0:64, :] = kvall[64:128, :]
    kt[...] = jnp.transpose(ka[...].astype(F32)).astype(BF16)

    def block_lanes(quarter, j):
        return pl.ds(pl.multiple_of(quarter * QUARTER + j * LB, LB), LB)

    def finish(scores, slot, j):
        peak = jnp.max(scores[...], axis=0, keepdims=True)
        probs = jnp.exp(scores[...] - peak).astype(BF16)
        both = dot(va[...], probs)
        total = both[64:65, :]
        here = slice(j * LB, j * LB + LB)
        xsend[slot, :, here] = (both[0:64, :] / total).astype(BF16)
        xlse_send[slot, :, here] = peak + jnp.log(total)

    def x_copies(i):
        device = at_x(i)
        return (
            pltpu.make_async_remote_copy(
                src_ref=xsend.at[i], dst_ref=xrecv.at[i], send_sem=xs, recv_sem=xr,
                device_id=device, device_id_type=MESH),
            pltpu.make_async_remote_copy(
                src_ref=xlse_send.at[i], dst_ref=xlse.at[i], send_sem=xls, recv_sem=xlr,
                device_id=device, device_id_type=MESH),
        )

    def attend(n, carry):
        quarter = lax.rem(x + n + 1, NX)
        slot = lax.rem(n + 1, NX)
        score1[...] = dot(kt[...], qa[:, block_lanes(quarter, 1)])
        finish(score0, slot, 0)
        score0[...] = dot(kt[...], qa[:, block_lanes(lax.rem(quarter + 1, NX), 0)])
        finish(score1, slot, 1)

        @pl.when(n < NX - 1)
        def _():
            for copy in x_copies(n + 1):
                copy.start()

        return carry

    score0[...] = dot(kt[...], qa[:, block_lanes(lax.rem(x + 1, NX), 0)])
    lax.fori_loop(0, NX, attend, 0)

    def merge(parts, lses):
        peak = lses[0]
        for v in lses[1:]:
            peak = jnp.maximum(peak, v)
        total = jnp.zeros_like(peak)
        out = None
        for part, v in zip(parts, lses):
            weight = jnp.exp(v - peak)
            total = total + weight
            term = part.astype(F32) * weight
            out = term if out is None else out + term
        return out / total, peak + jnp.log(total)

    drain(xr, xrecv.at[1:4])
    drain(xlr, xlse.at[1:4])
    for b in range(4):
        lanes = slice(128 * b, 128 * b + 128)
        out, lse = merge(
            [xsend[0, :, lanes]] + [xrecv[i, :, lanes] for i in range(1, NX)],
            [xlse_send[0, :, lanes]] + [xlse[i, :, lanes] for i in range(1, NX)],
        )
        zsend[:, lanes] = out.astype(BF16)
        zlse_send[b] = lse

    pl.semaphore_wait(z4, 2)

    def tile_of(zz):
        a, b = zz // 4, lax.rem(zz, 4)
        return pl.ds(pl.multiple_of(16 * a, 16), 16), pl.ds(pl.multiple_of(128 * b, 128), 128), b

    def z_copies(i):
        rows, lanes, b = tile_of(lax.rem(z + i, NZ))
        device = at_z(i)
        return (
            pltpu.make_async_remote_copy(
                src_ref=zsend.at[rows, lanes], dst_ref=zrecv.at[i], send_sem=zs,
                recv_sem=zr, device_id=device, device_id_type=MESH),
            pltpu.make_async_remote_copy(
                src_ref=zlse_send.at[b], dst_ref=zlse.at[i], send_sem=zls,
                recv_sem=zlr, device_id=device, device_id_type=MESH),
        )

    def far_first(n):
        k = (n + 1) // 2
        return 8 + k * (1 - 2 * lax.rem(n, 2))

    def z_start(n, carry):
        for copy in z_copies(far_first(n)):
            copy.start()
        return carry

    lax.fori_loop(0, NZ - 1, z_start, 0)
    my_rows, my_lanes, my_b = tile_of(z)
    zrecv[0] = zsend[my_rows, my_lanes]
    zlse[0] = zlse_send[my_b]
    drain(zr, zrecv.at[1:16])
    drain(zlr, zlse.at[1:16])
    out, _ = merge([zrecv[i] for i in range(NZ)], [zlse[i] for i in range(NZ)])

    def out_tile(zz):
        rows, _, b = tile_of(zz)
        return rows, pl.ds(pl.multiple_of(512 * x + 128 * b, 128), 128)

    rows, lanes = out_tile(z)
    att_ref[rows, lanes] = out.astype(BF16)

    def a_copy(i, zz):
        tile = att_ref.at[out_tile(zz)]
        return pltpu.make_async_remote_copy(
            src_ref=tile, dst_ref=tile, send_sem=as_, recv_sem=ar.at[zz // 4],
            device_id=at_z(i), device_id_type=MESH)

    def spread(da):
        a = lax.rem(z // 4 + da + 4, 4)
        strip = att_ref.at[
            pl.ds(pl.multiple_of(16 * a, 16), 16), pl.ds(pl.multiple_of(512 * x, 512), 512)
        ]
        for i in range(1, NX):
            remote(strip, strip, bs, br, at_x(i)).start()

    def a_start(n, carry):
        a_copy(far_first(n), z).start()
        return carry

    lax.fori_loop(0, NZ - 1, a_start, 0)
    for da in (0, 1, -1, 2):
        strip = zsend.at[0:16, 0 : 384 if da == 0 else 512]
        drain(ar.at[lax.rem(z // 4 + da + 4, 4)], strip)
        spread(da)
    drain(br, xrecv.at[1:4])
    drain(bs, xrecv.at[1:4])
    drain(as_, zrecv.at[1:16])
    drain(zs, zrecv.at[1:16])
    drain(zls, zlse.at[1:16])
    drain(xs, xrecv.at[1:4])
    drain(xls, xlse.at[1:4])
    drain(kv_s, kvall.at[:, 0:896])
    drain(f_s, h3.at[0:448])
    drain(f_r, h3.at[0:448])


def hand_on(feat, att, feat_out, att_out, sem_f, sem_a):
    copies = [pltpu.make_async_copy(feat, feat_out, sem_f), pltpu.make_async_copy(att, att_out, sem_a)]
    for copy in copies:
        copy.start()
    for copy in copies:
        copy.wait()


def on_device(recording, spatial_w, conv_w, conv_b, dilations, valid_frames, key_w, value_w, queries):
    vmem = pl.BlockSpec(memory_space=pltpu.VMEM)
    hbm = pl.BlockSpec(memory_space=pl.ANY)
    dma = pltpu.SemaphoreType.DMA
    regular = pltpu.SemaphoreType.REGULAR
    V = pltpu.VMEM
    results = pl.pallas_call(
        kernel,
        out_shape=(
            jax.ShapeDtypeStruct((64, 1024), BF16),
            jax.ShapeDtypeStruct((64, LATENTS), BF16),
        ),
        in_specs=[vmem, vmem, vmem, vmem, hbm, vmem, hbm, hbm, hbm],
        out_specs=(vmem, vmem),
        scratch_shapes=[
            V((256, 512), BF16), V((512, 256), BF16), V((256, 640), BF16), V((256, 256), BF16),
            V((3, 3, 4, 2, 4, 16, 512), BF16), V((8, 8, 128), F32), V((4, 2, 4, 32, 512), BF16),
            V((512, 256), BF16), V((512, 256), BF16), V((512, 256), BF16), V((512, 128), BF16),
            V((384, 256), F32), V((1024, 128), BF16), V((128, 1024), BF16),
            V((128, 1024), BF16), V((1024, 128), BF16), V((80, 1024), BF16), V((128, LATENTS), BF16),
            V((1024, LB), F32), V((1024, LB), F32),
            V((4, 64, 512), BF16), V((4, 1, 512), F32), V((4, 64, 512), BF16), V((4, 1, 512), F32),
            V((64, 512), BF16), V((4, 1, 128), F32), V((16, 16, 128), BF16), V((16, 1, 128), F32),
            dma((4,)), dma, dma, dma, dma, dma, dma, dma, dma, dma, dma,
            dma((4,)), dma((4,)), dma((4,)), dma((4,)), dma((4,)), dma((4,)),
            dma, dma, dma, dma, regular, regular, regular,
            dma, dma, dma, dma, dma, dma, dma, dma, dma, dma((4,)), dma, dma,
        ],
        compiler_params=pltpu.CompilerParams(
            collective_id=0, has_side_effects=True, vmem_limit_bytes=56 * 2**20
        ),
        name="encoder",
    )(
        dilations.reshape(1, 3), valid_frames.reshape(1, 1), recording, spatial_w.T, conv_w.reshape(3, 3, 4, 16, 512), conv_b,
        key_w.reshape(2, 32, 512), value_w.reshape(2, 32, 512), queries,
    )
    return pl.pallas_call(
        hand_on,
        out_shape=tuple(jax.ShapeDtypeStruct(r.shape, r.dtype) for r in results),
        in_specs=[hbm, hbm],
        out_specs=(hbm, hbm),
        scratch_shapes=[dma, dma],
        name="hand_on",
    )(*results)


def solution(mesh):
    return jax.shard_map(
        on_device,
        mesh=mesh,
        in_specs=(
            P("sensor", "tm"),
            P(None, "sensor"),
            P(None, None, "sensor", None),
            P(None, "sensor"),
            P(),
            P("tm"),
            P("sensor", None),
            P("sensor", None),
            P("sensor", None),
        ),
        out_specs=(P("sensor", "tm"), P("sensor", None)),
        check_vma=False,
    )
```

```python
import jax
import jax.numpy as jnp
from jax import lax
from jax.experimental import pallas as pl
from jax.experimental.pallas import tpu as pltpu
from jax.sharding import PartitionSpec as P

MESH = pl.DeviceIdType.MESH
BF16 = jnp.bfloat16
F32 = jnp.float32
NY, NX, NZ = 4, 4, 16
HD = 64
LATENTS = 2048
QUARTER = 512
LB = 256


def dot(a, b):
    return jnp.dot(a, b, preferred_element_type=F32)


def kernel(
    dil_ref, valid_ref, rec_ref, sw_ref, cw_ref, cb_ref, kw_ref, vw_ref, q_ref,
    feat_ref, att_ref,
    st, sfull, rec, rwin, wc, bias, kvw, h0, h1, h2, h3, taps, kv, kvall, ka, kt, va, qa,
    score0, score1, xsend, xlse_send, xrecv, xlse, zsend, zlse_send, zrecv, zlse,
    loc, rec_s, rec_r, hal_s, hal_r, b_s, b_r, st_s, st_r, sf_s, sf_r,
    y_s, y_r, r_s, r_r, c_s, c_r, f_s, f_r, kv_s, kv_r, z1, z2, z4,
    xs, xr, xls, xlr, zs, zr, zls, zlr, as_, ar, bs, br,
):
    s = lax.axis_index("sensor")
    t = lax.axis_index("tm")
    y, c = s // 2, lax.rem(s, 2)
    z, x = t // NX, lax.rem(t, NX)
    other = 1 - c
    parity = lax.rem(x, 2)

    def at_y(i, core):
        return (lax.rem(y + i, NY) * 2 + core, t)

    def at_x(i):
        return (s, z * NX + lax.rem(x + i, NX))

    def at_z(i):
        return (s, lax.rem(z + i, NZ) * NX + x)

    sibling = (y * 2 + other, t)
    prev_tm = lax.rem(t + 63, 64)
    next_tm = lax.rem(t + 1, 64)
    peers = [(i, k) for i in range(1, NY) for k in range(2)] + [(0, 1)]

    def signal(sem, device):
        pl.semaphore_signal(sem, inc=1, device_id=device, device_id_type=MESH)

    barrier = pltpu.get_barrier_semaphore()
    for i, k in peers:
        signal(barrier, at_y(i, lax.rem(c + k, 2)))
    for i in range(1, NX):
        signal(barrier, at_x(i))
    signal(barrier, at_z(1))
    signal(barrier, at_z(NZ - 1))

    @pl.when((s == 0) | (s == 7))
    def _():
        block = jnp.where(s == 0, prev_tm, next_tm)
        for k in range(8):
            signal(barrier, (k, block))

    def rows(start, size, align):
        return pl.ds(pl.multiple_of(start, align), size)

    def of_head(index):
        return rows(128 * index, 128, 128)

    own_rec = rows(32 * s, 32, 32)
    own_out = rows(64 * s, 64, 64)
    local = [
        pltpu.make_async_copy(cw_ref, wc.at[:, :, :, c, 0], loc.at[0]),
        pltpu.make_async_copy(kw_ref, kvw.at[0:2, c, 0], loc.at[1]),
        pltpu.make_async_copy(vw_ref, kvw.at[2:4, c, 0], loc.at[2]),
        pltpu.make_async_copy(q_ref, qa.at[0:64], loc.at[3]),
    ]
    for copy in local:
        copy.start()
    st[own_rec, :] = sw_ref[...]
    bias[NY * c] = jnp.zeros((8, 128), F32)
    bias[NY * c, 0:3, 0:64] = cb_ref[...]

    def rec_window(index):
        start = jnp.clip(index - 1, 0, 5)
        return rows(128 * start, 384, 128), rows(128 * (start - index + 2), 384, 128)

    here_src, here_dst = rec_window(s)
    rec[own_rec, here_dst] = rec_ref[:, here_src]

    pl.semaphore_wait(barrier, 7 + 3 + 2 + 2)

    def remote(src, dst, ssem, rsem, device):
        return pltpu.make_async_remote_copy(
            src_ref=src, dst_ref=dst, send_sem=ssem, recv_sem=rsem,
            device_id=device, device_id_type=MESH,
        )

    def same(ref, ssem, rsem, device):
        return remote(ref, ref, ssem, rsem, device)

    def drain(sem, ref):
        pltpu.make_async_copy(ref, ref, sem).wait()

    signal(z1, at_z(1))
    signal(z1, at_z(NZ - 1))

    def of_sensor(i):
        return lax.rem(y + NY - i, NY) * 2 + c

    st_y = [same(st.at[own_rec], st_s, st_r, at_y(i, c)) for i in range(1, NY)]
    st_own = same(st.at[own_rec], sf_s, sf_r, sibling)
    rec_copies = []
    for n, (i, k) in enumerate(peers):
        core = lax.rem(c + k, 2)
        src, dst = rec_window(lax.rem(y + i, NY) * 2 + core)
        rec_copies.append(
            remote(rec_ref.at[:, src], rec.at[own_rec, dst], rec_s, rec_r, at_y(i, core))
        )
    halo = [
        remote(rec_ref.at[:, 896:1024], rec.at[own_rec, 128:256], hal_s, hal_r, (0, next_tm)),
        remote(rec_ref.at[:, 0:128], rec.at[own_rec, 384:512], hal_s, hal_r, (7, prev_tm)),
    ]
    bias_copies = [
        remote(bias.at[NY * c], bias.at[NY * c + i], b_s, b_r, at_y(i, lax.rem(c + k, 2)))
        for n, (i, k) in enumerate(peers)
    ]

    def colour(g):
        return lax.rem(x + 2 * z, 4) if g % 2 == 0 else lax.rem(2 * x + z, 4)

    def along(g):
        ways = ((at_x(1), at_x(NX - 1)), (at_z(1), at_z(NZ - 1)))
        return ways if g % 2 == 0 else ways[::-1]

    def piece(g, quarter, core, blocks, lanes=slice(0, 512)):
        if g < 3:
            return wc.at[g, :, quarter, core, blocks, :, lanes]
        return kvw.at[quarter, core, blocks, :, lanes]

    def y_copies(g):
        return [
            remote(
                piece(g, colour(g), c, 0), piece(g, colour(g), c, i),
                y_s.at[g], y_r.at[g], at_y(i, c),
            )
            for i in range(1, NY)
        ]

    def own_copy(g):
        own = wc.at[g, :, :, c, 0] if g < 3 else kvw.at[:, c, 0]
        return same(own, c_s.at[g], c_r.at[g], sibling)

    def issue(g):
        for copy in y_copies(g):
            copy.start()
        own_copy(g).start()

    others = slice(1, NY)

    def relays(g):
        (next_full, prev_full), (next_half, prev_half) = along(g)
        full = piece(g, colour(g), c, others)
        low_half = piece(g, colour(g), c, others, slice(0, 256))
        high_half = piece(g, colour(g), c, others, slice(256, 512))
        return [
            same(full, r_s.at[g], r_r.at[g], next_full),
            same(full, r_s.at[g], r_r.at[g], prev_full),
            same(low_half, r_s.at[g], r_r.at[g], next_half),
            same(high_half, r_s.at[g], r_r.at[g], prev_half),
        ]

    def to_sibling(g, k):
        quarter = lax.rem(colour(g) + k, 4)
        return same(piece(g, quarter, c, others), c_s.at[g], c_r.at[g], sibling)

    def forward_y(g):
        drain(y_r.at[g], piece(g, 0, c, others))
        for copy in relays(g):
            copy.start()
        to_sibling(g, 0).start()

    def three_quarters(g):
        return wc.at[g, :, others, c, others] if g < 3 else kvw.at[others, c, others]

    def forward_relays(g):
        drain(r_r.at[g], three_quarters(g))
        for k in (3, 1, 2):
            to_sibling(g, k).start()

    def core_blocks(g, core):
        return wc.at[g, :, :, core] if g < 3 else kvw.at[:, core]

    def ready(g):
        drain(c_r.at[g], core_blocks(g, other))

    def sent(g):
        drain(y_s.at[g], piece(g, 0, c, others))
        drain(r_s.at[g], three_quarters(g))
        drain(c_s.at[g], core_blocks(g, c))

    for copy in local:
        copy.wait()
    issue(0)
    for copy in st_y + [st_own] + halo + rec_copies + bias_copies:
        copy.start()
    issue(1)

    first = lax.broadcasted_iota(jnp.int32, (64, LATENTS), 0) == 0
    qa[64:128, :] = jnp.where(first, 1.0, 0.0).astype(BF16)
    va[64:80, :] = jnp.ones((16, 1024), BF16)
    frame = lax.broadcasted_iota(jnp.int32, (64, 1024), 1)
    row = lax.broadcasted_iota(jnp.int32, (64, 1024), 0)
    ka[64:128, :] = jnp.where((row == 0) & (frame >= valid_ref[...]), -1e30, 0.0).astype(BF16)

    def sib_st(i):
        return same(
            st.at[rows(32 * of_sensor(i), 32, 32)], sf_s, sf_r, sibling
        )

    forward_y(0)
    issue(2)
    drain(st_r, st.at[0:96])
    for i in range(1, NY):
        sib_st(i).start()
    drain(rec_r, rec.at[0:224, 0:384])

    @pl.when((s == 0) | (s == 7))
    def _():
        drain(hal_r, rec.at[:, 0:128])

    def turned(tiles, count, amount):
        lane = lax.broadcasted_iota(jnp.int32, tiles[0].shape, 1)
        keep = lane < 128 - amount
        turn = lax.rem(128 - amount, 128)
        rolled = [pltpu.roll(tile, turn, 1) for tile in tiles]
        last = len(tiles) - 1
        return [jnp.where(keep, rolled[k], rolled[min(k + 1, last)]) for k in range(count)]

    window = turned(
        [rec[:, 128 * k : 128 * k + 128].astype(F32) for k in range(1, 4)], 2, jnp.int32(64)
    )
    for k in range(2):
        rwin[:, 128 * k : 128 * k + 128] = window[k].astype(BF16)

    low = jnp.where((t == 0) & (s == 0), 0, -4096)
    high = jnp.where((t == 63) & (s == 7), 128, 4096)

    def inside(lanes, start):
        f = lax.broadcasted_iota(jnp.int32, (128, lanes), 1) + start
        return (f >= low) & (f < high)

    drain(sf_r, st.at[0:128])
    sfull[...] = jnp.transpose(st[...].astype(F32)).astype(BF16)
    for n in range(0, 512, 128):
        part = dot(sfull[n : n + 128, :], rwin[...])
        h0[n : n + 128, :] = jnp.where(inside(256, -64), part, 0.0).astype(BF16)

    drain(b_r, bias.at[1:8])
    order = [(core, i) for core in range(2) for i in range(NY)]
    place = [2 * lax.rem(y + NY - i, NY) + core for core, i in order]
    columns = [jnp.transpose(bias[NY * core + i]) for core, i in order]

    def conv(layer, source, target, offset, tiles, start):
        d = dil_ref[0, layer]
        for q in range(4):
            if q == 2:
                forward_relays(layer + 1)
            w = wc[layer, :, q].reshape(384, 512)
            taps[...] = dot(w, source[...])
            here = [rows(64 * p + 16 * q, 16, 16) for p in place]
            old = jnp.concatenate([source[h, :] for h in here], axis=0).astype(F32)
            col = jnp.concatenate([v[16 * q : 16 * q + 16] for v in columns], axis=0)
            col = col[:, layer : layer + 1]
            a, b, e = [
                turned(
                    [taps[128 * j : 128 * j + 128, 128 * k : 128 * k + 128] for k in range(2)],
                    tiles, offset + (j - 1) * d,
                )
                for j in range(3)
            ]
            r = turned([old[:, 0:128], old[:, 128:256]], tiles, jnp.int32(offset))
            for k in range(tiles):
                pre = col + a[k] + b[k] + e[k]
                out = r[k] + 0.5 * pre * (1.0 + lax.erf(pre * 0.7071067811865476))
                out = jnp.where(inside(128, start + 128 * k), out, 0.0).astype(BF16)
                for n, h in enumerate(here):
                    target[h, 128 * k : 128 * k + 128] = out[16 * n : 16 * n + 16]

    forward_y(1)
    issue(3)
    pl.semaphore_wait(z1, 2)
    signal(z2, at_z(2))
    signal(z2, at_z(NZ - 2))
    forward_y(2)
    forward_relays(0)
    forward_y(3)
    ready(0)
    conv(0, h0, h1, 16, 2, -48)
    pl.semaphore_wait(z2, 2)
    signal(z4, at_z(4))
    signal(z4, at_z(NZ - 4))
    ready(1)
    conv(1, h1, h2, 16, 2, -32)
    ready(2)
    conv(2, h2, h3, 32, 1, 0)
    ready(3)

    own_lanes = rows(128 * s, 128, 128)
    for q in range(4):
        part = dot(kvw[q].reshape(256, 512), h3[...]).astype(BF16)
        for n, p in enumerate(place):
            kv[rows(128 * p + 32 * q, 32, 32), :] = part[32 * n : 32 * n + 32]
    kv_copies = []
    feature_copies = []
    for n, (i, k) in enumerate(peers):
        core = lax.rem(c + k, 2)
        to = lax.rem(y + i, NY) * 2 + core
        kv_copies.append(
            remote(kv.at[of_head(to)], kvall.at[:, own_lanes], kv_s, kv_r, at_y(i, core))
        )
        feature_copies.append(
            remote(
                h3.at[rows(64 * to, 64, 64)], feat_ref.at[:, own_lanes],
                f_s, f_r, at_y(i, core),
            )
        )
    for copy in kv_copies:
        copy.start()
    kvall[:, own_lanes] = kv[of_head(s), :]
    feat_ref[:, own_lanes] = h3[own_out, :]
    drain(st_s, st.at[0:96])
    drain(sf_s, st.at[0:128])
    drain(rec_s, rec.at[0:224, 0:384])
    drain(hal_s, rec.at[0:64, 0:128])
    drain(b_s, bias.at[1:8])
    for g in range(4):
        sent(g)
    drain(kv_r, kvall.at[:, 0:896])
    for copy in feature_copies:
        copy.start()
    ka[0:64, :] = (kvall[0:64, :].astype(F32) * 0.125).astype(BF16)
    va[0:64, :] = kvall[64:128, :]
    kt[...] = jnp.transpose(ka[...].astype(F32)).astype(BF16)

    def block_lanes(quarter, j):
        return pl.ds(pl.multiple_of(quarter * QUARTER + j * LB, LB), LB)

    def finish(scores, slot, j):
        peak = jnp.max(scores[...], axis=0, keepdims=True)
        probs = jnp.exp(scores[...] - peak).astype(BF16)
        both = dot(va[...], probs)
        total = both[64:65, :]
        here = slice(j * LB, j * LB + LB)
        xsend[slot, :, here] = (both[0:64, :] / total).astype(BF16)
        xlse_send[slot, :, here] = peak + jnp.log(total)

    def x_copies(i):
        device = at_x(i)
        return (
            pltpu.make_async_remote_copy(
                src_ref=xsend.at[i], dst_ref=xrecv.at[i], send_sem=xs, recv_sem=xr,
                device_id=device, device_id_type=MESH),
            pltpu.make_async_remote_copy(
                src_ref=xlse_send.at[i], dst_ref=xlse.at[i], send_sem=xls, recv_sem=xlr,
                device_id=device, device_id_type=MESH),
        )

    def attend(n, carry):
        quarter = lax.rem(x + n + 1, NX)
        slot = lax.rem(n + 1, NX)
        score1[...] = dot(kt[...], qa[:, block_lanes(quarter, 1)])
        finish(score0, slot, 0)
        score0[...] = dot(kt[...], qa[:, block_lanes(lax.rem(quarter + 1, NX), 0)])
        finish(score1, slot, 1)

        @pl.when(n < NX - 1)
        def _():
            for copy in x_copies(n + 1):
                copy.start()

        return carry

    score0[...] = dot(kt[...], qa[:, block_lanes(lax.rem(x + 1, NX), 0)])
    lax.fori_loop(0, NX, attend, 0)

    def merge(parts, lses):
        peak = lses[0]
        for v in lses[1:]:
            peak = jnp.maximum(peak, v)
        total = jnp.zeros_like(peak)
        out = None
        for part, v in zip(parts, lses):
            weight = jnp.exp(v - peak)
            total = total + weight
            term = part.astype(F32) * weight
            out = term if out is None else out + term
        return out / total, peak + jnp.log(total)

    drain(xr, xrecv.at[1:4])
    drain(xlr, xlse.at[1:4])
    for b in range(4):
        lanes = slice(128 * b, 128 * b + 128)
        out, lse = merge(
            [xsend[0, :, lanes]] + [xrecv[i, :, lanes] for i in range(1, NX)],
            [xlse_send[0, :, lanes]] + [xlse[i, :, lanes] for i in range(1, NX)],
        )
        zsend[:, lanes] = out.astype(BF16)
        zlse_send[b] = lse

    pl.semaphore_wait(z4, 2)

    def tile_of(zz):
        a, b = zz // 4, lax.rem(zz, 4)
        return pl.ds(pl.multiple_of(16 * a, 16), 16), pl.ds(pl.multiple_of(128 * b, 128), 128), b

    def z_copies(i):
        rows, lanes, b = tile_of(lax.rem(z + i, NZ))
        device = at_z(i)
        return (
            pltpu.make_async_remote_copy(
                src_ref=zsend.at[rows, lanes], dst_ref=zrecv.at[i], send_sem=zs,
                recv_sem=zr, device_id=device, device_id_type=MESH),
            pltpu.make_async_remote_copy(
                src_ref=zlse_send.at[b], dst_ref=zlse.at[i], send_sem=zls,
                recv_sem=zlr, device_id=device, device_id_type=MESH),
        )

    def far_first(n):
        k = (n + 1) // 2
        return 8 + k * (1 - 2 * lax.rem(n, 2))

    def z_start(n, carry):
        for copy in z_copies(far_first(n)):
            copy.start()
        return carry

    lax.fori_loop(0, NZ - 1, z_start, 0)
    my_rows, my_lanes, my_b = tile_of(z)
    zrecv[0] = zsend[my_rows, my_lanes]
    zlse[0] = zlse_send[my_b]
    drain(zr, zrecv.at[1:16])
    drain(zlr, zlse.at[1:16])
    out, _ = merge([zrecv[i] for i in range(NZ)], [zlse[i] for i in range(NZ)])

    def out_tile(zz):
        rows, _, b = tile_of(zz)
        return rows, pl.ds(pl.multiple_of(512 * x + 128 * b, 128), 128)

    rows, lanes = out_tile(z)
    att_ref[rows, lanes] = out.astype(BF16)

    def a_copy(i, zz):
        tile = att_ref.at[out_tile(zz)]
        return pltpu.make_async_remote_copy(
            src_ref=tile, dst_ref=tile, send_sem=as_, recv_sem=ar.at[zz // 4],
            device_id=at_z(i), device_id_type=MESH)

    def spread(da):
        a = lax.rem(z // 4 + da + 4, 4)
        strip = att_ref.at[
            pl.ds(pl.multiple_of(16 * a, 16), 16), pl.ds(pl.multiple_of(512 * x, 512), 512)
        ]
        for i in range(1, NX):
            remote(strip, strip, bs, br, at_x(i)).start()

    def a_start(n, carry):
        a_copy(far_first(n), z).start()
        return carry

    lax.fori_loop(0, NZ - 1, a_start, 0)
    for da in (0, 1, -1, 2):
        strip = zsend.at[0:16, 0 : 384 if da == 0 else 512]
        drain(ar.at[lax.rem(z // 4 + da + 4, 4)], strip)
        spread(da)
    drain(br, xrecv.at[1:4])
    drain(bs, xrecv.at[1:4])
    drain(as_, zrecv.at[1:16])
    drain(zs, zrecv.at[1:16])
    drain(zls, zlse.at[1:16])
    drain(xs, xrecv.at[1:4])
    drain(xls, xlse.at[1:4])
    drain(kv_s, kvall.at[:, 0:896])
    drain(f_s, h3.at[0:448])
    drain(f_r, h3.at[0:448])


def hand_on(feat, att, feat_out, att_out):
    feat_out[...] = feat[...]
    att_out[...] = att[...]


def on_device(recording, spatial_w, conv_w, conv_b, dilations, valid_frames, key_w, value_w, queries):
    vmem = pl.BlockSpec(memory_space=pltpu.VMEM)
    hbm = pl.BlockSpec(memory_space=pl.ANY)
    dma = pltpu.SemaphoreType.DMA
    regular = pltpu.SemaphoreType.REGULAR
    V = pltpu.VMEM
    results = pl.pallas_call(
        kernel,
        out_shape=(
            jax.ShapeDtypeStruct((64, 1024), BF16),
            jax.ShapeDtypeStruct((64, LATENTS), BF16),
        ),
        in_specs=[vmem, vmem, vmem, vmem, hbm, vmem, hbm, hbm, hbm],
        out_specs=(vmem, vmem),
        scratch_shapes=[
            V((256, 512), BF16), V((512, 256), BF16), V((256, 640), BF16), V((256, 256), BF16),
            V((3, 3, 4, 2, 4, 16, 512), BF16), V((8, 8, 128), F32), V((4, 2, 4, 32, 512), BF16),
            V((512, 256), BF16), V((512, 256), BF16), V((512, 256), BF16), V((512, 128), BF16),
            V((384, 256), F32), V((1024, 128), BF16), V((128, 1024), BF16),
            V((128, 1024), BF16), V((1024, 128), BF16), V((80, 1024), BF16), V((128, LATENTS), BF16),
            V((1024, LB), F32), V((1024, LB), F32),
            V((4, 64, 512), BF16), V((4, 1, 512), F32), V((4, 64, 512), BF16), V((4, 1, 512), F32),
            V((64, 512), BF16), V((4, 1, 128), F32), V((16, 16, 128), BF16), V((16, 1, 128), F32),
            dma((4,)), dma, dma, dma, dma, dma, dma, dma, dma, dma, dma,
            dma((4,)), dma((4,)), dma((4,)), dma((4,)), dma((4,)), dma((4,)),
            dma, dma, dma, dma, regular, regular, regular,
            dma, dma, dma, dma, dma, dma, dma, dma, dma, dma((4,)), dma, dma,
        ],
        compiler_params=pltpu.CompilerParams(
            collective_id=0, has_side_effects=True, vmem_limit_bytes=56 * 2**20
        ),
        name="encoder",
    )(
        dilations.reshape(1, 3), valid_frames.reshape(1, 1), recording, spatial_w.T, conv_w.reshape(3, 3, 4, 16, 512), conv_b,
        key_w.reshape(2, 32, 512), value_w.reshape(2, 32, 512), queries,
    )
    return pl.pallas_call(
        hand_on,
        out_shape=tuple(jax.ShapeDtypeStruct(r.shape, r.dtype) for r in results),
        in_specs=[vmem, vmem],
        out_specs=(vmem, vmem),
        name="hand_on",
    )(*results)


def solution(mesh):
    return jax.shard_map(
        on_device,
        mesh=mesh,
        in_specs=(
            P("sensor", "tm"),
            P(None, "sensor"),
            P(None, None, "sensor", None),
            P(None, "sensor"),
            P(),
            P("tm"),
            P("sensor", None),
            P("sensor", None),
            P("sensor", None),
        ),
        out_specs=(P("sensor", "tm"), P("sensor", None)),
        check_vma=False,
    )
```

```python
import jax
import jax.numpy as jnp
from jax import lax
from jax.experimental import pallas as pl
from jax.experimental.pallas import tpu as pltpu
from jax.sharding import PartitionSpec as P

MESH = pl.DeviceIdType.MESH
BF16 = jnp.bfloat16
F32 = jnp.float32
NY, NX, NZ = 4, 4, 16
HD = 64
LATENTS = 2048
QUARTER = 512
LB = 256


def dot(a, b):
    return jnp.dot(a, b, preferred_element_type=F32)


def kernel(
    dil_ref, valid_ref, rec_ref, sw_ref, cw_ref, cb_ref, kw_ref, vw_ref, q_ref,
    feat_ref, att_ref,
    st, sfull, rec, rwin, wc, bias, kvw, h0, h1, h2, h3, taps, kv, kvall, ka, kt, va, qa,
    score0, score1, xsend, xlse_send, xrecv, xlse, zsend, zlse_send, zrecv, zlse,
    loc, rec_s, rec_r, hal_s, hal_r, b_s, b_r, st_s, st_r, sf_s, sf_r,
    y_s, y_r, r_s, r_r, c_s, c_r, f_s, f_r, kv_s, kv_r, z1, z2, z4,
    xs, xr, xls, xlr, zs, zr, zls, zlr, as_, ar, bs, br,
):
    s = lax.axis_index("sensor")
    t = lax.axis_index("tm")
    y, c = s // 2, lax.rem(s, 2)
    z, x = t // NX, lax.rem(t, NX)
    other = 1 - c
    parity = lax.rem(x, 2)

    def at_y(i, core):
        return (lax.rem(y + i, NY) * 2 + core, t)

    def at_x(i):
        return (s, z * NX + lax.rem(x + i, NX))

    def at_z(i):
        return (s, lax.rem(z + i, NZ) * NX + x)

    sibling = (y * 2 + other, t)
    prev_tm = lax.rem(t + 63, 64)
    next_tm = lax.rem(t + 1, 64)
    peers = [(i, k) for i in range(1, NY) for k in range(2)] + [(0, 1)]

    def signal(sem, device):
        pl.semaphore_signal(sem, inc=1, device_id=device, device_id_type=MESH)

    barrier = pltpu.get_barrier_semaphore()
    for i, k in peers:
        signal(barrier, at_y(i, lax.rem(c + k, 2)))
    for i in range(1, NX):
        signal(barrier, at_x(i))
    signal(barrier, at_z(1))
    signal(barrier, at_z(NZ - 1))

    @pl.when((s == 0) | (s == 7))
    def _():
        block = jnp.where(s == 0, prev_tm, next_tm)
        for k in range(8):
            signal(barrier, (k, block))

    def rows(start, size, align):
        return pl.ds(pl.multiple_of(start, align), size)

    def of_head(index):
        return rows(128 * index, 128, 128)

    own_rec = rows(32 * s, 32, 32)
    own_out = rows(64 * s, 64, 64)
    local = [
        pltpu.make_async_copy(cw_ref, wc.at[:, :, :, c, 0], loc.at[0]),
        pltpu.make_async_copy(kw_ref, kvw.at[0:2, c, 0], loc.at[1]),
        pltpu.make_async_copy(vw_ref, kvw.at[2:4, c, 0], loc.at[2]),
        pltpu.make_async_copy(q_ref, qa.at[0:64], loc.at[3]),
    ]
    for copy in local:
        copy.start()
    st[own_rec, :] = sw_ref[...]
    bias[NY * c] = jnp.zeros((8, 128), F32)
    bias[NY * c, 0:3, 0:64] = cb_ref[...]

    def rec_window(index):
        start = jnp.clip(index - 1, 0, 5)
        return rows(128 * start, 384, 128), rows(128 * (start - index + 2), 384, 128)

    here_src, here_dst = rec_window(s)
    rec[own_rec, here_dst] = rec_ref[:, here_src]

    pl.semaphore_wait(barrier, 7 + 3 + 2 + 2)

    def remote(src, dst, ssem, rsem, device):
        return pltpu.make_async_remote_copy(
            src_ref=src, dst_ref=dst, send_sem=ssem, recv_sem=rsem,
            device_id=device, device_id_type=MESH,
        )

    def same(ref, ssem, rsem, device):
        return remote(ref, ref, ssem, rsem, device)

    def drain(sem, ref):
        pltpu.make_async_copy(ref, ref, sem).wait()

    signal(z1, at_z(1))
    signal(z1, at_z(NZ - 1))

    def of_sensor(i):
        return lax.rem(y + NY - i, NY) * 2 + c

    st_y = [same(st.at[own_rec], st_s, st_r, at_y(i, c)) for i in range(1, NY)]
    st_own = same(st.at[own_rec], sf_s, sf_r, sibling)
    rec_copies = []
    for n, (i, k) in enumerate(peers):
        core = lax.rem(c + k, 2)
        src, dst = rec_window(lax.rem(y + i, NY) * 2 + core)
        rec_copies.append(
            remote(rec_ref.at[:, src], rec.at[own_rec, dst], rec_s, rec_r, at_y(i, core))
        )
    halo = [
        remote(rec_ref.at[:, 896:1024], rec.at[own_rec, 128:256], hal_s, hal_r, (0, next_tm)),
        remote(rec_ref.at[:, 0:128], rec.at[own_rec, 384:512], hal_s, hal_r, (7, prev_tm)),
    ]
    bias_copies = [
        remote(bias.at[NY * c], bias.at[NY * c + i], b_s, b_r, at_y(i, lax.rem(c + k, 2)))
        for n, (i, k) in enumerate(peers)
    ]

    def colour(g):
        return lax.rem(x + 2 * z, 4) if g % 2 == 0 else lax.rem(2 * x + z, 4)

    def along(g):
        ways = ((at_x(1), at_x(NX - 1)), (at_z(1), at_z(NZ - 1)))
        return ways if g % 2 == 0 else ways[::-1]

    def piece(g, quarter, core, blocks, lanes=slice(0, 512)):
        if g < 3:
            return wc.at[g, :, quarter, core, blocks, :, lanes]
        return kvw.at[quarter, core, blocks, :, lanes]

    def y_copies(g):
        return [
            remote(
                piece(g, colour(g), c, 0), piece(g, colour(g), c, i),
                y_s.at[g], y_r.at[g], at_y(i, c),
            )
            for i in range(1, NY)
        ]

    def own_copy(g):
        own = wc.at[g, :, :, c, 0] if g < 3 else kvw.at[:, c, 0]
        return same(own, c_s.at[g], c_r.at[g], sibling)

    def issue(g):
        for copy in y_copies(g):
            copy.start()
        own_copy(g).start()

    others = slice(1, NY)

    def relays(g):
        (next_full, prev_full), (next_half, prev_half) = along(g)
        full = piece(g, colour(g), c, others)
        low_half = piece(g, colour(g), c, others, slice(0, 256))
        high_half = piece(g, colour(g), c, others, slice(256, 512))
        return [
            same(full, r_s.at[g], r_r.at[g], next_full),
            same(full, r_s.at[g], r_r.at[g], prev_full),
            same(low_half, r_s.at[g], r_r.at[g], next_half),
            same(high_half, r_s.at[g], r_r.at[g], prev_half),
        ]

    def to_sibling(g, k):
        quarter = lax.rem(colour(g) + k, 4)
        return same(piece(g, quarter, c, others), c_s.at[g], c_r.at[g], sibling)

    def forward_y(g):
        drain(y_r.at[g], piece(g, 0, c, others))
        for copy in relays(g):
            copy.start()
        to_sibling(g, 0).start()

    def three_quarters(g):
        return wc.at[g, :, others, c, others] if g < 3 else kvw.at[others, c, others]

    def forward_relays(g):
        drain(r_r.at[g], three_quarters(g))
        for k in (3, 1, 2):
            to_sibling(g, k).start()

    def core_blocks(g, core):
        return wc.at[g, :, :, core] if g < 3 else kvw.at[:, core]

    def ready(g):
        drain(c_r.at[g], core_blocks(g, other))

    def sent(g):
        drain(y_s.at[g], piece(g, 0, c, others))
        drain(r_s.at[g], three_quarters(g))
        drain(c_s.at[g], core_blocks(g, c))

    for copy in local:
        copy.wait()
    for g in range(4):
        issue(g)
    for copy in st_y + [st_own] + halo + rec_copies + bias_copies:
        copy.start()

    first = lax.broadcasted_iota(jnp.int32, (64, LATENTS), 0) == 0
    qa[64:128, :] = jnp.where(first, 1.0, 0.0).astype(BF16)
    va[64:80, :] = jnp.ones((16, 1024), BF16)
    frame = lax.broadcasted_iota(jnp.int32, (64, 1024), 1)
    row = lax.broadcasted_iota(jnp.int32, (64, 1024), 0)
    ka[64:128, :] = jnp.where((row == 0) & (frame >= valid_ref[...]), -1e30, 0.0).astype(BF16)

    def sib_st(i):
        return same(
            st.at[rows(32 * of_sensor(i), 32, 32)], sf_s, sf_r, sibling
        )

    forward_y(0)
    forward_y(1)
    forward_y(2)
    forward_relays(0)
    forward_y(3)
    pl.semaphore_wait(z1, 2)
    signal(z2, at_z(2))
    signal(z2, at_z(NZ - 2))
    drain(st_r, st.at[0:96])
    for i in range(1, NY):
        sib_st(i).start()
    forward_relays(1)
    drain(rec_r, rec.at[0:224, 0:384])

    @pl.when((s == 0) | (s == 7))
    def _():
        drain(hal_r, rec.at[:, 0:128])

    def turned(tiles, count, amount):
        lane = lax.broadcasted_iota(jnp.int32, tiles[0].shape, 1)
        keep = lane < 128 - amount
        turn = lax.rem(128 - amount, 128)
        rolled = [pltpu.roll(tile, turn, 1) for tile in tiles]
        last = len(tiles) - 1
        return [jnp.where(keep, rolled[k], rolled[min(k + 1, last)]) for k in range(count)]

    window = turned(
        [rec[:, 128 * k : 128 * k + 128].astype(F32) for k in range(1, 4)], 2, jnp.int32(64)
    )
    for k in range(2):
        rwin[:, 128 * k : 128 * k + 128] = window[k].astype(BF16)

    low = jnp.where((t == 0) & (s == 0), 0, -4096)
    high = jnp.where((t == 63) & (s == 7), 128, 4096)

    def inside(lanes, start):
        f = lax.broadcasted_iota(jnp.int32, (128, lanes), 1) + start
        return (f >= low) & (f < high)

    drain(sf_r, st.at[0:128])
    sfull[...] = jnp.transpose(st[...].astype(F32)).astype(BF16)
    for n in range(0, 512, 128):
        part = dot(sfull[n : n + 128, :], rwin[...])
        h0[n : n + 128, :] = jnp.where(inside(256, -64), part, 0.0).astype(BF16)

    drain(b_r, bias.at[1:8])
    order = [(core, i) for core in range(2) for i in range(NY)]
    place = [2 * lax.rem(y + NY - i, NY) + core for core, i in order]
    columns = [jnp.transpose(bias[NY * core + i]) for core, i in order]

    def conv(layer, source, target, offset, tiles, start, forwarded=None):
        d = dil_ref[0, layer]
        for q in range(4):
            if q == 2 and forwarded is not None:
                forward_relays(forwarded)
            w = wc[layer, :, q].reshape(384, 512)
            taps[...] = dot(w, source[...])
            here = [rows(64 * p + 16 * q, 16, 16) for p in place]
            old = jnp.concatenate([source[h, :] for h in here], axis=0).astype(F32)
            col = jnp.concatenate([v[16 * q : 16 * q + 16] for v in columns], axis=0)
            col = col[:, layer : layer + 1]
            a, b, e = [
                turned(
                    [taps[128 * j : 128 * j + 128, 128 * k : 128 * k + 128] for k in range(2)],
                    tiles, offset + (j - 1) * d,
                )
                for j in range(3)
            ]
            r = turned([old[:, 0:128], old[:, 128:256]], tiles, jnp.int32(offset))
            for k in range(tiles):
                pre = col + a[k] + b[k] + e[k]
                out = r[k] + 0.5 * pre * (1.0 + lax.erf(pre * 0.7071067811865476))
                out = jnp.where(inside(128, start + 128 * k), out, 0.0).astype(BF16)
                for n, h in enumerate(here):
                    target[h, 128 * k : 128 * k + 128] = out[16 * n : 16 * n + 16]

    forward_relays(2)
    ready(0)
    conv(0, h0, h1, 16, 2, -48, 3)
    pl.semaphore_wait(z2, 2)
    signal(z4, at_z(4))
    signal(z4, at_z(NZ - 4))
    ready(1)
    conv(1, h1, h2, 16, 2, -32)
    ready(2)
    conv(2, h2, h3, 32, 1, 0)
    ready(3)

    own_lanes = rows(128 * s, 128, 128)
    for q in range(4):
        part = dot(kvw[q].reshape(256, 512), h3[...]).astype(BF16)
        for n, p in enumerate(place):
            kv[rows(128 * p + 32 * q, 32, 32), :] = part[32 * n : 32 * n + 32]
    kv_copies = []
    feature_copies = []
    for n, (i, k) in enumerate(peers):
        core = lax.rem(c + k, 2)
        to = lax.rem(y + i, NY) * 2 + core
        kv_copies.append(
            remote(kv.at[of_head(to)], kvall.at[:, own_lanes], kv_s, kv_r, at_y(i, core))
        )
        feature_copies.append(
            remote(
                h3.at[rows(64 * to, 64, 64)], feat_ref.at[:, own_lanes],
                f_s, f_r, at_y(i, core),
            )
        )
    for copy in kv_copies:
        copy.start()
    kvall[:, own_lanes] = kv[of_head(s), :]
    feat_ref[:, own_lanes] = h3[own_out, :]
    drain(st_s, st.at[0:96])
    drain(sf_s, st.at[0:128])
    drain(rec_s, rec.at[0:224, 0:384])
    drain(hal_s, rec.at[0:64, 0:128])
    drain(b_s, bias.at[1:8])
    for g in range(4):
        sent(g)
    drain(kv_r, kvall.at[:, 0:896])
    for copy in feature_copies:
        copy.start()
    ka[0:64, :] = (kvall[0:64, :].astype(F32) * 0.125).astype(BF16)
    va[0:64, :] = kvall[64:128, :]
    kt[...] = jnp.transpose(ka[...].astype(F32)).astype(BF16)

    def block_lanes(quarter, j):
        return pl.ds(pl.multiple_of(quarter * QUARTER + j * LB, LB), LB)

    def finish(scores, slot, j):
        peak = jnp.max(scores[...], axis=0, keepdims=True)
        probs = jnp.exp(scores[...] - peak).astype(BF16)
        both = dot(va[...], probs)
        total = both[64:65, :]
        here = slice(j * LB, j * LB + LB)
        xsend[slot, :, here] = (both[0:64, :] / total).astype(BF16)
        xlse_send[slot, :, here] = peak + jnp.log(total)

    def x_copies(i):
        device = at_x(i)
        return (
            pltpu.make_async_remote_copy(
                src_ref=xsend.at[i], dst_ref=xrecv.at[i], send_sem=xs, recv_sem=xr,
                device_id=device, device_id_type=MESH),
            pltpu.make_async_remote_copy(
                src_ref=xlse_send.at[i], dst_ref=xlse.at[i], send_sem=xls, recv_sem=xlr,
                device_id=device, device_id_type=MESH),
        )

    score0[...] = dot(kt[...], qa[:, block_lanes(lax.rem(x + 1, NX), 0)])
    for n in range(NX):
        slot = (n + 1) % NX
        quarter = lax.rem(x + n + 1, NX)
        score1[...] = dot(kt[...], qa[:, block_lanes(quarter, 1)])
        finish(score0, slot, 0)
        if n < NX - 1:
            score0[...] = dot(kt[...], qa[:, block_lanes(lax.rem(quarter + 1, NX), 0)])
        finish(score1, slot, 1)
        if n < NX - 1:
            for copy in x_copies(slot):
                copy.start()

    def merge(parts, lses):
        peak = lses[0]
        for v in lses[1:]:
            peak = jnp.maximum(peak, v)
        total = jnp.zeros_like(peak)
        out = None
        for part, v in zip(parts, lses):
            weight = jnp.exp(v - peak)
            total = total + weight
            term = part.astype(F32) * weight
            out = term if out is None else out + term
        return out / total, peak + jnp.log(total)

    drain(xr, xrecv.at[1:4])
    drain(xlr, xlse.at[1:4])
    for b in range(4):
        lanes = slice(128 * b, 128 * b + 128)
        out, lse = merge(
            [xsend[0, :, lanes]] + [xrecv[i, :, lanes] for i in range(1, NX)],
            [xlse_send[0, :, lanes]] + [xlse[i, :, lanes] for i in range(1, NX)],
        )
        zsend[:, lanes] = out.astype(BF16)
        zlse_send[b] = lse

    pl.semaphore_wait(z4, 2)

    def tile_of(zz):
        a, b = zz // 4, lax.rem(zz, 4)
        return pl.ds(pl.multiple_of(16 * a, 16), 16), pl.ds(pl.multiple_of(128 * b, 128), 128), b

    def z_copies(i):
        rows, lanes, b = tile_of(lax.rem(z + i, NZ))
        device = at_z(i)
        return (
            pltpu.make_async_remote_copy(
                src_ref=zsend.at[rows, lanes], dst_ref=zrecv.at[i], send_sem=zs,
                recv_sem=zr, device_id=device, device_id_type=MESH),
            pltpu.make_async_remote_copy(
                src_ref=zlse_send.at[b], dst_ref=zlse.at[i], send_sem=zls,
                recv_sem=zlr, device_id=device, device_id_type=MESH),
        )

    def far_first(n):
        k = (n + 1) // 2
        return 8 + k * (1 - 2 * lax.rem(n, 2))

    def z_start(n, carry):
        for copy in z_copies(far_first(n)):
            copy.start()
        return carry

    lax.fori_loop(0, NZ - 1, z_start, 0)
    my_rows, my_lanes, my_b = tile_of(z)
    zrecv[0] = zsend[my_rows, my_lanes]
    zlse[0] = zlse_send[my_b]
    drain(zr, zrecv.at[1:16])
    drain(zlr, zlse.at[1:16])
    out, _ = merge([zrecv[i] for i in range(NZ)], [zlse[i] for i in range(NZ)])

    def out_tile(zz):
        rows, _, b = tile_of(zz)
        return rows, pl.ds(pl.multiple_of(512 * x + 128 * b, 128), 128)

    rows, lanes = out_tile(z)
    att_ref[rows, lanes] = out.astype(BF16)

    def a_copy(i, zz):
        tile = att_ref.at[out_tile(zz)]
        return pltpu.make_async_remote_copy(
            src_ref=tile, dst_ref=tile, send_sem=as_, recv_sem=ar.at[zz // 4],
            device_id=at_z(i), device_id_type=MESH)

    def spread(da):
        a = lax.rem(z // 4 + da + 4, 4)
        strip = att_ref.at[
            pl.ds(pl.multiple_of(16 * a, 16), 16), pl.ds(pl.multiple_of(512 * x, 512), 512)
        ]
        for i in range(1, NX):
            remote(strip, strip, bs, br, at_x(i)).start()

    def a_start(n, carry):
        a_copy(far_first(n), z).start()
        return carry

    lax.fori_loop(0, NZ - 1, a_start, 0)
    for da in (0, 1, -1, 2):
        strip = zsend.at[0:16, 0 : 384 if da == 0 else 512]
        drain(ar.at[lax.rem(z // 4 + da + 4, 4)], strip)
        spread(da)
    drain(br, xrecv.at[1:4])
    drain(bs, xrecv.at[1:4])
    drain(as_, zrecv.at[1:16])
    drain(zs, zrecv.at[1:16])
    drain(zls, zlse.at[1:16])
    drain(xs, xrecv.at[1:4])
    drain(xls, xlse.at[1:4])
    drain(kv_s, kvall.at[:, 0:896])
    drain(f_s, h3.at[0:448])
    drain(f_r, h3.at[0:448])


def hand_on(feat, att, feat_out, att_out):
    feat_out[...] = feat[...]
    att_out[...] = att[...]


def on_device(recording, spatial_w, conv_w, conv_b, dilations, valid_frames, key_w, value_w, queries):
    vmem = pl.BlockSpec(memory_space=pltpu.VMEM)
    hbm = pl.BlockSpec(memory_space=pl.ANY)
    dma = pltpu.SemaphoreType.DMA
    regular = pltpu.SemaphoreType.REGULAR
    V = pltpu.VMEM
    results = pl.pallas_call(
        kernel,
        out_shape=(
            jax.ShapeDtypeStruct((64, 1024), BF16),
            jax.ShapeDtypeStruct((64, LATENTS), BF16),
        ),
        in_specs=[vmem, vmem, vmem, vmem, hbm, vmem, hbm, hbm, hbm],
        out_specs=(vmem, vmem),
        scratch_shapes=[
            V((256, 512), BF16), V((512, 256), BF16), V((256, 640), BF16), V((256, 256), BF16),
            V((3, 3, 4, 2, 4, 16, 512), BF16), V((8, 8, 128), F32), V((4, 2, 4, 32, 512), BF16),
            V((512, 256), BF16), V((512, 256), BF16), V((512, 256), BF16), V((512, 128), BF16),
            V((384, 256), F32), V((1024, 128), BF16), V((128, 1024), BF16),
            V((128, 1024), BF16), V((1024, 128), BF16), V((80, 1024), BF16), V((128, LATENTS), BF16),
            V((1024, LB), F32), V((1024, LB), F32),
            V((4, 64, 512), BF16), V((4, 1, 512), F32), V((4, 64, 512), BF16), V((4, 1, 512), F32),
            V((64, 512), BF16), V((4, 1, 128), F32), V((16, 16, 128), BF16), V((16, 1, 128), F32),
            dma((4,)), dma, dma, dma, dma, dma, dma, dma, dma, dma, dma,
            dma((4,)), dma((4,)), dma((4,)), dma((4,)), dma((4,)), dma((4,)),
            dma, dma, dma, dma, regular, regular, regular,
            dma, dma, dma, dma, dma, dma, dma, dma, dma, dma((4,)), dma, dma,
        ],
        compiler_params=pltpu.CompilerParams(
            collective_id=0, has_side_effects=True, vmem_limit_bytes=56 * 2**20
        ),
        name="encoder",
    )(
        dilations.reshape(1, 3), valid_frames.reshape(1, 1), recording, spatial_w.T, conv_w.reshape(3, 3, 4, 16, 512), conv_b,
        key_w.reshape(2, 32, 512), value_w.reshape(2, 32, 512), queries,
    )
    return pl.pallas_call(
        hand_on,
        out_shape=tuple(jax.ShapeDtypeStruct(r.shape, r.dtype) for r in results),
        in_specs=[vmem, vmem],
        out_specs=(vmem, vmem),
        name="hand_on",
    )(*results)


def solution(mesh):
    return jax.shard_map(
        on_device,
        mesh=mesh,
        in_specs=(
            P("sensor", "tm"),
            P(None, "sensor"),
            P(None, None, "sensor", None),
            P(None, "sensor"),
            P(),
            P("tm"),
            P("sensor", None),
            P("sensor", None),
            P("sensor", None),
        ),
        out_specs=(P("sensor", "tm"), P("sensor", None)),
        check_vma=False,
    )
```

```python
import jax
import jax.numpy as jnp
from jax import lax
from jax.experimental import pallas as pl
from jax.experimental.pallas import tpu as pltpu
from jax.sharding import PartitionSpec as P

MESH = pl.DeviceIdType.MESH
BF16 = jnp.bfloat16
F32 = jnp.float32
NY, NX, NZ = 4, 4, 16
HD = 64
LATENTS = 2048
QUARTER = 512
LB = 256


def dot(a, b):
    return jnp.dot(a, b, preferred_element_type=F32)


def kernel(
    dil_ref, valid_ref, rec_ref, sw_ref, cw_ref, cb_ref, kw_ref, vw_ref, q_ref,
    feat_ref, att_ref,
    st, sfull, rec, rwin, wc, bias, kvw, h0, h1, h2, h3, taps, kv, kvall, ka, kt, va, qa,
    score0, score1, xsend, xlse_send, xrecv, xlse, zsend, zlse_send, zrecv, zlse,
    loc, rec_s, rec_r, hal_s, hal_r, b_s, b_r,
    y_s, y_r, r_s, r_r, c_s, c_r, f_s, f_r, kv_s, kv_r, z1, z2, z4,
    xs, xr, xls, xlr, zs, zr, zls, zlr, as_, ar, bs, br,
):
    s = lax.axis_index("sensor")
    t = lax.axis_index("tm")
    y, c = s // 2, lax.rem(s, 2)
    z, x = t // NX, lax.rem(t, NX)
    other = 1 - c
    parity = lax.rem(x, 2)

    def at_y(i, core):
        return (lax.rem(y + i, NY) * 2 + core, t)

    def at_x(i):
        return (s, z * NX + lax.rem(x + i, NX))

    def at_z(i):
        return (s, lax.rem(z + i, NZ) * NX + x)

    sibling = (y * 2 + other, t)
    prev_tm = lax.rem(t + 63, 64)
    next_tm = lax.rem(t + 1, 64)
    peers = [(i, k) for i in range(1, NY) for k in range(2)] + [(0, 1)]

    def signal(sem, device):
        pl.semaphore_signal(sem, inc=1, device_id=device, device_id_type=MESH)

    barrier = pltpu.get_barrier_semaphore()
    for i, k in peers:
        signal(barrier, at_y(i, lax.rem(c + k, 2)))
    for i in range(1, NX):
        signal(barrier, at_x(i))
    signal(barrier, at_z(1))
    signal(barrier, at_z(NZ - 1))

    @pl.when((s == 0) | (s == 7))
    def _():
        block = jnp.where(s == 0, prev_tm, next_tm)
        for k in range(8):
            signal(barrier, (k, block))

    def rows(start, size, align):
        return pl.ds(pl.multiple_of(start, align), size)

    def of_head(index):
        return rows(128 * index, 128, 128)

    own_out = rows(64 * s, 64, 64)
    local = [
        pltpu.make_async_copy(cw_ref, wc.at[:, :, :, c, 0], loc.at[0]),
        pltpu.make_async_copy(kw_ref, kvw.at[0:2, c, 0], loc.at[1]),
        pltpu.make_async_copy(vw_ref, kvw.at[2:4, c, 0], loc.at[2]),
        pltpu.make_async_copy(q_ref, qa.at[0:64], loc.at[3]),
    ]
    for copy in local:
        copy.start()
    st[NY * c] = sw_ref[...]
    bias[NY * c] = jnp.zeros((8, 128), F32)
    bias[NY * c, 0:3, 0:64] = cb_ref[...]

    def rec_window(index):
        start = jnp.clip(index - 1, 0, 5)
        return rows(128 * start, 384, 128), rows(128 * (start - index + 2), 384, 128)

    here_src, here_dst = rec_window(s)
    rec[NY * c, :, here_dst] = rec_ref[:, here_src]

    pl.semaphore_wait(barrier, 7 + 3 + 2 + 2)

    def remote(src, dst, ssem, rsem, device):
        return pltpu.make_async_remote_copy(
            src_ref=src, dst_ref=dst, send_sem=ssem, recv_sem=rsem,
            device_id=device, device_id_type=MESH,
        )

    def same(ref, ssem, rsem, device):
        return remote(ref, ref, ssem, rsem, device)

    def drain(sem, ref):
        pltpu.make_async_copy(ref, ref, sem).wait()

    signal(z1, at_z(1))
    signal(z1, at_z(NZ - 1))

    rec_copies = []
    for n, (i, k) in enumerate(peers):
        core = lax.rem(c + k, 2)
        src, dst = rec_window(lax.rem(y + i, NY) * 2 + core)
        rec_copies.append(
            remote(rec_ref.at[:, src], rec.at[NY * c + i, :, dst], rec_s, rec_r, at_y(i, core))
        )
    halo = [
        remote(rec_ref.at[:, 896:1024], rec.at[NY * c + lax.rem(NY - y, NY), :, 128:256], hal_s, hal_r, (0, next_tm)),
        remote(rec_ref.at[:, 0:128], rec.at[NY * c + NY - 1 - y, :, 384:512], hal_s, hal_r, (7, prev_tm)),
    ]
    bias_copies = [
        remote(bias.at[NY * c], bias.at[NY * c + i], b_s, b_r, at_y(i, lax.rem(c + k, 2)))
        for n, (i, k) in enumerate(peers)
    ]

    others = slice(1, NY)

    def colour(g):
        return lax.rem(x + 2 * z, 4) if g % 2 == 0 else lax.rem(2 * x + z, 4)

    def along(g):
        ways = ((at_x(1), at_x(NX - 1)), (at_z(1), at_z(NZ - 1)))
        return ways if g % 2 == 0 else ways[::-1]

    def piece(g, quarter, core, blocks, half=None):
        if g == 4:
            if blocks == others:
                blocks = pl.ds(NY * core + 1, NY - 1)
            else:
                blocks = NY * core + blocks
            part = slice(0, 32) if half is None else slice(16 * half, 16 * half + 16)
            return st.at[blocks, part, rows(128 * quarter, 128, 128)]
        lanes = slice(0, 512) if half is None else slice(256 * half, 256 * half + 256)
        if g == 3:
            return kvw.at[quarter, core, blocks, :, lanes]
        return wc.at[g, :, quarter, core, blocks, :, lanes]

    def y_copies(g):
        return [
            remote(
                piece(g, colour(g), c, 0), piece(g, colour(g), c, i),
                y_s.at[g], y_r.at[g], at_y(i, c),
            )
            for i in range(1, NY)
        ]

    def own_copy(g):
        own = st.at[NY * c] if g == 4 else kvw.at[:, c, 0] if g == 3 else wc.at[g, :, :, c, 0]
        return same(own, c_s.at[g], c_r.at[g], sibling)

    def issue(g):
        for copy in y_copies(g):
            copy.start()
        own_copy(g).start()

    def relays(g):
        (next_full, prev_full), (next_half, prev_half) = along(g)
        full = piece(g, colour(g), c, others)
        low_half = piece(g, colour(g), c, others, 0)
        high_half = piece(g, colour(g), c, others, 1)
        return [
            same(full, r_s.at[g], r_r.at[g], next_full),
            same(full, r_s.at[g], r_r.at[g], prev_full),
            same(low_half, r_s.at[g], r_r.at[g], next_half),
            same(high_half, r_s.at[g], r_r.at[g], prev_half),
        ]

    def to_sibling(g, k):
        quarter = lax.rem(colour(g) + k, 4)
        return same(piece(g, quarter, c, others), c_s.at[g], c_r.at[g], sibling)

    def forward_y(g):
        drain(y_r.at[g], piece(g, 0, c, others))
        for copy in relays(g):
            copy.start()
        to_sibling(g, 0).start()

    def three_quarters(g):
        if g == 4:
            return st.at[0:3, :, 0:384]
        return kvw.at[others, c, others] if g == 3 else wc.at[g, :, others, c, others]

    def forward_relays(g):
        drain(r_r.at[g], three_quarters(g))
        for k in (3, 1, 2):
            to_sibling(g, k).start()

    def core_blocks(g, core):
        if g == 4:
            return st.at[0:4]
        return kvw.at[:, core] if g == 3 else wc.at[g, :, :, core]

    def ready(g):
        drain(c_r.at[g], core_blocks(g, other))

    def sent(g):
        drain(y_s.at[g], piece(g, 0, c, others))
        drain(r_s.at[g], three_quarters(g))
        drain(c_s.at[g], core_blocks(g, c))

    for copy in local:
        copy.wait()
    for g in (4, 0, 1, 2, 3):
        issue(g)
    for copy in halo + rec_copies + bias_copies:
        copy.start()

    first = lax.broadcasted_iota(jnp.int32, (64, LATENTS), 0) == 0
    qa[64:128, :] = jnp.where(first, 1.0, 0.0).astype(BF16)
    va[64:80, :] = jnp.ones((16, 1024), BF16)
    frame = lax.broadcasted_iota(jnp.int32, (64, 1024), 1)
    row = lax.broadcasted_iota(jnp.int32, (64, 1024), 0)
    ka[64:128, :] = jnp.where((row == 0) & (frame >= valid_ref[...]), -1e30, 0.0).astype(BF16)

    forward_y(4)
    forward_y(0)
    forward_y(1)
    forward_relays(4)
    forward_y(2)
    forward_relays(0)
    forward_y(3)
    pl.semaphore_wait(z1, 2)
    signal(z2, at_z(2))
    signal(z2, at_z(NZ - 2))
    forward_relays(1)
    drain(rec_r, rec.at[0:7, :, 0:384])

    @pl.when((s == 0) | (s == 7))
    def _():
        drain(hal_r, rec.at[:, :, 0:128])

    def turned(tiles, count, amount):
        lane = lax.broadcasted_iota(jnp.int32, tiles[0].shape, 1)
        keep = lane < 128 - amount
        turn = lax.rem(128 - amount, 128)
        rolled = [pltpu.roll(tile, turn, 1) for tile in tiles]
        last = len(tiles) - 1
        return [jnp.where(keep, rolled[k], rolled[min(k + 1, last)]) for k in range(count)]

    window = turned(
        [rec[:, :, 128 * k : 128 * k + 128].reshape(256, 128).astype(F32) for k in range(1, 4)], 2, jnp.int32(64)
    )
    for k in range(2):
        rwin[:, 128 * k : 128 * k + 128] = window[k].astype(BF16)

    low = jnp.where((t == 0) & (s == 0), 0, -4096)
    high = jnp.where((t == 63) & (s == 7), 128, 4096)

    def inside(lanes, start):
        f = lax.broadcasted_iota(jnp.int32, (128, lanes), 1) + start
        return (f >= low) & (f < high)

    ready(4)
    sfull[...] = jnp.transpose(st[...].reshape(256, 512).astype(F32)).astype(BF16)
    for n in range(0, 512, 128):
        part = dot(sfull[n : n + 128, :], rwin[...])
        h0[n : n + 128, :] = jnp.where(inside(256, -64), part, 0.0).astype(BF16)

    drain(b_r, bias.at[1:8])
    order = [(core, i) for core in range(2) for i in range(NY)]
    place = [2 * lax.rem(y + NY - i, NY) + core for core, i in order]
    columns = [jnp.transpose(bias[NY * core + i]) for core, i in order]

    def conv(layer, source, target, offset, tiles, start, forwarded=None):
        d = dil_ref[0, layer]
        for q in range(4):
            if q == 2 and forwarded is not None:
                forward_relays(forwarded)
            w = wc[layer, :, q].reshape(384, 512)
            tap = taps.at[q % 2]
            tap[...] = dot(w, source[...])
            here = [rows(64 * p + 16 * q, 16, 16) for p in place]
            old = jnp.concatenate([source[h, :] for h in here], axis=0).astype(F32)
            col = jnp.concatenate([v[16 * q : 16 * q + 16] for v in columns], axis=0)
            col = col[:, layer : layer + 1]
            a, b, e = [
                turned(
                    [tap[128 * j : 128 * j + 128, 128 * k : 128 * k + 128] for k in range(2)],
                    tiles, offset + (j - 1) * d,
                )
                for j in range(3)
            ]
            r = turned([old[:, 0:128], old[:, 128:256]], tiles, jnp.int32(offset))
            for k in range(tiles):
                pre = col + a[k] + b[k] + e[k]
                out = r[k] + 0.5 * pre * (1.0 + lax.erf(pre * 0.7071067811865476))
                out = jnp.where(inside(128, start + 128 * k), out, 0.0).astype(BF16)
                for n, h in enumerate(here):
                    target[h, 128 * k : 128 * k + 128] = out[16 * n : 16 * n + 16]

    forward_relays(2)
    ready(0)
    conv(0, h0, h1, 16, 2, -48, 3)
    pl.semaphore_wait(z2, 2)
    signal(z4, at_z(4))
    signal(z4, at_z(NZ - 4))
    ready(1)
    conv(1, h1, h2, 16, 2, -32)
    ready(2)
    conv(2, h2, h3, 32, 1, 0)
    ready(3)

    own_lanes = rows(128 * s, 128, 128)
    for q in range(4):
        part = dot(kvw[q].reshape(256, 512), h3[...]).astype(BF16)
        for n, p in enumerate(place):
            kv[rows(128 * p + 32 * q, 32, 32), :] = part[32 * n : 32 * n + 32]
    kv_copies = []
    feature_copies = []
    for n, (i, k) in enumerate(peers):
        core = lax.rem(c + k, 2)
        to = lax.rem(y + i, NY) * 2 + core
        kv_copies.append(
            remote(kv.at[of_head(to)], kvall.at[:, own_lanes], kv_s, kv_r, at_y(i, core))
        )
        feature_copies.append(
            remote(
                h3.at[rows(64 * to, 64, 64)], feat_ref.at[:, own_lanes],
                f_s, f_r, at_y(i, core),
            )
        )
    for copy in kv_copies:
        copy.start()
    kvall[:, own_lanes] = kv[of_head(s), :]
    feat_ref[:, own_lanes] = h3[own_out, :]
    drain(rec_s, rec.at[0:7, :, 0:384])
    drain(hal_s, rec.at[0:2, :, 0:128])
    drain(b_s, bias.at[1:8])
    for g in range(5):
        sent(g)
    drain(kv_r, kvall.at[:, 0:896])
    for copy in feature_copies:
        copy.start()
    ka[0:64, :] = (kvall[0:64, :].astype(F32) * 0.125).astype(BF16)
    va[0:64, :] = kvall[64:128, :]
    kt[...] = jnp.transpose(ka[...].astype(F32)).astype(BF16)

    def block_lanes(quarter, j):
        return pl.ds(pl.multiple_of(quarter * QUARTER + j * LB, LB), LB)

    def finish(scores, slot, j):
        peak = jnp.max(scores[...], axis=0, keepdims=True)
        probs = jnp.exp(scores[...] - peak).astype(BF16)
        both = dot(va[...], probs)
        total = both[64:65, :]
        here = slice(j * LB, j * LB + LB)
        xsend[slot, :, here] = (both[0:64, :] / total).astype(BF16)
        xlse_send[slot, :, here] = peak + jnp.log(total)

    def x_copies(i):
        device = at_x(i)
        return (
            pltpu.make_async_remote_copy(
                src_ref=xsend.at[i], dst_ref=xrecv.at[i], send_sem=xs, recv_sem=xr,
                device_id=device, device_id_type=MESH),
            pltpu.make_async_remote_copy(
                src_ref=xlse_send.at[i], dst_ref=xlse.at[i], send_sem=xls, recv_sem=xlr,
                device_id=device, device_id_type=MESH),
        )

    score0[...] = dot(kt[...], qa[:, block_lanes(lax.rem(x + 1, NX), 0)])
    for n in range(NX):
        slot = (n + 1) % NX
        quarter = lax.rem(x + n + 1, NX)
        score1[...] = dot(kt[...], qa[:, block_lanes(quarter, 1)])
        finish(score0, slot, 0)
        if n < NX - 1:
            score0[...] = dot(kt[...], qa[:, block_lanes(lax.rem(quarter + 1, NX), 0)])
        finish(score1, slot, 1)
        if n < NX - 1:
            for copy in x_copies(slot):
                copy.start()

    def merge(parts, lses):
        peak = lses[0]
        for v in lses[1:]:
            peak = jnp.maximum(peak, v)
        total = jnp.zeros_like(peak)
        out = None
        for part, v in zip(parts, lses):
            weight = jnp.exp(v - peak)
            total = total + weight
            term = part.astype(F32) * weight
            out = term if out is None else out + term
        return out / total, peak + jnp.log(total)

    drain(xr, xrecv.at[1:4])
    drain(xlr, xlse.at[1:4])
    for b in range(4):
        lanes = slice(128 * b, 128 * b + 128)
        out, lse = merge(
            [xsend[0, :, lanes]] + [xrecv[i, :, lanes] for i in range(1, NX)],
            [xlse_send[0, :, lanes]] + [xlse[i, :, lanes] for i in range(1, NX)],
        )
        zsend[:, lanes] = out.astype(BF16)
        zlse_send[b] = lse

    pl.semaphore_wait(z4, 2)

    def tile_of(zz):
        a, b = zz // 4, lax.rem(zz, 4)
        return pl.ds(pl.multiple_of(16 * a, 16), 16), pl.ds(pl.multiple_of(128 * b, 128), 128), b

    def z_copies(i):
        rows, lanes, b = tile_of(lax.rem(z + i, NZ))
        device = at_z(i)
        return (
            pltpu.make_async_remote_copy(
                src_ref=zsend.at[rows, lanes], dst_ref=zrecv.at[i], send_sem=zs,
                recv_sem=zr, device_id=device, device_id_type=MESH),
            pltpu.make_async_remote_copy(
                src_ref=zlse_send.at[b], dst_ref=zlse.at[i], send_sem=zls,
                recv_sem=zlr, device_id=device, device_id_type=MESH),
        )

    def far_first(n):
        k = (n + 1) // 2
        return 8 + k * (1 - 2 * lax.rem(n, 2))

    def z_start(n, carry):
        for copy in z_copies(far_first(n)):
            copy.start()
        return carry

    lax.fori_loop(0, NZ - 1, z_start, 0)
    my_rows, my_lanes, my_b = tile_of(z)
    zrecv[0] = zsend[my_rows, my_lanes]
    zlse[0] = zlse_send[my_b]
    drain(zr, zrecv.at[1:16])
    drain(zlr, zlse.at[1:16])
    out, _ = merge([zrecv[i] for i in range(NZ)], [zlse[i] for i in range(NZ)])

    def out_tile(zz):
        rows, _, b = tile_of(zz)
        return rows, pl.ds(pl.multiple_of(512 * x + 128 * b, 128), 128)

    rows, lanes = out_tile(z)
    att_ref[rows, lanes] = out.astype(BF16)

    def a_copy(i, zz):
        tile = att_ref.at[out_tile(zz)]
        return pltpu.make_async_remote_copy(
            src_ref=tile, dst_ref=tile, send_sem=as_, recv_sem=ar.at[zz // 4],
            device_id=at_z(i), device_id_type=MESH)

    def spread(da):
        a = lax.rem(z // 4 + da + 4, 4)
        strip = att_ref.at[
            pl.ds(pl.multiple_of(16 * a, 16), 16), pl.ds(pl.multiple_of(512 * x, 512), 512)
        ]
        for i in range(1, NX):
            remote(strip, strip, bs, br, at_x(i)).start()

    def a_start(n, carry):
        a_copy(far_first(n), z).start()
        return carry

    lax.fori_loop(0, NZ - 1, a_start, 0)
    for da in (0, 1, -1, 2):
        strip = zsend.at[0:16, 0 : 384 if da == 0 else 512]
        drain(ar.at[lax.rem(z // 4 + da + 4, 4)], strip)
        spread(da)
    drain(br, xrecv.at[1:4])
    drain(bs, xrecv.at[1:4])
    drain(as_, zrecv.at[1:16])
    drain(zs, zrecv.at[1:16])
    drain(zls, zlse.at[1:16])
    drain(xs, xrecv.at[1:4])
    drain(xls, xlse.at[1:4])
    drain(kv_s, kvall.at[:, 0:896])
    drain(f_s, h3.at[0:448])
    drain(f_r, h3.at[0:448])


def hand_on(feat, att, feat_out, att_out):
    feat_out[...] = feat[...]
    att_out[...] = att[...]


def on_device(recording, spatial_w, conv_w, conv_b, dilations, valid_frames, key_w, value_w, queries):
    vmem = pl.BlockSpec(memory_space=pltpu.VMEM)
    hbm = pl.BlockSpec(memory_space=pl.ANY)
    dma = pltpu.SemaphoreType.DMA
    regular = pltpu.SemaphoreType.REGULAR
    V = pltpu.VMEM
    results = pl.pallas_call(
        kernel,
        out_shape=(
            jax.ShapeDtypeStruct((64, 1024), BF16),
            jax.ShapeDtypeStruct((64, LATENTS), BF16),
        ),
        in_specs=[vmem, vmem, vmem, vmem, hbm, vmem, hbm, hbm, hbm],
        out_specs=(vmem, vmem),
        scratch_shapes=[
            V((8, 32, 512), BF16), V((512, 256), BF16), V((8, 32, 640), BF16), V((256, 256), BF16),
            V((3, 3, 4, 2, 4, 16, 512), BF16), V((8, 8, 128), F32), V((4, 2, 4, 32, 512), BF16),
            V((512, 256), BF16), V((512, 256), BF16), V((512, 256), BF16), V((512, 128), BF16),
            V((2, 384, 256), F32), V((1024, 128), BF16), V((128, 1024), BF16),
            V((128, 1024), BF16), V((1024, 128), BF16), V((80, 1024), BF16), V((128, LATENTS), BF16),
            V((1024, LB), F32), V((1024, LB), F32),
            V((4, 64, 512), BF16), V((4, 1, 512), F32), V((4, 64, 512), BF16), V((4, 1, 512), F32),
            V((64, 512), BF16), V((4, 1, 128), F32), V((16, 16, 128), BF16), V((16, 1, 128), F32),
            dma((4,)), dma, dma, dma, dma, dma, dma,
            dma((5,)), dma((5,)), dma((5,)), dma((5,)), dma((5,)), dma((5,)),
            dma, dma, dma, dma, regular, regular, regular,
            dma, dma, dma, dma, dma, dma, dma, dma, dma, dma((4,)), dma, dma,
        ],
        compiler_params=pltpu.CompilerParams(
            collective_id=0, has_side_effects=True, vmem_limit_bytes=56 * 2**20
        ),
        name="encoder",
    )(
        dilations.reshape(1, 3), valid_frames.reshape(1, 1), recording, spatial_w.T, conv_w.reshape(3, 3, 4, 16, 512), conv_b,
        key_w.reshape(2, 32, 512), value_w.reshape(2, 32, 512), queries,
    )
    return pl.pallas_call(
        hand_on,
        out_shape=tuple(jax.ShapeDtypeStruct(r.shape, r.dtype) for r in results),
        in_specs=[vmem, vmem],
        out_specs=(vmem, vmem),
        name="hand_on",
    )(*results)


def solution(mesh):
    return jax.shard_map(
        on_device,
        mesh=mesh,
        in_specs=(
            P("sensor", "tm"),
            P(None, "sensor"),
            P(None, None, "sensor", None),
            P(None, "sensor"),
            P(),
            P("tm"),
            P("sensor", None),
            P("sensor", None),
            P("sensor", None),
        ),
        out_specs=(P("sensor", "tm"), P("sensor", None)),
        check_vma=False,
    )
```

```python
import jax
import jax.numpy as jnp
from jax import lax
from jax.experimental import pallas as pl
from jax.experimental.pallas import tpu as pltpu
from jax.sharding import PartitionSpec as P

MESH = pl.DeviceIdType.MESH
BF16 = jnp.bfloat16
F32 = jnp.float32
NY, NX, NZ = 4, 4, 16
HD = 64
LATENTS = 2048
QUARTER = 512
LB = 256


def dot(a, b):
    return jnp.dot(a, b, preferred_element_type=F32)


def kernel(
    dil_ref, valid_ref, rec_ref, sw_ref, cw_ref, cb_ref, kw_ref, vw_ref, q_ref,
    feat_ref, att_ref,
    st, sfull, rec, rwin, wc, bias, kvw, h0, h1, h2, h3, taps, kv, kvall, ka, kt, va, qa,
    score0, score1, xsend, xlse_send, xrecv, xlse, zsend, zlse_send, zrecv, zlse,
    loc, rec_s, rec_r, hal_s, hal_r, b_s, b_r, st_s, st_r, sf_s, sf_r,
    y_s, y_r, r_s, r_r, c_s, c_r, f_s, f_r, kv_s, kv_r, z1, z2, z4,
    xs, xr, xls, xlr, zs, zr, zls, zlr, as_, ar, bs, br,
):
    s = lax.axis_index("sensor")
    t = lax.axis_index("tm")
    y, c = s // 2, lax.rem(s, 2)
    z, x = t // NX, lax.rem(t, NX)
    other = 1 - c
    parity = lax.rem(x, 2)

    def at_y(i, core):
        return (lax.rem(y + i, NY) * 2 + core, t)

    def at_x(i):
        return (s, z * NX + lax.rem(x + i, NX))

    def at_z(i):
        return (s, lax.rem(z + i, NZ) * NX + x)

    sibling = (y * 2 + other, t)
    prev_tm = lax.rem(t + 63, 64)
    next_tm = lax.rem(t + 1, 64)
    peers = [(i, k) for i in range(1, NY) for k in range(2)] + [(0, 1)]

    def signal(sem, device):
        pl.semaphore_signal(sem, inc=1, device_id=device, device_id_type=MESH)

    barrier = pltpu.get_barrier_semaphore()
    for i, k in peers:
        signal(barrier, at_y(i, lax.rem(c + k, 2)))
    for i in range(1, NX):
        signal(barrier, at_x(i))
    signal(barrier, at_z(1))
    signal(barrier, at_z(NZ - 1))

    @pl.when((s == 0) | (s == 7))
    def _():
        block = jnp.where(s == 0, prev_tm, next_tm)
        for k in range(8):
            signal(barrier, (k, block))

    def rows(start, size, align):
        return pl.ds(pl.multiple_of(start, align), size)

    def of_head(index):
        return rows(128 * index, 128, 128)

    own_rec = rows(32 * s, 32, 32)
    own_out = rows(64 * s, 64, 64)
    local = [
        pltpu.make_async_copy(cw_ref, wc.at[:, :, :, c, 0], loc.at[0]),
        pltpu.make_async_copy(kw_ref, kvw.at[0:2, c, 0], loc.at[1]),
        pltpu.make_async_copy(vw_ref, kvw.at[2:4, c, 0], loc.at[2]),
        pltpu.make_async_copy(q_ref, qa.at[0:64], loc.at[3]),
    ]
    for copy in local:
        copy.start()
    st[own_rec, :] = sw_ref[...]
    bias[NY * c] = jnp.zeros((8, 128), F32)
    bias[NY * c, 0:3, 0:64] = cb_ref[...]

    def rec_window(index):
        start = jnp.clip(index - 1, 0, 5)
        return rows(128 * start, 384, 128), rows(128 * (start - index + 2), 384, 128)

    here_src, here_dst = rec_window(s)
    rec[own_rec, here_dst] = rec_ref[:, here_src]

    pl.semaphore_wait(barrier, 7 + 3 + 2 + 2)

    def remote(src, dst, ssem, rsem, device):
        return pltpu.make_async_remote_copy(
            src_ref=src, dst_ref=dst, send_sem=ssem, recv_sem=rsem,
            device_id=device, device_id_type=MESH,
        )

    def same(ref, ssem, rsem, device):
        return remote(ref, ref, ssem, rsem, device)

    def drain(sem, ref):
        pltpu.make_async_copy(ref, ref, sem).wait()

    signal(z1, at_z(1))
    signal(z1, at_z(NZ - 1))

    def of_sensor(i):
        return lax.rem(y + NY - i, NY) * 2 + c

    st_y = [same(st.at[own_rec], st_s, st_r, at_y(i, c)) for i in range(1, NY)]
    st_own = same(st.at[own_rec], sf_s, sf_r, sibling)
    rec_copies = []
    for n, (i, k) in enumerate(peers):
        core = lax.rem(c + k, 2)
        src, dst = rec_window(lax.rem(y + i, NY) * 2 + core)
        rec_copies.append(
            remote(rec_ref.at[:, src], rec.at[own_rec, dst], rec_s, rec_r, at_y(i, core))
        )
    halo = [
        remote(rec_ref.at[:, 896:1024], rec.at[own_rec, 128:256], hal_s, hal_r, (0, next_tm)),
        remote(rec_ref.at[:, 0:128], rec.at[own_rec, 384:512], hal_s, hal_r, (7, prev_tm)),
    ]
    bias_copies = [
        remote(bias.at[NY * c], bias.at[NY * c + i], b_s, b_r, at_y(i, lax.rem(c + k, 2)))
        for n, (i, k) in enumerate(peers)
    ]

    def colour(g):
        return lax.rem(x + 2 * z, 4) if g % 2 == 0 else lax.rem(2 * x + z, 4)

    def along(g):
        ways = ((at_x(1), at_x(NX - 1)), (at_z(1), at_z(NZ - 1)))
        return ways if g % 2 == 0 else ways[::-1]

    def piece(g, quarter, core, blocks, lanes=slice(0, 512)):
        if g < 3:
            return wc.at[g, :, quarter, core, blocks, :, lanes]
        return kvw.at[quarter, core, blocks, :, lanes]

    def y_copies(g):
        return [
            remote(
                piece(g, colour(g), c, 0), piece(g, colour(g), c, i),
                y_s.at[g], y_r.at[g], at_y(i, c),
            )
            for i in range(1, NY)
        ]

    def own_copy(g):
        own = wc.at[g, :, :, c, 0] if g < 3 else kvw.at[:, c, 0]
        return same(own, c_s.at[g], c_r.at[g], sibling)

    def issue(g):
        for copy in y_copies(g):
            copy.start()
        own_copy(g).start()

    others = slice(1, NY)

    def relays(g):
        (next_full, prev_full), (next_half, prev_half) = along(g)
        full = piece(g, colour(g), c, others)
        low_half = piece(g, colour(g), c, others, slice(0, 256))
        high_half = piece(g, colour(g), c, others, slice(256, 512))
        return [
            same(full, r_s.at[g], r_r.at[g], next_full),
            same(full, r_s.at[g], r_r.at[g], prev_full),
            same(low_half, r_s.at[g], r_r.at[g], next_half),
            same(high_half, r_s.at[g], r_r.at[g], prev_half),
        ]

    def to_sibling(g, k):
        quarter = lax.rem(colour(g) + k, 4)
        return same(piece(g, quarter, c, others), c_s.at[g], c_r.at[g], sibling)

    def forward_y(g):
        drain(y_r.at[g], piece(g, 0, c, others))
        for copy in relays(g):
            copy.start()
        to_sibling(g, 0).start()

    def three_quarters(g):
        return wc.at[g, :, others, c, others] if g < 3 else kvw.at[others, c, others]

    def forward_relays(g):
        drain(r_r.at[g], three_quarters(g))
        for k in (3, 1, 2):
            to_sibling(g, k).start()

    def core_blocks(g, core):
        return wc.at[g, :, :, core] if g < 3 else kvw.at[:, core]

    def ready(g):
        drain(c_r.at[g], core_blocks(g, other))

    def sent(g):
        drain(y_s.at[g], piece(g, 0, c, others))
        drain(r_s.at[g], three_quarters(g))
        drain(c_s.at[g], core_blocks(g, c))

    for copy in local:
        copy.wait()
    for g in range(4):
        issue(g)
    for copy in st_y + [st_own] + halo + rec_copies + bias_copies:
        copy.start()

    first = lax.broadcasted_iota(jnp.int32, (64, LATENTS), 0) == 0
    qa[64:128, :] = jnp.where(first, 1.0, 0.0).astype(BF16)
    va[64:80, :] = jnp.ones((16, 1024), BF16)
    frame = lax.broadcasted_iota(jnp.int32, (64, 1024), 1)
    row = lax.broadcasted_iota(jnp.int32, (64, 1024), 0)
    ka[64:128, :] = jnp.where((row == 0) & (frame >= valid_ref[...]), -1e30, 0.0).astype(BF16)

    def sib_st(i):
        return same(
            st.at[rows(32 * of_sensor(i), 32, 32)], sf_s, sf_r, sibling
        )

    forward_y(0)
    forward_y(1)
    forward_y(2)
    forward_relays(0)
    forward_y(3)
    pl.semaphore_wait(z1, 2)
    signal(z2, at_z(2))
    signal(z2, at_z(NZ - 2))
    drain(st_r, st.at[0:96])
    for i in range(1, NY):
        sib_st(i).start()
    forward_relays(1)
    drain(rec_r, rec.at[0:224, 0:384])

    @pl.when((s == 0) | (s == 7))
    def _():
        drain(hal_r, rec.at[:, 0:128])

    def turned(tiles, count, amount):
        lane = lax.broadcasted_iota(jnp.int32, tiles[0].shape, 1)
        keep = lane < 128 - amount
        turn = lax.rem(128 - amount, 128)
        rolled = [pltpu.roll(tile, turn, 1) for tile in tiles]
        last = len(tiles) - 1
        return [jnp.where(keep, rolled[k], rolled[min(k + 1, last)]) for k in range(count)]

    window = turned(
        [rec[:, 128 * k : 128 * k + 128].astype(F32) for k in range(1, 4)], 2, jnp.int32(64)
    )
    for k in range(2):
        rwin[:, 128 * k : 128 * k + 128] = window[k].astype(BF16)

    low = jnp.where((t == 0) & (s == 0), 0, -4096)
    high = jnp.where((t == 63) & (s == 7), 128, 4096)

    def inside(lanes, start):
        f = lax.broadcasted_iota(jnp.int32, (128, lanes), 1) + start
        return (f >= low) & (f < high)

    drain(sf_r, st.at[0:128])
    sfull[...] = jnp.transpose(st[...].astype(F32)).astype(BF16)
    for n in range(0, 512, 128):
        part = dot(sfull[n : n + 128, :], rwin[...])
        h0[n : n + 128, :] = jnp.where(inside(256, -64), part, 0.0).astype(BF16)

    drain(b_r, bias.at[1:8])
    order = [(core, i) for core in range(2) for i in range(NY)]
    place = [2 * lax.rem(y + NY - i, NY) + core for core, i in order]
    columns = [jnp.transpose(bias[NY * core + i]) for core, i in order]

    def conv(layer, source, target, offset, tiles, start, forwarded=None):
        d = dil_ref[0, layer]
        for q in range(4):
            if q == 2 and forwarded is not None:
                forward_relays(forwarded)
            w = wc[layer, :, q].reshape(384, 512)
            taps[...] = dot(w, source[...])
            here = [rows(64 * p + 16 * q, 16, 16) for p in place]
            old = jnp.concatenate([source[h, :] for h in here], axis=0).astype(F32)
            col = jnp.concatenate([v[16 * q : 16 * q + 16] for v in columns], axis=0)
            col = col[:, layer : layer + 1]
            a, b, e = [
                turned(
                    [taps[128 * j : 128 * j + 128, 128 * k : 128 * k + 128] for k in range(2)],
                    tiles, offset + (j - 1) * d,
                )
                for j in range(3)
            ]
            r = turned([old[:, 0:128], old[:, 128:256]], tiles, jnp.int32(offset))
            for k in range(tiles):
                pre = col + a[k] + b[k] + e[k]
                out = r[k] + 0.5 * pre * (1.0 + lax.erf(pre * 0.7071067811865476))
                out = jnp.where(inside(128, start + 128 * k), out, 0.0).astype(BF16)
                for n, h in enumerate(here):
                    target[h, 128 * k : 128 * k + 128] = out[16 * n : 16 * n + 16]

    forward_relays(2)
    ready(0)
    conv(0, h0, h1, 16, 2, -48, 3)
    pl.semaphore_wait(z2, 2)
    signal(z4, at_z(4))
    signal(z4, at_z(NZ - 4))
    ready(1)
    conv(1, h1, h2, 16, 2, -32)
    ready(2)
    conv(2, h2, h3, 32, 1, 0)
    ready(3)

    own_lanes = rows(128 * s, 128, 128)
    for q in range(4):
        part = dot(kvw[q].reshape(256, 512), h3[...]).astype(BF16)
        for n, p in enumerate(place):
            kv[rows(128 * p + 32 * q, 32, 32), :] = part[32 * n : 32 * n + 32]
    kv_copies = []
    feature_copies = []
    for n, (i, k) in enumerate(peers):
        core = lax.rem(c + k, 2)
        to = lax.rem(y + i, NY) * 2 + core
        kv_copies.append(
            remote(kv.at[of_head(to)], kvall.at[:, own_lanes], kv_s, kv_r, at_y(i, core))
        )
        feature_copies.append(
            remote(
                h3.at[rows(64 * to, 64, 64)], feat_ref.at[:, own_lanes],
                f_s, f_r, at_y(i, core),
            )
        )
    for copy in kv_copies:
        copy.start()
    kvall[:, own_lanes] = kv[of_head(s), :]
    feat_ref[:, own_lanes] = h3[own_out, :]
    drain(st_s, st.at[0:96])
    drain(sf_s, st.at[0:128])
    drain(rec_s, rec.at[0:224, 0:384])
    drain(hal_s, rec.at[0:64, 0:128])
    drain(b_s, bias.at[1:8])
    for g in range(4):
        sent(g)
    drain(kv_r, kvall.at[:, 0:896])
    ka[0:64, :] = (kvall[0:64, :].astype(F32) * 0.125).astype(BF16)
    va[0:64, :] = kvall[64:128, :]
    kt[...] = jnp.transpose(ka[...].astype(F32)).astype(BF16)

    def block_lanes(quarter, j):
        return pl.ds(pl.multiple_of(quarter * QUARTER + j * LB, LB), LB)

    def finish(scores, slot, j):
        peak = jnp.max(scores[...], axis=0, keepdims=True)
        probs = jnp.exp(scores[...] - peak).astype(BF16)
        both = dot(va[...], probs)
        total = both[64:65, :]
        here = slice(j * LB, j * LB + LB)
        xsend[slot, :, here] = (both[0:64, :] / total).astype(BF16)
        xlse_send[slot, :, here] = peak + jnp.log(total)

    def x_copies(i):
        device = at_x(i)
        return (
            pltpu.make_async_remote_copy(
                src_ref=xsend.at[i], dst_ref=xrecv.at[i], send_sem=xs, recv_sem=xr,
                device_id=device, device_id_type=MESH),
            pltpu.make_async_remote_copy(
                src_ref=xlse_send.at[i], dst_ref=xlse.at[i], send_sem=xls, recv_sem=xlr,
                device_id=device, device_id_type=MESH),
        )

    score0[...] = dot(kt[...], qa[:, block_lanes(lax.rem(x + 1, NX), 0)])
    for n in range(NX):
        slot = (n + 1) % NX
        quarter = lax.rem(x + n + 1, NX)
        score1[...] = dot(kt[...], qa[:, block_lanes(quarter, 1)])
        finish(score0, slot, 0)
        if n < NX - 1:
            score0[...] = dot(kt[...], qa[:, block_lanes(lax.rem(quarter + 1, NX), 0)])
        finish(score1, slot, 1)
        if n < NX - 1:
            for copy in x_copies(slot):
                copy.start()

    def merge(parts, lses):
        peak = lses[0]
        for v in lses[1:]:
            peak = jnp.maximum(peak, v)
        total = jnp.zeros_like(peak)
        out = None
        for part, v in zip(parts, lses):
            weight = jnp.exp(v - peak)
            total = total + weight
            term = part.astype(F32) * weight
            out = term if out is None else out + term
        return out / total, peak + jnp.log(total)

    for copy in feature_copies:
        copy.start()
    drain(xr, xrecv.at[1:4])
    drain(xlr, xlse.at[1:4])
    for b in range(4):
        lanes = slice(128 * b, 128 * b + 128)
        out, lse = merge(
            [xsend[0, :, lanes]] + [xrecv[i, :, lanes] for i in range(1, NX)],
            [xlse_send[0, :, lanes]] + [xlse[i, :, lanes] for i in range(1, NX)],
        )
        zsend[:, lanes] = out.astype(BF16)
        zlse_send[b] = lse

    pl.semaphore_wait(z4, 2)

    def tile_of(zz):
        a, b = zz // 4, lax.rem(zz, 4)
        return pl.ds(pl.multiple_of(16 * a, 16), 16), pl.ds(pl.multiple_of(128 * b, 128), 128), b

    def z_copies(i):
        rows, lanes, b = tile_of(lax.rem(z + i, NZ))
        device = at_z(i)
        return (
            pltpu.make_async_remote_copy(
                src_ref=zsend.at[rows, lanes], dst_ref=zrecv.at[i], send_sem=zs,
                recv_sem=zr, device_id=device, device_id_type=MESH),
            pltpu.make_async_remote_copy(
                src_ref=zlse_send.at[b], dst_ref=zlse.at[i], send_sem=zls,
                recv_sem=zlr, device_id=device, device_id_type=MESH),
        )

    far_first = [8, 7, 9, 6, 10, 5, 11, 4, 12, 3, 13, 2, 14, 1, 15]
    for i in far_first:
        for copy in z_copies(i):
            copy.start()
    my_rows, my_lanes, my_b = tile_of(z)
    zrecv[0] = zsend[my_rows, my_lanes]
    zlse[0] = zlse_send[my_b]
    drain(zr, zrecv.at[1:16])
    drain(zlr, zlse.at[1:16])
    out, _ = merge([zrecv[i] for i in range(NZ)], [zlse[i] for i in range(NZ)])

    def out_tile(zz):
        rows, _, b = tile_of(zz)
        return rows, pl.ds(pl.multiple_of(512 * x + 128 * b, 128), 128)

    rows, lanes = out_tile(z)
    att_ref[rows, lanes] = out.astype(BF16)

    def a_copy(i, zz):
        tile = att_ref.at[out_tile(zz)]
        return pltpu.make_async_remote_copy(
            src_ref=tile, dst_ref=tile, send_sem=as_, recv_sem=ar.at[zz // 4],
            device_id=at_z(i), device_id_type=MESH)

    def spread(da):
        a = lax.rem(z // 4 + da + 4, 4)
        strip = att_ref.at[
            pl.ds(pl.multiple_of(16 * a, 16), 16), pl.ds(pl.multiple_of(512 * x, 512), 512)
        ]
        for i in range(1, NX):
            remote(strip, strip, bs, br, at_x(i)).start()

    for i in far_first:
        a_copy(i, z).start()
    for da in (0, 1, -1, 2):
        strip = zsend.at[0:16, 0 : 384 if da == 0 else 512]
        drain(ar.at[lax.rem(z // 4 + da + 4, 4)], strip)
        spread(da)
    drain(br, xrecv.at[1:4])
    drain(bs, xrecv.at[1:4])
    drain(as_, zrecv.at[1:16])
    drain(zs, zrecv.at[1:16])
    drain(zls, zlse.at[1:16])
    drain(xs, xrecv.at[1:4])
    drain(xls, xlse.at[1:4])
    drain(kv_s, kvall.at[:, 0:896])
    drain(f_s, h3.at[0:448])
    drain(f_r, h3.at[0:448])


def hand_on(feat, att, feat_out, att_out):
    feat_out[...] = feat[...]
    att_out[...] = att[...]


def on_device(recording, spatial_w, conv_w, conv_b, dilations, valid_frames, key_w, value_w, queries):
    vmem = pl.BlockSpec(memory_space=pltpu.VMEM)
    hbm = pl.BlockSpec(memory_space=pl.ANY)
    dma = pltpu.SemaphoreType.DMA
    regular = pltpu.SemaphoreType.REGULAR
    V = pltpu.VMEM
    results = pl.pallas_call(
        kernel,
        out_shape=(
            jax.ShapeDtypeStruct((64, 1024), BF16),
            jax.ShapeDtypeStruct((64, LATENTS), BF16),
        ),
        in_specs=[vmem, vmem, vmem, vmem, hbm, vmem, hbm, hbm, hbm],
        out_specs=(vmem, vmem),
        scratch_shapes=[
            V((256, 512), BF16), V((512, 256), BF16), V((256, 640), BF16), V((256, 256), BF16),
            V((3, 3, 4, 2, 4, 16, 512), BF16), V((8, 8, 128), F32), V((4, 2, 4, 32, 512), BF16),
            V((512, 256), BF16), V((512, 256), BF16), V((512, 256), BF16), V((512, 128), BF16),
            V((384, 256), F32), V((1024, 128), BF16), V((128, 1024), BF16),
            V((128, 1024), BF16), V((1024, 128), BF16), V((80, 1024), BF16), V((128, LATENTS), BF16),
            V((1024, LB), F32), V((1024, LB), F32),
            V((4, 64, 512), BF16), V((4, 1, 512), F32), V((4, 64, 512), BF16), V((4, 1, 512), F32),
            V((64, 512), BF16), V((4, 1, 128), F32), V((16, 16, 128), BF16), V((16, 1, 128), F32),
            dma((4,)), dma, dma, dma, dma, dma, dma, dma, dma, dma, dma,
            dma((4,)), dma((4,)), dma((4,)), dma((4,)), dma((4,)), dma((4,)),
            dma, dma, dma, dma, regular, regular, regular,
            dma, dma, dma, dma, dma, dma, dma, dma, dma, dma((4,)), dma, dma,
        ],
        compiler_params=pltpu.CompilerParams(
            collective_id=0, has_side_effects=True, vmem_limit_bytes=56 * 2**20
        ),
        name="encoder",
    )(
        dilations.reshape(1, 3), valid_frames.reshape(1, 1), recording, spatial_w.T, conv_w.reshape(3, 3, 4, 16, 512), conv_b,
        key_w.reshape(2, 32, 512), value_w.reshape(2, 32, 512), queries,
    )
    return pl.pallas_call(
        hand_on,
        out_shape=tuple(jax.ShapeDtypeStruct(r.shape, r.dtype) for r in results),
        in_specs=[vmem, vmem],
        out_specs=(vmem, vmem),
        name="hand_on",
    )(*results)


def solution(mesh):
    return jax.shard_map(
        on_device,
        mesh=mesh,
        in_specs=(
            P("sensor", "tm"),
            P(None, "sensor"),
            P(None, None, "sensor", None),
            P(None, "sensor"),
            P(),
            P("tm"),
            P("sensor", None),
            P("sensor", None),
            P("sensor", None),
        ),
        out_specs=(P("sensor", "tm"), P("sensor", None)),
        check_vma=False,
    )
```
